32 devices in a mesh: expert: 8 (over z, y), context: 2 (over core), dp: 2 (over x).
Axes of the slice: x: 2, y: 2, z: 4, core: 2. Of those that a mesh axis runs over, the one named last changes fastest.
Arguments:
- residual: bfloat16 [2, 2, 256, 4096], P('dp', 'context', 'expert'), may hold values from -6 to 6
- x_raw: bfloat16 [2, 2, 256, 8192], P('dp', 'context', None, 'expert'), may hold values from -6 to 6
- z_gate: bfloat16 [2, 2, 256, 8192], P('dp', 'context', None, 'expert'), may hold values from -6 to 6
- conv_w: float32 [4, 8192], P(None, 'expert'), may hold values from -3 to 3
- conv_b: float32 [8192], P('expert'), may hold values from -0.5 to 0.5
- xproj_w: bfloat16 [8192, 288], P('expert'), may hold values from -0.0625 to 0.0625
- dtproj_w: bfloat16 [256, 8192], P(None, 'expert'), may hold values from -0.375 to 0.375
- dt_bias: float32 [8192], P('expert'), may hold values from -4 to -1
- a_rate: float32 [16, 8192], P(None, 'expert'), may hold values from 0.02 to 2
- skip_gain: float32 [8192], P('expert'), may hold values from 0.5 to 1.5
- out_w: bfloat16 [8192, 4096], P('expert'), may hold values from -0.0625 to 0.0625
- norm_gain: float32 [4096], replicated, may hold values from 0.5 to 1.5
- route_ids: int32 [2, 2, 256, 2], P('dp', 'context', 'expert'), may hold values from 0 to 3, all different within a row; in each aligned block of 32 rows (0 to 31, 32 to 63, ..., all dimensions but the last counted through in order) at most 24 rows name the same one
- route_w: float32 [2, 2, 256, 2], P('dp', 'context', 'expert'), may hold values from 0.2 to 1
- w_gate: bfloat16 [8, 4096, 6144], P('expert', None, ('context', 'dp')), may hold values from -0.09375 to 0.09375
- w_up: bfloat16 [8, 4096, 6144], P('expert', None, ('context', 'dp')), may hold values from -0.09375 to 0.09375
- w_down: bfloat16 [8, 6144, 4096], P('expert', ('context', 'dp')), may hold values from -0.0546875 to 0.0546875
Outputs:
- mixed: bfloat16 [2, 2, 256, 4096], P('dp', 'context', 'expert')
The draws below stay inside these ranges and needn't reach their ends.
Inputs may be any that keep to these rules, and one draw needn't show every extreme that they name: `route_ids`: each row names 2 different experts; in each aligned block of 32 rows no expert is named by more than 24 rows, a bound that some block reaches.
All inputs are finite; a program needn't handle non-finite values.
Results may differ from the reference program's by a relative error of at most 0.018.
Values may be sent and summed in bfloat16 or wider, within the bound.
No kernel may reach another device: no remote copies, remote signals or barrier semaphores. Data moves between devices by JAX's collectives and lax.ppermute only.
A program may use at most 192 MiB of HBM per device.

```python
import math
import jax
import jax.numpy as jnp
import numpy as np
from jax import lax

D = 4096
FF = 12288
DI = 8192
NSTATE = 16
DT_RANK = 256
CONV = 4
TOP = 2
SPAN = 256
SEQS = 2
SPANS = 2
ROWS = 32
EXPERTS = 4
OWNERS = 8
HALF = 6144
HID = 1536
XW = 288
CAP = 24
N_EXPERT = 8
N_CONTEXT = 2
N_DP = 2


def steps_of(key, extent, pieces, least, top_value):
    def one(position, shards_of):
        steps = jax.random.uniform(jax.random.fold_in(jax.random.fold_in(key, 6), position), (shards_of,), jnp.float32, least / len(pieces), top_value / len(pieces))
        return jnp.repeat(jnp.exp(steps), extent[position] // shards_of).reshape((-1,) + (1,) * (len(extent) - position - 1))

    loudness = one(*pieces[0])
    for cut in pieces[1:]:
        loudness = loudness * one(*cut)
    return loudness


def deal_out(stream_key, own, number, rows, count, top, most, skew):
    sequence = jax.random.permutation(stream_key, count)
    heavy_load, usual = load_shares(count, rows * top, most, skew, True), load_shares(count, rows * top, most, skew, False)
    places = jnp.arange(count)

    def named(lengths, offset_by):
        used = int((lengths > 0).sum())
        fixed = max(1, used // 4)
        shifted = fixed + (places - fixed + offset_by * (used - fixed)) % max(1, count - fixed)
        return jnp.zeros((count,), jnp.int32).at[sequence[jnp.where(places < fixed, places, shifted)]].set(jnp.asarray(lengths, jnp.int32))

    lengths = jnp.where(number % 4 == 0, named(heavy_load, number // 4), named(usual, number - number // 4 - 1))
    mixed = jax.random.permutation(jax.random.fold_in(own, 3), count)
    giver, sink = mixed[0:count // 2 * 2:2], mixed[1:count // 2 * 2:2]
    margin = jnp.minimum(lengths[giver] - 1, most - lengths[sink]) // 2
    margin = jnp.where((giver == sequence[0]) | (sink == sequence[0]) | (lengths[sink] == 0), 0, jnp.maximum(margin, 0))
    shifted = jax.random.randint(jax.random.fold_in(own, 4), (count // 2,), 0, 1 << 20) % (margin + 1)
    lengths = lengths.at[giver].add(-shifted).at[sink].add(shifted)
    labels = jnp.searchsorted(jnp.cumsum(lengths), jnp.arange(rows * top), side="right").astype(jnp.int32)
    grid = labels.reshape(top, rows).T
    grid = grid[jax.random.permutation(jax.random.fold_in(own, 1), rows)]
    offset_by = jax.random.randint(jax.random.fold_in(own, 2), (rows, 1), 0, top)
    return jnp.take_along_axis(grid, (jnp.arange(top)[None, :] + offset_by) % top, axis=1)


def load_shares(number_of, total, bound, skew, full):
    loads = [(1 << 20) // math.isqrt(rank ** skew) + 1 for rank in range(1, number_of + 1)]
    largest = bound if full else min(bound, max(-(-total // number_of), total * loads[0] // sum(loads)))
    least = 1 if total - largest >= number_of - 1 else 0
    given, spare = [largest] + [least] * (number_of - 1), total - largest - least * (number_of - 1)
    while spare > 0:
        free = [i for i in range(1, number_of) if given[i] < largest] or [i for i in range(1, number_of) if given[i] < bound]
        pool, left = sum([loads[i] for i in free]), spare
        for i in free:
            more = min(bound - given[i], max(1, left * loads[i] // pool), spare)
            given[i] = given[i] + more
            spare = spare - more
    return np.array(given)


def scatter_about(key, shape, scale, reach, split=(), kind=jnp.bfloat16):
    values = jax.random.normal(key, shape, jnp.float32) * scale
    if len(split) > 0:
        values = steps_of(key, shape, split, -0.22, 0.18) * values
    return jnp.clip(values, min=-reach, max=reach).astype(kind)


def setup_inputs(seed: int = 0) -> dict:
    splits = jax.random.split(jax.random.key(seed), 18)
    residual = scatter_about(splits[0], (SEQS, SPANS, SPAN, D), 1.0, 6.0, ((0, 2), (1, 2), (2, 8)))
    x_raw = scatter_about(splits[1], (SEQS, SPANS, SPAN, DI), 1.0, 6.0, ((0, 2), (1, 2), (3, 8)))
    z_gate = scatter_about(splits[2], (SEQS, SPANS, SPAN, DI), 1.0, 6.0, ((0, 2), (1, 2), (3, 8)))
    conv_w = scatter_about(splits[3], (CONV, DI), CONV ** -0.5, 3.0, ((1, 8),), jnp.float32)
    conv_b = jnp.clip(jax.random.uniform(splits[4], (DI,), jnp.float32, -0.5, 0.5) * steps_of(splits[4], (DI,), ((0, 8),), -0.4, 0.0), -0.5, 0.5)
    xproj_w = scatter_about(splits[5], (DI, XW), DI ** -0.5, 0.0625, ((0, 8),))
    dtproj_w = scatter_about(splits[6], (DT_RANK, DI), DT_RANK ** -0.5, 0.375, ((1, 8),))
    dt_bias = jnp.clip(-4.0 + 3.0 * jax.random.uniform(splits[7], (DI,), jnp.float32) ** steps_of(splits[7], (DI,), ((0, 8),), -0.2, 0.2), -4.0, -1.0)
    a_rate = jnp.clip(jnp.exp(math.log(2.0) - 4.6051702 * jax.random.uniform(splits[8], (NSTATE, DI), jnp.float32) ** steps_of(splits[8], (NSTATE, DI), ((1, 8),), -0.2, 0.2)), 0.02, 2.0)
    skip_gain = jnp.clip(0.5 + 1.0 * jax.random.uniform(splits[9], (DI,), jnp.float32) ** steps_of(splits[9], (DI,), ((0, 8),), -0.2, 0.2), 0.5, 1.5)
    out_w = scatter_about(splits[10], (DI, D), DI ** -0.5, 0.0625, ((0, 8),))
    norm_gain = jnp.clip(1.0 + 0.1 * jax.random.normal(splits[11], (D,), jnp.float32), 0.5, 1.5)
    route_ids_keys = jax.random.split(jax.random.fold_in(splits[12], 1), SEQS * SPANS * SPAN // ROWS)
    route_ids_turns = jax.random.permutation(jax.random.fold_in(splits[12], 3), SEQS * SPANS * SPAN // ROWS)
    route_ids = jax.vmap(lambda own, number: deal_out(jax.random.fold_in(splits[12], 2), own, number, ROWS, EXPERTS, TOP, CAP, 2))(route_ids_keys, route_ids_turns).reshape((SEQS, SPANS, SPAN, TOP))
    route_w = jnp.clip(0.2 + 0.8 * jax.random.uniform(splits[13], (SEQS, SPANS, SPAN, TOP), jnp.float32) ** steps_of(splits[13], (SEQS, SPANS, SPAN, TOP), ((0, 2), (1, 2), (2, 8)), -0.2, 0.2), 0.2, 1.0)
    w_gate = scatter_about(splits[14], (OWNERS, D, HALF), D ** -0.5, 0.09375, ((0, 8), (2, 4)))
    w_up = scatter_about(splits[15], (OWNERS, D, HALF), D ** -0.5, 0.09375, ((0, 8), (2, 4)))
    w_down = scatter_about(splits[16], (OWNERS, HALF, D), FF ** -0.5, 0.0546875, ((0, 8), (1, 4)))
    return dict(residual=residual, x_raw=x_raw, z_gate=z_gate, conv_w=conv_w, conv_b=conv_b, xproj_w=xproj_w, dtproj_w=dtproj_w, dt_bias=dt_bias, a_rate=a_rate, skip_gain=skip_gain, out_w=out_w, norm_gain=norm_gain, route_ids=route_ids, route_w=route_w, w_gate=w_gate, w_up=w_up, w_down=w_down)


def combine_pairs(earlier, later):
    return (earlier[0] * later[0], later[0] * earlier[1] + later[1])

def mixer_sequence(seq_x, seq_z, conv_w, conv_b, xproj_w, dtproj_w, dt_bias, a_rate, skip_gain, out_w):
    window = seq_x.shape[0]
    values = seq_x.astype(jnp.float32)
    padded = jnp.concatenate([jnp.zeros((CONV - 1, DI), jnp.float32), values], axis=0)
    conv_sum = conv_b[None, :] + sum((conv_w[lag_index][None, :] * padded[lag_index:lag_index + window] for lag_index in range(CONV)))
    mixed_in = jax.nn.silu(conv_sum).astype(jnp.bfloat16)
    projected = jnp.dot(mixed_in, xproj_w, preferred_element_type=jnp.float32)
    dt_low = projected[:, :DT_RANK].astype(jnp.bfloat16)
    b_in = projected[:, DT_RANK:DT_RANK + NSTATE]
    c_out = projected[:, DT_RANK + NSTATE:]
    step_size = jax.nn.softplus(jnp.dot(dt_low, dtproj_w, preferred_element_type=jnp.float32) + dt_bias[None, :])
    inner_in = mixed_in.astype(jnp.float32)
    decays = jnp.exp(-step_size[:, None, :] * a_rate[None, :, :])
    drives = (step_size * inner_in)[:, None, :] * b_in[:, :, None]
    cumulated, states = lax.associative_scan(combine_pairs, (decays, drives), axis=0)
    readout = lax.optimization_barrier(jnp.sum(c_out[:, :, None] * states, axis=1)) + skip_gain[None, :] * inner_in
    gated = (readout * jax.nn.silu(seq_z.astype(jnp.float32))).astype(jnp.bfloat16)
    return jnp.dot(gated, out_w, preferred_element_type=jnp.float32)

def reference(residual, x_raw, z_gate, conv_w, conv_b, xproj_w, dtproj_w, dt_bias, a_rate, skip_gain, out_w, norm_gain, route_ids, route_w, w_gate, w_up, w_down):
    window = SPANS * SPAN
    all_rows = SEQS * window
    seq_xs = x_raw.reshape(SEQS, window, DI)
    seq_zs = z_gate.reshape(SEQS, window, DI)

    def one_sequence(inputs):
        return mixer_sequence(inputs[0], inputs[1], conv_w, conv_b, xproj_w, dtproj_w, dt_bias, a_rate, skip_gain, out_w)
    mixer_out = lax.map(one_sequence, (seq_xs, seq_zs))
    stream = (residual.reshape(all_rows, D).astype(jnp.float32) + mixer_out.reshape(all_rows, D)).astype(jnp.bfloat16)
    stream_f = stream.astype(jnp.float32)
    normed = (stream_f * lax.rsqrt(lax.optimization_barrier(jnp.mean(stream_f * stream_f, axis=1, keepdims=True)) + 1e-05) * norm_gain[None, :]).astype(jnp.bfloat16)
    choices_flat = route_ids.reshape(all_rows * TOP)
    weights_flat = route_w.reshape(all_rows * TOP)
    sources = jnp.repeat(normed, TOP, axis=0)
    groups = N_CONTEXT * N_DP
    limit = SEQS * SPANS * N_EXPERT * CAP

    def one_expert(accum, expert):
        picked = jnp.nonzero(choices_flat == expert, size=limit, fill_value=0)[0]
        gathered = sources[picked]
        gate_full = jnp.concatenate([w_gate[2 * expert], w_gate[2 * expert + 1]], axis=1)
        up_full = jnp.concatenate([w_up[2 * expert], w_up[2 * expert + 1]], axis=1)
        down_full = jnp.concatenate([w_down[2 * expert], w_down[2 * expert + 1]], axis=0)
        gate_val = jnp.dot(gathered, gate_full, preferred_element_type=jnp.float32)
        up_val = jnp.dot(gathered, up_full, preferred_element_type=jnp.float32)
        hidden = (jax.nn.silu(gate_val) * up_val).astype(jnp.bfloat16)
        parts = jnp.einsum('mgh,ghd->mgd', hidden.reshape(limit, 2 * groups, HID).astype(jnp.float32), down_full.reshape(2 * groups, HID, D).astype(jnp.float32))
        parts = lax.optimization_barrier(parts.astype(jnp.bfloat16)).astype(jnp.float32)
        halves = lax.optimization_barrier(jnp.sum(parts.reshape(limit, 2, groups, D), axis=2))
        halves = lax.optimization_barrier(halves.astype(jnp.bfloat16)).astype(jnp.float32)
        result = lax.optimization_barrier(jnp.sum(halves, axis=1))
        live_count = jnp.sum((choices_flat == expert).astype(jnp.int32))
        live_mask = (jnp.arange(limit) < live_count).astype(jnp.float32)
        weighted = result * (weights_flat[picked] * live_mask)[:, None]
        return (accum.at[picked].add(weighted), 0)
    start_acc = jnp.zeros((all_rows * TOP, D), jnp.float32)
    accum, unused = lax.scan(one_expert, start_acc, jnp.arange(EXPERTS, dtype=jnp.int32))
    expert_sum = lax.optimization_barrier(jnp.sum(accum.reshape(all_rows, TOP, D), axis=1))
    mixed = (stream_f + expert_sum).astype(jnp.bfloat16)
    return mixed.reshape(SEQS, SPANS, SPAN, D)
```

```python
import functools

import jax
import jax.numpy as jnp
from jax import lax
from jax.experimental import pallas as pl
from jax.experimental.pallas import tpu as pltpu
from jax.sharding import PartitionSpec as P

NSTATE = 16
DT_RANK = 256
CONV = 4
TOP = 2
LANES = 128
SUB = 8
F32 = jnp.float32
BF16 = jnp.bfloat16
MIB = 1 << 20


def from_behind(block, axis, distance):
    devices = range(lax.axis_size(axis))
    route = [(i - distance, i) for i in devices if i - distance in devices]
    return lax.ppermute(block, axis, route)


def shift(block, axis, distance):
    size = lax.axis_size(axis)
    return lax.ppermute(block, axis, [(i, (i + distance) % size) for i in range(size)])


def swap_pair(block):
    size = lax.axis_size("expert")
    return lax.ppermute(block, "expert", [(i, i ^ 1) for i in range(size)])


def cost(flops, bytes_accessed, transcendentals=0):
    return pl.CostEstimate(
        flops=int(flops), bytes_accessed=int(bytes_accessed), transcendentals=int(transcendentals)
    )


def spread_rows(values, wide_ref):
    length, count = values.shape
    col = lax.broadcasted_iota(jnp.int32, (count, count * LANES), 1)
    row = lax.broadcasted_iota(jnp.int32, (count, count * LANES), 0)
    ones = jnp.where((col >= row * LANES) & (col < (row + 1) * LANES), 1.0, 0.0).astype(BF16)
    out = jnp.dot(values, ones, preferred_element_type=F32)
    for n in range(count):
        wide_ref[pl.ds(n * length, length), :] = out[:, n * LANES : (n + 1) * LANES]


def scan_kernel(groups, low_ref, bc_ref, w_ref, bias_ref, neg_ref, x_ref, y_ref, sum_ref, end_ref,
                step_ref, drive_ref, wide_ref):
    length = x_ref.shape[0]
    spread_rows(bc_ref[...], wide_ref)
    for g in range(SUB):
        rows = pl.ds(g, length, stride=SUB)
        if g >= groups:
            step_ref[rows, :] = jnp.zeros((length, LANES), F32)
            drive_ref[rows, :] = jnp.zeros((length, LANES), F32)
            continue
        cols = pl.ds(g * LANES, LANES)
        raw = jnp.dot(low_ref[...], w_ref[:, cols], preferred_element_type=F32) + bias_ref[:, cols]
        step = jnp.maximum(raw, 0.0) + jnp.log1p(jnp.exp(-jnp.abs(raw)))
        step_ref[rows, :] = step
        drive_ref[rows, :] = step * x_ref[:, cols].astype(F32)

    def block(k, carry):
        states, total = list(carry[0]), carry[1]
        for u in range(SUB):
            t = k * SUB + u
            here = pl.ds(pl.multiple_of(t * SUB, SUB), SUB)
            step, drive = step_ref[here, :], drive_ref[here, :]
            total = total + step
            out = jnp.zeros((SUB, LANES), F32)
            for n in range(NSTATE):
                decay = jnp.exp(step * neg_ref[n])
                b = wide_ref[pl.ds(n * length + t, 1), :]
                c = wide_ref[pl.ds((NSTATE + n) * length + t, 1), :]
                states[n] = states[n] * decay + drive * b
                out = out + states[n] * c
            y_ref[here, :] = out
            sum_ref[here, :] = total
        return tuple(states), total

    zero = jnp.zeros((SUB, LANES), F32)
    states, total = lax.fori_loop(0, length // SUB, block, ((zero,) * NSTATE, zero))
    for n in range(NSTATE):
        end_ref[n] = states[n]


def run_scan(low, bc, w, bias, neg, x):
    length, channels = x.shape
    vmem = pl.BlockSpec(memory_space=pltpu.VMEM)
    tall = jax.ShapeDtypeStruct((length * SUB, LANES), F32)
    return pl.pallas_call(
        functools.partial(scan_kernel, channels // LANES),
        out_shape=(tall, tall, jax.ShapeDtypeStruct((NSTATE, SUB, LANES), F32)),
        in_specs=[vmem] * 6,
        out_specs=(vmem,) * 3,
        scratch_shapes=[
            pltpu.VMEM((length * SUB, LANES), F32),
            pltpu.VMEM((length * SUB, LANES), F32),
            pltpu.VMEM((2 * NSTATE * length, LANES), F32),
        ],
        compiler_params=pltpu.CompilerParams(vmem_limit_bytes=24 * MIB),
        cost_estimate=cost(2e8, 4 * MIB, NSTATE * length * channels),
        name="state_scan",
    )(low, bc, w, bias, neg, x)


def out_kernel(groups, piece, half_ref, y_ref, sum_ref, enter_ref, c_ref, neg_ref, x_ref, z_ref,
               skip_ref, w_hbm, kept_ref, sent_ref, full_ref, wide_ref, gated_ref, order_ref, w_ref,
               sem):
    length = x_ref.shape[0]
    fetch = pltpu.make_async_copy(w_hbm, w_ref, sem)
    fetch.start()
    spread_rows(c_ref[...], wide_ref)

    def block(k, carry):
        for u in range(SUB):
            t = k * SUB + u
            here = pl.ds(pl.multiple_of(t * SUB, SUB), SUB)
            total = sum_ref[here, :]
            out = y_ref[here, :]
            for n in range(NSTATE):
                c = wide_ref[pl.ds(n * length + t, 1), :]
                out = out + jnp.exp(total * neg_ref[n]) * enter_ref[n] * c
            full_ref[here, :] = out
        return carry

    lax.fori_loop(0, length // SUB, block, 0)
    for g in range(groups):
        cols = pl.ds(g * LANES, LANES)
        mixed_in = x_ref[:, cols].astype(F32)
        read = full_ref[pl.ds(g, length, stride=SUB), :] + skip_ref[:, cols] * mixed_in
        z = z_ref[:, cols].astype(F32)
        gated_ref[:, cols] = (read * (z / (1.0 + jnp.exp(-z)))).astype(BF16)
    half = half_ref[0]
    count = length // 2
    for k in range(count // piece):
        for r in range(2):
            source = pl.multiple_of((2 * k + (half ^ r)) * piece, piece)
            order_ref[pl.ds(r * count + k * piece, piece), :] = gated_ref[pl.ds(source, piece), :]
    fetch.wait()
    wide = w_ref.shape[1]
    tile = min(512, wide)
    for j in range(wide // tile):
        cols = pl.ds(j * tile, tile)
        out = jnp.dot(order_ref[...], w_ref[:, cols], preferred_element_type=F32).astype(BF16)
        kept_ref[:, cols] = out[:count]
        sent_ref[:, cols] = out[count:]


def run_out(half, piece, y, total, enter, c, neg, x, z, skip, w):
    length, channels = x.shape
    wide = w.shape[1]
    vmem = pl.BlockSpec(memory_space=pltpu.VMEM)
    part = jax.ShapeDtypeStruct((length // 2, wide), BF16)
    return pl.pallas_call(
        functools.partial(out_kernel, channels // LANES, piece),
        out_shape=(part, part),
        in_specs=[pl.BlockSpec(memory_space=pltpu.SMEM)] + [vmem] * 8 + [pl.BlockSpec(memory_space=pl.ANY)],
        out_specs=(vmem, vmem),
        scratch_shapes=[
            pltpu.VMEM((length * SUB, LANES), F32),
            pltpu.VMEM((NSTATE * length, LANES), F32),
            pltpu.VMEM((length, channels), BF16),
            pltpu.VMEM((length, channels), BF16),
            pltpu.VMEM((channels, wide), BF16),
            pltpu.SemaphoreType.DMA,
        ],
        compiler_params=pltpu.CompilerParams(vmem_limit_bytes=32 * MIB),
        cost_estimate=cost(
            2 * length * channels * wide, 2 * channels * wide + 8 * MIB, NSTATE * length * channels
        ),
        name="readout_project",
    )(half, y, total, enter, c, neg, x, z, skip, w)


def gate_up_kernel(count, *refs):
    pieces, (gate_ref, up_ref, out_ref, rows_ref) = refs[:count], refs[count:]

    @pl.when(pl.program_id(0) == 0)
    def _():
        at = 0
        for piece in pieces:
            rows_ref[pl.ds(at, piece.shape[0]), :] = piece[...]
            at += piece.shape[0]

    gate = jnp.dot(rows_ref[...], gate_ref[...], preferred_element_type=F32)
    up = jnp.dot(rows_ref[...], up_ref[...], preferred_element_type=F32)
    out_ref[...] = (gate / (1.0 + jnp.exp(-gate)) * up).astype(BF16)


def gate_up(pieces, w_gate, w_up):
    depth, hidden = w_gate.shape
    rows = sum(p.shape[0] for p in pieces)
    tile = min(256, hidden)
    fixed = [pl.BlockSpec(p.shape, lambda j: (0, 0)) for p in pieces]
    weight = pl.BlockSpec((depth, tile), lambda j: (0, j))
    return pl.pallas_call(
        functools.partial(gate_up_kernel, len(pieces)),
        out_shape=jax.ShapeDtypeStruct((rows, hidden), BF16),
        grid=(hidden // tile,),
        in_specs=fixed + [weight, weight],
        out_specs=pl.BlockSpec((rows, tile), lambda j: (0, j)),
        scratch_shapes=[pltpu.VMEM((rows, depth), BF16)],
        compiler_params=pltpu.CompilerParams(vmem_limit_bytes=40 * MIB),
        cost_estimate=cost(4 * rows * depth * hidden, 4 * depth * hidden + 2 * rows * depth),
        name="gate_up",
    )(*pieces, w_gate, w_up)


def down_kernel(count, places, *refs):
    pieces, (w_ref, own_ref, far_ref, rows_ref) = refs[:count], refs[count:]

    @pl.when(pl.program_id(0) == 0)
    def _():
        for source, start, target, size in places:
            rows_ref[pl.ds(target, size), :] = pieces[source][pl.ds(start, size), :]

    near = own_ref.shape[0]
    out = jnp.dot(rows_ref[...], w_ref[...], preferred_element_type=F32).astype(BF16)
    own_ref[...] = out[:near]
    far_ref[...] = out[near:]


def down(pieces, places, near, w_down, first, width):
    hidden = w_down.shape[0]
    rows = sum(p.shape[0] for p in pieces)
    tile = min(512, width)
    offset = first // tile
    fixed = [pl.BlockSpec(p.shape, lambda j: (0, 0)) for p in pieces]
    return pl.pallas_call(
        functools.partial(down_kernel, len(pieces), places),
        out_shape=(
            jax.ShapeDtypeStruct((near, width), BF16),
            jax.ShapeDtypeStruct((rows - near, width), BF16),
        ),
        grid=(width // tile,),
        in_specs=fixed + [pl.BlockSpec((hidden, tile), lambda j: (0, j + offset))],
        out_specs=(
            pl.BlockSpec((near, tile), lambda j: (0, j)),
            pl.BlockSpec((rows - near, tile), lambda j: (0, j)),
        ),
        scratch_shapes=[pltpu.VMEM((rows, hidden), BF16)],
        compiler_params=pltpu.CompilerParams(vmem_limit_bytes=32 * MIB),
        cost_estimate=cost(2 * rows * hidden * width, 2 * hidden * width + 2 * rows * (hidden + width)),
        name="down",
    )(*pieces, w_down)


def add_up(*parts):
    return sum(p.astype(F32) for p in parts)


def line_sum(blocks, place):
    size = blocks.shape[0]
    forth, back = [], []
    for s in range(1, size):
        forth.append([(2 * i + o, 2 * i + o + 2) for i in range(s) for o in range(2)])
        back.append([(2 * i + o, 2 * i + o - 2) for i in range(size - s, size) for o in range(2)])

    def block(k):
        return lax.dynamic_index_in_dim(blocks, jnp.clip(k, 0, size - 1), 0, keepdims=False)

    up, low = block(place + size - 1), block(place - size + 1)
    for s in range(1, size):
        up = lax.ppermute(up.astype(BF16), "expert", forth[s - 1]).astype(F32)
        low = lax.ppermute(low.astype(BF16), "expert", back[s - 1]).astype(F32)
        if s < size - 1:
            up = up + block(place + size - 1 - s)
            low = low + block(place - size + 1 + s)
    return block(place) + up + low


def on_device(
    residual,
    x_raw,
    z_gate,
    conv_w,
    conv_b,
    xproj_w,
    dtproj_w,
    dt_bias,
    a_rate,
    skip_gain,
    out_w,
    norm_gain,
    route_ids,
    route_w,
    w_gate,
    w_up,
    w_down,
):
    owners, contexts, dps = (lax.axis_size(a) for a in ("expert", "context", "dp"))
    me = lax.axis_index("expert")
    place, half = me // 2, me % 2
    line = owners // 2
    length, channels = x_raw.shape[2:]
    width = residual.shape[3]
    row_count = residual.shape[2]

    values = x_raw[0, 0]
    prior_rim = from_behind(values[length - (CONV - 1) :], "context", 1)
    padded = jnp.concatenate([prior_rim, values], axis=0).astype(F32)
    conv_sum = conv_b[None, :] + sum(
        (
            conv_w[lag_index][None, :] * padded[lag_index : lag_index + length]
            for lag_index in range(CONV)
        )
    )
    mixed_in = jax.nn.silu(conv_sum).astype(BF16)
    projected = jnp.dot(mixed_in, xproj_w, preferred_element_type=F32).astype(BF16)
    shares = lax.all_to_all(
        projected.reshape(owners, length // owners, -1), "expert", split_axis=0, concat_axis=0, tiled=True
    )
    share = add_up(*[shares[i] for i in range(owners)]).astype(BF16)
    projected = lax.all_to_all(
        jnp.broadcast_to(share[None], (owners,) + share.shape),
        "expert",
        split_axis=0,
        concat_axis=0,
        tiled=True,
    ).reshape(length, -1)
    dt_low = projected[:, :DT_RANK]
    bc = projected[:, DT_RANK:]

    neg = -a_rate.reshape(NSTATE, channels // LANES, LANES)
    neg = jnp.pad(neg, ((0, 0), (0, SUB - channels // LANES), (0, 0)))
    y, total, end = run_scan(dt_low, bc, dtproj_w, dt_bias[None, :], neg, mixed_in)
    enter = from_behind(end, "context", 1)
    for step in range(contexts - 2):
        decay = jnp.exp(total[-SUB:][None] * neg)
        enter = from_behind(end + decay * enter, "context", 1)
    kept, sent = run_out(
        half.astype(jnp.int32).reshape(1),
        row_count,
        y,
        total,
        enter,
        bc[:, NSTATE:],
        neg,
        mixed_in,
        z_gate[0, 0],
        skip_gain[None, :],
        out_w,
    )
    parts = 2
    part = width // parts
    sums = []
    for k in range(parts):
        cols = slice(k * part, (k + 1) * part)
        blocks = add_up(kept[:, cols], swap_pair(sent[:, cols])).reshape(line, row_count, part)
        sums.append(line_sum(blocks, place))
    mixer_out = jnp.concatenate(sums, axis=1)

    stream_f = (residual[0, 0].astype(F32) + mixer_out).astype(BF16).astype(F32)
    normed = (
        stream_f
        * lax.rsqrt(jnp.mean(stream_f * stream_f, axis=1, keepdims=True) + 1e-05)
        * norm_gain[None, :]
    ).astype(BF16)
    ids, weights = route_ids[0, 0], route_w[0, 0]
    capacity = min(row_count, 8 * ((3 * row_count * TOP + 16 * line - 1) // (16 * line)))
    named = jnp.any(ids[:, :, None] == jnp.arange(line, dtype=jnp.int32), axis=1)
    rank = jnp.cumsum(named.astype(jnp.int32), axis=0) - 1
    rank_of = jnp.take_along_axis(rank, ids, axis=1)
    slots = jnp.arange(line * capacity, dtype=jnp.int32)
    slot_of = ids * capacity + rank_of
    placing = jnp.any(slot_of[:, :, None] == slots, axis=1).astype(BF16)
    packed = lax.dot_general(
        placing, normed, (((0,), (0,)), ((), ())), preferred_element_type=F32
    ).astype(BF16)
    groups = [[2 * i + o for i in range(line)] for o in range(2)]
    own = lax.all_to_all(
        packed, "expert", split_axis=0, concat_axis=0, axis_index_groups=groups, tiled=True
    )
    rows = line * capacity
    cut = rows // 2
    far_dp = range(1, dps)
    from_y = swap_pair(own)
    from_x = [shift(own, "dp", s) for s in far_dp]
    diagonal = [
        (shift(from_y[:cut], "dp", s), swap_pair(from_x[s - 1][cut:])) for s in far_dp
    ]

    def all_cores(pieces):
        return pieces + [shift(p, "context", s) for s in range(1, contexts) for p in pieces]

    hidden = []
    for pieces in ([own], [from_y] + from_x, [p for pair in diagonal for p in pair]):
        hidden.append(gate_up(all_cores(pieces), w_gate[0], w_up[0]))
    near = 2 * dps * rows
    places = []
    for core in range(contexts):
        base = core * near
        places.append((0, core * rows, base, rows))
        places.append((1, core * dps * rows, base + rows, dps * rows))
        places.append((2, core * (dps - 1) * rows, base + (dps + 1) * rows, (dps - 1) * rows))

    back = []
    for k in range(parts):
        out, far = down(hidden, places, near, w_down[0], k * part, part)
        for s in range(1, contexts):
            got = shift(far[(s - 1) * near : s * near], "context", -s)
            out = add_up(out, got)
        blocks = out.astype(BF16).reshape(2 * dps, rows, part)
        mid = part // 2
        own_sum = blocks[0]
        by_y, by_x, by_both = blocks[1], blocks[2 : dps + 1], blocks[dps + 1 :]
        y_left = add_up(by_y[:, :mid], *[shift(by_both[s - 1, :, :mid], "dp", -s) for s in far_dp])
        y_all = jnp.concatenate([y_left.astype(BF16), by_y[:, mid:]], axis=1)
        x_right = add_up(by_x[:, :, mid:], swap_pair(by_both[:, :, mid:])).astype(BF16)
        x_all = jnp.concatenate([by_x[:, :, :mid], x_right], axis=2)
        total_out = add_up(own_sum, swap_pair(y_all), *[shift(x_all[s - 1], "dp", -s) for s in far_dp])
        outbound = total_out.astype(BF16).reshape(line, capacity, part)
        came = [lax.dynamic_index_in_dim(outbound, place, 0, keepdims=False)]
        for s in range(1, line):
            block = lax.dynamic_index_in_dim(outbound, (place - s) % line, 0, keepdims=False)
            came.append(
                lax.ppermute(block, "expert", [(e, (e - 2 * s) % owners) for e in range(owners)])
            )
        back.append(jnp.concatenate(came, axis=0))
    slot_here = ((ids - place) % line) * capacity + rank_of
    weighting = jnp.sum(
        jnp.where(slot_here[:, :, None] == slots, weights[:, :, None], 0.0), axis=1
    )
    expert_sum = jnp.concatenate(
        [
            jnp.dot(
                weighting, b.astype(F32), precision=lax.Precision.HIGHEST, preferred_element_type=F32
            )
            for b in back
        ],
        axis=1,
    )
    mixed = (stream_f + expert_sum).astype(BF16)
    return mixed.reshape(1, 1, row_count, width)


def solution(mesh):
    placed = (
        P("dp", "context", "expert", None),
        P("dp", "context", None, "expert"),
        P("dp", "context", None, "expert"),
        P(None, "expert"),
        P("expert"),
        P("expert", None),
        P(None, "expert"),
        P("expert"),
        P(None, "expert"),
        P("expert"),
        P("expert", None),
        P(),
        P("dp", "context", "expert", None),
        P("dp", "context", "expert", None),
        P("expert", None, ("context", "dp")),
        P("expert", None, ("context", "dp")),
        P("expert", ("context", "dp"), None),
    )
    return jax.shard_map(
        on_device,
        mesh=mesh,
        in_specs=placed,
        out_specs=P("dp", "context", "expert", None),
        check_vma=False,
    )
```

```python
import functools

import jax
import jax.numpy as jnp
from jax import lax
from jax.experimental import pallas as pl
from jax.experimental.pallas import tpu as pltpu
from jax.sharding import PartitionSpec as P

NSTATE = 16
DT_RANK = 256
CONV = 4
TOP = 2
LANES = 128
SUB = 8
F32 = jnp.float32
BF16 = jnp.bfloat16
MIB = 1 << 20


def from_behind(block, axis, distance):
    devices = range(lax.axis_size(axis))
    route = [(i - distance, i) for i in devices if i - distance in devices]
    return lax.ppermute(block, axis, route)


def shift(block, axis, distance):
    size = lax.axis_size(axis)
    return lax.ppermute(block, axis, [(i, (i + distance) % size) for i in range(size)])


def swap_pair(block):
    size = lax.axis_size("expert")
    return lax.ppermute(block, "expert", [(i, i ^ 1) for i in range(size)])


def cost(flops, bytes_accessed, transcendentals=0):
    return pl.CostEstimate(
        flops=int(flops), bytes_accessed=int(bytes_accessed), transcendentals=int(transcendentals)
    )


def spread_rows(values, wide_ref):
    length, count = values.shape
    col = lax.broadcasted_iota(jnp.int32, (count, count * LANES), 1)
    row = lax.broadcasted_iota(jnp.int32, (count, count * LANES), 0)
    ones = jnp.where((col >= row * LANES) & (col < (row + 1) * LANES), 1.0, 0.0).astype(BF16)
    out = jnp.dot(values, ones, preferred_element_type=F32)
    for n in range(count):
        wide_ref[pl.ds(n * length, length), :] = out[:, n * LANES : (n + 1) * LANES]


def scan_kernel(groups, line, place_ref, *refs):
    pieces, refs = refs[:line], refs[line:]
    w_ref, bias_ref, neg_ref, x_ref, y_ref, sum_ref, end_ref, bc_ref = refs[:8]
    low_ref, step_ref, drive_ref, wide_ref = refs[8:]
    length = x_ref.shape[0]
    share = length // line
    for s in range(line):
        start = pl.multiple_of((place_ref[0] + (line - s)) % line * share, share)
        low_ref[pl.ds(start, share), :] = pieces[s][:, :DT_RANK]
        bc_ref[pl.ds(start, share), :] = pieces[s][:, DT_RANK:]
    spread_rows(bc_ref[...], wide_ref)
    for g in range(SUB):
        rows = pl.ds(g, length, stride=SUB)
        if g >= groups:
            step_ref[rows, :] = jnp.zeros((length, LANES), F32)
            drive_ref[rows, :] = jnp.zeros((length, LANES), F32)
            continue
        cols = pl.ds(g * LANES, LANES)
        raw = jnp.dot(low_ref[...], w_ref[:, cols], preferred_element_type=F32) + bias_ref[:, cols]
        step = jnp.maximum(raw, 0.0) + jnp.log1p(jnp.exp(-jnp.abs(raw)))
        step_ref[rows, :] = step
        drive_ref[rows, :] = step * x_ref[:, cols].astype(F32)

    def block(k, carry):
        states, total = list(carry[0]), carry[1]
        for u in range(SUB):
            t = k * SUB + u
            here = pl.ds(pl.multiple_of(t * SUB, SUB), SUB)
            step, drive = step_ref[here, :], drive_ref[here, :]
            total = total + step
            out = jnp.zeros((SUB, LANES), F32)
            for n in range(NSTATE):
                decay = jnp.exp(step * neg_ref[n])
                b = wide_ref[pl.ds(n * length + t, 1), :]
                c = wide_ref[pl.ds((NSTATE + n) * length + t, 1), :]
                states[n] = states[n] * decay + drive * b
                out = out + states[n] * c
            y_ref[here, :] = out
            sum_ref[here, :] = total
        return tuple(states), total

    zero = jnp.zeros((SUB, LANES), F32)
    states, total = lax.fori_loop(0, length // SUB, block, ((zero,) * NSTATE, zero))
    for n in range(NSTATE):
        end_ref[n] = states[n]


def run_scan(place, pieces, w, bias, neg, x):
    length, channels = x.shape
    vmem = pl.BlockSpec(memory_space=pltpu.VMEM)
    tall = jax.ShapeDtypeStruct((length * SUB, LANES), F32)
    return pl.pallas_call(
        functools.partial(scan_kernel, channels // LANES, len(pieces)),
        out_shape=(
            tall,
            tall,
            jax.ShapeDtypeStruct((NSTATE, SUB, LANES), F32),
            jax.ShapeDtypeStruct((length, 2 * NSTATE), BF16),
        ),
        in_specs=[pl.BlockSpec(memory_space=pltpu.SMEM)] + [vmem] * (len(pieces) + 4),
        out_specs=(vmem,) * 4,
        scratch_shapes=[
            pltpu.VMEM((length, DT_RANK), BF16),
            pltpu.VMEM((length * SUB, LANES), F32),
            pltpu.VMEM((length * SUB, LANES), F32),
            pltpu.VMEM((2 * NSTATE * length, LANES), F32),
        ],
        compiler_params=pltpu.CompilerParams(vmem_limit_bytes=20 * MIB),
        cost_estimate=cost(2e8, 4 * MIB, NSTATE * length * channels),
        name="state_scan",
    )(place, *pieces, w, bias, neg, x)


def out_kernel(groups, line, parts, at_ref, y_ref, sum_ref, enter_ref, bc_ref, neg_ref, x_ref, z_ref,
               skip_ref, w_ref, *refs):
    kept_refs, sent_refs = refs[:parts], refs[parts : 2 * parts]
    full_ref, wide_ref, gated_ref, order_ref = refs[2 * parts :]
    length = x_ref.shape[0]
    spread_rows(bc_ref[:, NSTATE:], wide_ref)

    def block(k, carry):
        for u in range(SUB):
            t = k * SUB + u
            here = pl.ds(pl.multiple_of(t * SUB, SUB), SUB)
            total = sum_ref[here, :]
            out = y_ref[here, :]
            for n in range(NSTATE):
                c = wide_ref[pl.ds(n * length + t, 1), :]
                out = out + jnp.exp(total * neg_ref[n]) * enter_ref[n] * c
            full_ref[here, :] = out
        return carry

    lax.fori_loop(0, length // SUB, block, 0)
    for g in range(groups):
        cols = pl.ds(g * LANES, LANES)
        mixed_in = x_ref[:, cols].astype(F32)
        read = full_ref[pl.ds(g, length, stride=SUB), :] + skip_ref[:, cols] * mixed_in
        z = z_ref[:, cols].astype(F32)
        gated_ref[:, cols] = (read * (z / (1.0 + jnp.exp(-z)))).astype(BF16)
    place, half = at_ref[0], at_ref[1]
    count = length // 2
    piece = count // line
    for k in range(line):
        for r in range(2):
            source = pl.multiple_of((2 * ((place + k) % line) + (half ^ r)) * piece, piece)
            order_ref[pl.ds(r * count + k * piece, piece), :] = gated_ref[pl.ds(source, piece), :]
    wide = w_ref.shape[1] // parts
    for j in range(parts):
        cols = pl.ds(j * wide, wide)
        out = jnp.dot(order_ref[...], w_ref[:, cols], preferred_element_type=F32).astype(BF16)
        kept_refs[j][...] = out[:count]
        sent_refs[j][...] = out[count:]


def run_out(at, line, parts, y, total, enter, bc, neg, x, z, skip, w):
    length, channels = x.shape
    wide = w.shape[1]
    vmem = pl.BlockSpec(memory_space=pltpu.VMEM)
    return pl.pallas_call(
        functools.partial(out_kernel, channels // LANES, line, parts),
        out_shape=(jax.ShapeDtypeStruct((length // 2, wide // parts), BF16),) * (2 * parts),
        in_specs=[pl.BlockSpec(memory_space=pltpu.SMEM)] + [vmem] * 9,
        out_specs=(vmem,) * (2 * parts),
        scratch_shapes=[
            pltpu.VMEM((length * SUB, LANES), F32),
            pltpu.VMEM((NSTATE * length, LANES), F32),
            pltpu.VMEM((length, channels), BF16),
            pltpu.VMEM((length, channels), BF16),
        ],
        compiler_params=pltpu.CompilerParams(vmem_limit_bytes=16 * MIB),
        cost_estimate=cost(
            2 * length * channels * wide, 2 * channels * wide + 8 * MIB, NSTATE * length * channels
        ),
        name="readout_project",
    )(at, y, total, enter, bc, neg, x, z, skip, w)


def gate_up_kernel(count, *refs):
    pieces, (gate_ref, up_ref, out_ref, rows_ref) = refs[:count], refs[count:]

    @pl.when(pl.program_id(0) == 0)
    def _():
        at = 0
        for piece in pieces:
            rows_ref[pl.ds(at, piece.shape[0]), :] = piece[...]
            at += piece.shape[0]

    gate = jnp.dot(rows_ref[...], gate_ref[...], preferred_element_type=F32)
    up = jnp.dot(rows_ref[...], up_ref[...], preferred_element_type=F32)
    out_ref[...] = (gate / (1.0 + jnp.exp(-gate)) * up).astype(BF16)


def gate_up(pieces, w_gate, w_up):
    depth, hidden = w_gate.shape
    rows = sum(p.shape[0] for p in pieces)
    tile = min(256, hidden)
    weight = pl.BlockSpec((depth, tile), lambda j: (0, j))
    return pl.pallas_call(
        functools.partial(gate_up_kernel, len(pieces)),
        out_shape=jax.ShapeDtypeStruct((rows, hidden), BF16),
        grid=(hidden // tile,),
        in_specs=[pl.BlockSpec(p.shape, lambda j: (0, 0)) for p in pieces] + [weight, weight],
        out_specs=pl.BlockSpec((rows, tile), lambda j: (0, j)),
        scratch_shapes=[pltpu.VMEM((rows, depth), BF16)],
        compiler_params=pltpu.CompilerParams(vmem_limit_bytes=52 * MIB),
        cost_estimate=cost(4 * rows * depth * hidden, 4 * depth * hidden + 2 * rows * depth),
        name="gate_up",
    )(*pieces, w_gate, w_up)


def down_kernel(rows_ref, w_ref, *outs):
    out = jnp.dot(rows_ref[...], w_ref[...], preferred_element_type=F32).astype(BF16)
    start = 0
    for ref in outs:
        ref[...] = out[start : start + ref.shape[0]]
        start += ref.shape[0]


def down(rows, sizes, w_down):
    hidden, wide = w_down.shape
    tile = min(512, wide)
    return pl.pallas_call(
        down_kernel,
        out_shape=tuple(jax.ShapeDtypeStruct((n, wide), BF16) for n in sizes),
        grid=(wide // tile,),
        in_specs=[
            pl.BlockSpec(rows.shape, lambda j: (0, 0)),
            pl.BlockSpec((hidden, tile), lambda j: (0, j)),
        ],
        out_specs=tuple(pl.BlockSpec((n, tile), lambda j: (0, j)) for n in sizes),
        compiler_params=pltpu.CompilerParams(vmem_limit_bytes=52 * MIB),
        cost_estimate=cost(
            2 * rows.shape[0] * hidden * wide, 2 * hidden * wide + 2 * rows.shape[0] * (hidden + wide)
        ),
        name="down",
    )(rows, w_down)


def add_up(*parts):
    return sum(p.astype(F32) for p in parts)


def along_line(block, distance):
    size = lax.axis_size("expert")
    return lax.ppermute(block, "expert", [(e, (e + 2 * distance) % size) for e in range(size)])


def cross(block, turn):
    owners, dps = lax.axis_size("expert"), lax.axis_size("dp")
    route = []
    for e in range(owners):
        for core in range(2):
            for d in range(dps):
                to = (e ^ 1, core, d) if core == turn else (e, core, d ^ 1)
                route.append(((e * 2 + core) * dps + d, (to[0] * 2 + core) * dps + to[2]))
    return lax.ppermute(block, ("expert", "context", "dp"), route)


def after(block, other):
    return lax.optimization_barrier((block, other))[0]


class Chunk:
    def __init__(self, packed, line, square):
        self.line, self.square, self.packed = line, square, packed

    def send(self):
        size = self.packed.shape[0] // self.line
        parts = [self.packed[size * s : size * (s + 1)] for s in range(self.line)]
        self.arrived = [parts[0]] + [along_line(parts[s], s) for s in range(1, self.line)]

    def first(self):
        self.own = jnp.concatenate(self.arrived, axis=0)
        self.near = cross(self.own, 0) if self.square else swap_pair(self.own)

    def second(self):
        self.two = jnp.concatenate([self.own, self.near], axis=0)
        if self.square:
            self.two_far = shift(self.two, "context", 1)
            self.four = cross(self.two, 1)
        else:
            self.four = lax.all_gather(self.two, ("context", "dp"), axis=0, tiled=True)

    def third(self):
        self.pieces, self.sizes = [self.four], (self.four.shape[0],)
        if self.square:
            self.pieces = [self.two, self.four, self.two_far, shift(self.four, "context", 1)]
            self.sizes = (2 * self.two.shape[0],) * 2

    def work_first(self, w_gate, w_up, *others):
        pieces = lax.optimization_barrier((self.pieces, others))[0]
        self.hidden = gate_up(pieces, w_gate, w_up)

    def work_second(self, w_down, *others):
        self.outs = down(lax.optimization_barrier((self.hidden, others))[0], self.sizes, w_down)

    def back_first(self):
        if self.square:
            self.far = shift(self.outs[1], "context", 1)

    def back_second(self):
        rows = self.own.shape[0]
        if self.square:
            both = add_up(self.outs[0], self.far)
            self.kept, self.go = both[: 2 * rows], both[2 * rows :].astype(BF16)
            self.far = cross(self.go, 1)
        else:
            both = lax.psum_scatter(self.outs[0], ("context", "dp"), scatter_dimension=0, tiled=True)
            self.kept, self.go = both, both[rows:]

    def back_third(self):
        rows = self.own.shape[0]
        if self.square:
            two = add_up(self.kept, self.far)
            self.kept, self.go = two[:rows], two[rows:].astype(BF16)
            self.far = cross(self.go, 0)
        else:
            self.kept, self.far = self.kept[:rows], swap_pair(self.go)

    def home(self):
        result = add_up(self.kept, self.far).astype(BF16)
        size = result.shape[0] // self.line
        parts = [result[size * s : size * (s + 1)] for s in range(self.line)]
        self.result = parts[1]
        self.came = [parts[0]] + [along_line(parts[s], -s) for s in range(1, self.line)]


def on_device(
    residual,
    x_raw,
    z_gate,
    conv_w,
    conv_b,
    xproj_w,
    dtproj_w,
    dt_bias,
    a_rate,
    skip_gain,
    out_w,
    norm_gain,
    route_ids,
    route_w,
    w_gate,
    w_up,
    w_down,
):
    owners, contexts, dps = (lax.axis_size(a) for a in ("expert", "context", "dp"))
    me = lax.axis_index("expert")
    place, half = me // 2, me % 2
    line = owners // 2
    length, channels = x_raw.shape[2:]
    width = residual.shape[3]
    row_count = residual.shape[2]

    values = x_raw[0, 0]
    prior_rim = from_behind(values[length - (CONV - 1) :], "context", 1)
    padded = jnp.concatenate([prior_rim, values], axis=0).astype(F32)
    conv_sum = conv_b[None, :] + sum(
        (
            conv_w[lag_index][None, :] * padded[lag_index : lag_index + length]
            for lag_index in range(CONV)
        )
    )
    mixed_in = jax.nn.silu(conv_sum).astype(BF16)
    projected = jnp.dot(mixed_in, xproj_w, preferred_element_type=F32).astype(BF16)
    shares = projected.reshape(line, length // line, -1)

    def share_of(s):
        return lax.dynamic_index_in_dim(shares, (place + s) % line, 0, keepdims=False)

    share = add_up(share_of(0), *[along_line(share_of(s), s) for s in range(1, line)]).astype(BF16)
    share = add_up(share, swap_pair(share)).astype(BF16)
    pieces = [share] + [along_line(share, s) for s in range(1, line)]

    neg = -a_rate.reshape(NSTATE, channels // LANES, LANES)
    neg = jnp.pad(neg, ((0, 0), (0, SUB - channels // LANES), (0, 0)))
    where = jnp.stack([place, half]).astype(jnp.int32)
    y, total, end, bc = run_scan(where, pieces, dtproj_w, dt_bias[None, :], neg, mixed_in)
    enter = from_behind(end, "context", 1)
    for step in range(contexts - 2):
        decay = jnp.exp(total[-SUB:][None] * neg)
        enter = from_behind(end + decay * enter, "context", 1)
    parts = 4
    part = width // parts
    cut = run_out(
        where, line, parts, y, total, enter, bc, neg, mixed_in, z_gate[0, 0], skip_gain[None, :], out_w
    )
    kept, sent = cut[:parts], cut[parts:]
    sums, got = [], []
    for k in range(parts):
        block = sent[k] if k < 2 else after(sent[k], got[k - 2])
        got.append(swap_pair(block))
    for k in range(parts):
        both = add_up(kept[k], got[k]).reshape(line, row_count, part)
        sums.append(
            add_up(both[0], *[along_line(both[s].astype(BF16), s) for s in range(1, line)])
        )
    mixer_out = jnp.concatenate(sums, axis=1)

    stream_f = (residual[0, 0].astype(F32) + mixer_out).astype(BF16).astype(F32)
    normed = (
        stream_f
        * lax.rsqrt(jnp.mean(stream_f * stream_f, axis=1, keepdims=True) + 1e-05)
        * norm_gain[None, :]
    ).astype(BF16)
    ids, weights = route_ids[0, 0], route_w[0, 0]
    capacity = min(row_count, 8 * ((3 * row_count * TOP + 16 * line - 1) // (16 * line)))
    chunks = capacity // 8
    named = jnp.any(ids[:, :, None] == jnp.arange(line, dtype=jnp.int32), axis=1)
    rank = jnp.cumsum(named.astype(jnp.int32), axis=0) - 1
    chosen = ids[:, :, None] == jnp.arange(line, dtype=jnp.int32)
    rank_of = jnp.sum(jnp.where(chosen, rank[:, None, :], 0), axis=2)
    slot_of = (rank_of // 8) * (line * 8) + (ids - place + line) % line * 8 + rank_of % 8
    slots = jnp.arange(line * capacity, dtype=jnp.int32)
    hits = slot_of[:, :, None] == slots
    placing = jnp.any(hits, axis=1).astype(BF16)
    weighting = jnp.sum(jnp.where(hits, weights[:, :, None], 0.0), axis=1)
    square = contexts == 2 and dps == 2
    rows = line * 8
    chunk = []
    for k in range(chunks):
        packed = lax.dot_general(
            placing[:, k * rows : (k + 1) * rows],
            normed,
            (((0,), (0,)), ((), ())),
            preferred_element_type=F32,
        ).astype(BF16)
        chunk.append(Chunk(packed, line, square))
        chunk[k].send()
    for k in range(chunks):
        chunk[k].first()
        chunk[k].second()
        chunk[k].third()
    for k in range(chunks):
        before, between = [], []
        if k + 1 < chunks:
            before.append(chunk[k + 1].two)
            between.append(chunk[k + 1].four)
        if k + 2 < chunks:
            between.append(chunk[k + 2].own)
        if k >= 1:
            between.append(chunk[k - 1].go)
            chunk[k - 1].back_third()
        if k >= 2:
            before.append(chunk[k - 2].result_go)
        chunk[k].work_first(w_gate[0], w_up[0], *before)
        chunk[k].work_second(w_down[0], *between)
        chunk[k].back_first()
        chunk[k].back_second()
        chunk[k].result_go = chunk[k].go
    for k in range(chunks):
        if k == chunks - 1:
            chunk[k].back_third()
        chunk[k].home()
    expert_sum = 0.0
    for k in range(chunks):
        expert_sum = expert_sum + jnp.dot(
            weighting[:, k * rows : (k + 1) * rows],
            jnp.concatenate(chunk[k].came, axis=0).astype(F32),
            precision=lax.Precision.HIGHEST,
            preferred_element_type=F32,
        )
    mixed = (stream_f + expert_sum).astype(BF16)
    return mixed.reshape(1, 1, row_count, width)


def solution(mesh):
    placed = (
        P("dp", "context", "expert", None),
        P("dp", "context", None, "expert"),
        P("dp", "context", None, "expert"),
        P(None, "expert"),
        P("expert"),
        P("expert", None),
        P(None, "expert"),
        P("expert"),
        P(None, "expert"),
        P("expert"),
        P("expert", None),
        P(),
        P("dp", "context", "expert", None),
        P("dp", "context", "expert", None),
        P("expert", None, ("context", "dp")),
        P("expert", None, ("context", "dp")),
        P("expert", ("context", "dp"), None),
    )
    return jax.shard_map(
        on_device,
        mesh=mesh,
        in_specs=placed,
        out_specs=P("dp", "context", "expert", None),
        check_vma=False,
    )
```

```python
import functools

import jax
import jax.numpy as jnp
from jax import lax
from jax.experimental import pallas as pl
from jax.experimental.pallas import tpu as pltpu
from jax.sharding import PartitionSpec as P

NSTATE = 16
DT_RANK = 256
CONV = 4
TOP = 2
LANES = 128
SUB = 8
F32 = jnp.float32
BF16 = jnp.bfloat16
MIB = 1 << 20


def from_behind(block, axis, distance):
    devices = range(lax.axis_size(axis))
    route = [(i - distance, i) for i in devices if i - distance in devices]
    return lax.ppermute(block, axis, route)


def shift(block, axis, distance):
    size = lax.axis_size(axis)
    return lax.ppermute(block, axis, [(i, (i + distance) % size) for i in range(size)])


def swap_pair(block):
    size = lax.axis_size("expert")
    return lax.ppermute(block, "expert", [(i, i ^ 1) for i in range(size)])


def cost(flops, bytes_accessed, transcendentals=0):
    return pl.CostEstimate(
        flops=int(flops), bytes_accessed=int(bytes_accessed), transcendentals=int(transcendentals)
    )


def spread_rows(values, wide_ref):
    length, count = values.shape
    col = lax.broadcasted_iota(jnp.int32, (count, count * LANES), 1)
    row = lax.broadcasted_iota(jnp.int32, (count, count * LANES), 0)
    ones = jnp.where((col >= row * LANES) & (col < (row + 1) * LANES), 1.0, 0.0).astype(BF16)
    out = jnp.dot(values, ones, preferred_element_type=F32)
    for n in range(count):
        wide_ref[pl.ds(n * length, length), :] = out[:, n * LANES : (n + 1) * LANES]


def scan_kernel(groups, line, place_ref, *refs):
    pieces, refs = refs[:line], refs[line:]
    w_ref, bias_ref, neg_ref, x_ref, y_ref, sum_ref, end_ref, bc_ref = refs[:8]
    low_ref, step_ref, drive_ref, wide_ref = refs[8:]
    length = x_ref.shape[0]
    share = length // line
    for s in range(line):
        start = pl.multiple_of((place_ref[0] + (line - s)) % line * share, share)
        low_ref[pl.ds(start, share), :] = pieces[s][:, :DT_RANK]
        bc_ref[pl.ds(start, share), :] = pieces[s][:, DT_RANK:]
    spread_rows(bc_ref[...], wide_ref)
    for g in range(SUB):
        rows = pl.ds(g, length, stride=SUB)
        if g >= groups:
            step_ref[rows, :] = jnp.zeros((length, LANES), F32)
            drive_ref[rows, :] = jnp.zeros((length, LANES), F32)
            continue
        cols = pl.ds(g * LANES, LANES)
        raw = jnp.dot(low_ref[...], w_ref[:, cols], preferred_element_type=F32) + bias_ref[:, cols]
        step = jnp.maximum(raw, 0.0) + jnp.log1p(jnp.exp(-jnp.abs(raw)))
        step_ref[rows, :] = step
        drive_ref[rows, :] = step * x_ref[:, cols].astype(F32)

    def block(k, carry):
        states, total = list(carry[0]), carry[1]
        for u in range(SUB):
            t = k * SUB + u
            here = pl.ds(pl.multiple_of(t * SUB, SUB), SUB)
            step, drive = step_ref[here, :], drive_ref[here, :]
            total = total + step
            out = jnp.zeros((SUB, LANES), F32)
            for n in range(NSTATE):
                decay = jnp.exp(step * neg_ref[n])
                b = wide_ref[pl.ds(n * length + t, 1), :]
                c = wide_ref[pl.ds((NSTATE + n) * length + t, 1), :]
                states[n] = states[n] * decay + drive * b
                out = out + states[n] * c
            y_ref[here, :] = out
            sum_ref[here, :] = total
        return tuple(states), total

    zero = jnp.zeros((SUB, LANES), F32)
    states, total = lax.fori_loop(0, length // SUB, block, ((zero,) * NSTATE, zero))
    for n in range(NSTATE):
        end_ref[n] = states[n]


def run_scan(place, pieces, w, bias, neg, x):
    length, channels = x.shape
    vmem = pl.BlockSpec(memory_space=pltpu.VMEM)
    tall = jax.ShapeDtypeStruct((length * SUB, LANES), F32)
    return pl.pallas_call(
        functools.partial(scan_kernel, channels // LANES, len(pieces)),
        out_shape=(
            tall,
            tall,
            jax.ShapeDtypeStruct((NSTATE, SUB, LANES), F32),
            jax.ShapeDtypeStruct((length, 2 * NSTATE), BF16),
        ),
        in_specs=[pl.BlockSpec(memory_space=pltpu.SMEM)] + [vmem] * (len(pieces) + 4),
        out_specs=(vmem,) * 4,
        scratch_shapes=[
            pltpu.VMEM((length, DT_RANK), BF16),
            pltpu.VMEM((length * SUB, LANES), F32),
            pltpu.VMEM((length * SUB, LANES), F32),
            pltpu.VMEM((2 * NSTATE * length, LANES), F32),
        ],
        compiler_params=pltpu.CompilerParams(vmem_limit_bytes=20 * MIB),
        cost_estimate=cost(2e8, 4 * MIB, NSTATE * length * channels),
        name="state_scan",
    )(place, *pieces, w, bias, neg, x)


def out_kernel(groups, line, parts, at_ref, y_ref, sum_ref, enter_ref, bc_ref, neg_ref, x_ref, z_ref,
               skip_ref, w_hbm, *refs):
    kept_refs, sent_refs = refs[:parts], refs[parts : 2 * parts]
    full_ref, wide_ref, gated_ref, order_ref, w_ref, sems = refs[2 * parts :]
    length = x_ref.shape[0]
    part = w_ref.shape[1] // parts

    def fetch(j):
        cols = pl.ds(j * part, part)
        return pltpu.make_async_copy(w_hbm.at[:, cols], w_ref.at[:, cols], sems.at[j])

    for j in range(parts):
        fetch(j).start()
    spread_rows(bc_ref[:, NSTATE:], wide_ref)

    def block(k, carry):
        for u in range(SUB):
            t = k * SUB + u
            here = pl.ds(pl.multiple_of(t * SUB, SUB), SUB)
            total = sum_ref[here, :]
            out = y_ref[here, :]
            for n in range(NSTATE):
                c = wide_ref[pl.ds(n * length + t, 1), :]
                out = out + jnp.exp(total * neg_ref[n]) * enter_ref[n] * c
            full_ref[here, :] = out
        return carry

    lax.fori_loop(0, length // SUB, block, 0)
    for g in range(groups):
        cols = pl.ds(g * LANES, LANES)
        mixed_in = x_ref[:, cols].astype(F32)
        read = full_ref[pl.ds(g, length, stride=SUB), :] + skip_ref[:, cols] * mixed_in
        z = z_ref[:, cols].astype(F32)
        gated_ref[:, cols] = (read * (z / (1.0 + jnp.exp(-z)))).astype(BF16)
    place, half = at_ref[0], at_ref[1]
    count = length // 2
    piece = count // line
    for k in range(line):
        for r in range(2):
            source = pl.multiple_of((2 * ((place + k) % line) + (half ^ r)) * piece, piece)
            order_ref[pl.ds(r * count + k * piece, piece), :] = gated_ref[pl.ds(source, piece), :]
    for j in range(parts):
        cols = pl.ds(j * part, part)
        fetch(j).wait()
        out = jnp.dot(order_ref[...], w_ref[:, cols], preferred_element_type=F32).astype(BF16)
        kept_refs[j][...] = out[:count]
        sent_refs[j][...] = out[count:]


def run_out(at, line, parts, y, total, enter, bc, neg, x, z, skip, w):
    length, channels = x.shape
    wide = w.shape[1]
    vmem = pl.BlockSpec(memory_space=pltpu.VMEM)
    return pl.pallas_call(
        functools.partial(out_kernel, channels // LANES, line, parts),
        out_shape=(jax.ShapeDtypeStruct((length // 2, wide // parts), BF16),) * (2 * parts),
        in_specs=[pl.BlockSpec(memory_space=pltpu.SMEM)] + [vmem] * 8 + [pl.BlockSpec(memory_space=pl.ANY)],
        out_specs=(vmem,) * (2 * parts),
        scratch_shapes=[
            pltpu.VMEM((length * SUB, LANES), F32),
            pltpu.VMEM((NSTATE * length, LANES), F32),
            pltpu.VMEM((length, channels), BF16),
            pltpu.VMEM((length, channels), BF16),
            pltpu.VMEM((channels, wide), BF16),
            pltpu.SemaphoreType.DMA((parts,)),
        ],
        compiler_params=pltpu.CompilerParams(vmem_limit_bytes=52 * MIB),
        cost_estimate=cost(
            2 * length * channels * wide, 2 * channels * wide + 8 * MIB, NSTATE * length * channels
        ),
        name="readout_project",
    )(at, y, total, enter, bc, neg, x, z, skip, w)


def gate_up_kernel(count, tile, *refs):
    pieces, (gate_hbm, up_hbm, out_ref, rows_ref, gate_ref, up_ref, sems) = refs[:count], refs[count:]
    copies, at = [], 0
    for k, piece in enumerate(pieces):
        rows = pl.ds(at, piece.shape[0])
        copies.append(pltpu.make_async_copy(piece, rows_ref.at[rows, :], sems.at[k]))
        at += piece.shape[0]
    fetches = []
    for j in range(out_ref.shape[1] // tile):
        cols = pl.ds(j * tile, tile)
        for k, (source, target) in enumerate([(gate_hbm, gate_ref), (up_hbm, up_ref)]):
            sem = sems.at[count + 2 * j + k]
            fetches.append(pltpu.make_async_copy(source.at[:, cols], target.at[:, cols], sem))
    for copy in copies + fetches:
        copy.start()
    for copy in copies:
        copy.wait()
    for j in range(out_ref.shape[1] // tile):
        cols = pl.ds(j * tile, tile)
        fetches[2 * j].wait()
        gate = jnp.dot(rows_ref[...], gate_ref[:, cols], preferred_element_type=F32)
        fetches[2 * j + 1].wait()
        up = jnp.dot(rows_ref[...], up_ref[:, cols], preferred_element_type=F32)
        out_ref[:, cols] = (gate / (1.0 + jnp.exp(-gate)) * up).astype(BF16)


def gate_up(pieces, w_gate, w_up):
    depth, hidden = w_gate.shape
    rows = sum(p.shape[0] for p in pieces)
    tile = min(256, hidden)
    anywhere = pl.BlockSpec(memory_space=pl.ANY)
    return pl.pallas_call(
        functools.partial(gate_up_kernel, len(pieces), tile),
        out_shape=jax.ShapeDtypeStruct((rows, hidden), BF16),
        in_specs=[anywhere] * (len(pieces) + 2),
        out_specs=pl.BlockSpec(memory_space=pltpu.VMEM),
        scratch_shapes=[
            pltpu.VMEM((rows, depth), BF16),
            pltpu.VMEM((depth, hidden), BF16),
            pltpu.VMEM((depth, hidden), BF16),
            pltpu.SemaphoreType.DMA((len(pieces) + 2 * (hidden // tile),)),
        ],
        compiler_params=pltpu.CompilerParams(vmem_limit_bytes=52 * MIB),
        cost_estimate=cost(4 * rows * depth * hidden, 4 * depth * hidden + 2 * rows * depth),
        name="gate_up",
    )(*pieces, w_gate, w_up)


def down_kernel(first, tile, rows_ref, w_hbm, *refs):
    outs, (w_ref, sems) = refs[:-2], refs[-2:]
    width = w_ref.shape[1]
    fetches = []
    for j in range(width // tile):
        source, target = pl.ds(first + j * tile, tile), pl.ds(j * tile, tile)
        fetches.append(
            pltpu.make_async_copy(w_hbm.at[:, source], w_ref.at[:, target], sems.at[j])
        )
    for copy in fetches:
        copy.start()
    for j in range(width // tile):
        cols = pl.ds(j * tile, tile)
        fetches[j].wait()
        out = jnp.dot(rows_ref[...], w_ref[:, cols], preferred_element_type=F32).astype(BF16)
        start = 0
        for ref in outs:
            ref[:, cols] = out[start : start + ref.shape[0]]
            start += ref.shape[0]


def down(rows, sizes, w_down, first, width):
    hidden = w_down.shape[0]
    tile = min(512, width)
    vmem = pl.BlockSpec(memory_space=pltpu.VMEM)
    return pl.pallas_call(
        functools.partial(down_kernel, first, tile),
        out_shape=tuple(jax.ShapeDtypeStruct((n, width), BF16) for n in sizes),
        in_specs=[vmem, pl.BlockSpec(memory_space=pl.ANY)],
        out_specs=(vmem,) * len(sizes),
        scratch_shapes=[pltpu.VMEM((hidden, width), BF16), pltpu.SemaphoreType.DMA((width // tile,))],
        compiler_params=pltpu.CompilerParams(vmem_limit_bytes=52 * MIB),
        cost_estimate=cost(
            2 * rows.shape[0] * hidden * width, 2 * hidden * width + 2 * rows.shape[0] * (hidden + width)
        ),
        name="down",
    )(rows, w_down)


def add_up(*parts):
    return sum(p.astype(F32) for p in parts)


def along_line(block, distance):
    size = lax.axis_size("expert")
    return lax.ppermute(block, "expert", [(e, (e + 2 * distance) % size) for e in range(size)])


def cross(block, turn):
    owners, dps = lax.axis_size("expert"), lax.axis_size("dp")
    route = []
    for e in range(owners):
        for core in range(2):
            for d in range(dps):
                to = (e ^ 1, core, d) if core == turn else (e, core, d ^ 1)
                route.append(((e * 2 + core) * dps + d, (to[0] * 2 + core) * dps + to[2]))
    return lax.ppermute(block, ("expert", "context", "dp"), route)


def after(blocks, *others):
    return lax.optimization_barrier((blocks, others))[0]


def send_rows(packed, line):
    size = packed.shape[0] // line
    parts = [packed[size * s : size * (s + 1)] for s in range(line)]
    return [parts[0]] + [along_line(parts[s], s) for s in range(1, line)]


def send_home(result, line):
    size = result.shape[0] // line
    parts = [result[size * s : size * (s + 1)] for s in range(line)]
    came = [parts[0]] + [along_line(parts[s], -s) for s in range(1, line)]
    return jnp.concatenate(came, axis=0)


def plain_experts(packed, line, w_gate, w_up, w_down):
    own = jnp.concatenate(send_rows(packed, line), axis=0)
    rows = jnp.concatenate([own, swap_pair(own)], axis=0)
    rows = lax.all_gather(rows, ("context", "dp"), axis=0, tiled=True)
    hidden = gate_up([rows], w_gate, w_up)
    out = down(hidden, (rows.shape[0],), w_down, 0, w_down.shape[1])[0]
    mine = lax.psum_scatter(out, ("context", "dp"), scatter_dimension=0, tiled=True)
    count = own.shape[0]
    return send_home(add_up(mine[:count], swap_pair(mine[count:])).astype(BF16), line)


def square_experts(early, late, line, w_gate, w_up, w_down):
    width = w_down.shape[1]
    half = width // 2

    def pieces(two, four):
        return [two, four, shift(two, "context", 1), shift(four, "context", 1)]

    def home_first(outs):
        rows = outs[0].shape[0] // 4
        both = add_up(outs[0], shift(outs[1], "context", 1))
        return both[: 2 * rows], both[2 * rows :].astype(BF16)

    def home_second(kept, far):
        rows = kept.shape[0] // 2
        two = add_up(kept, far)
        return two[:rows], two[rows:].astype(BF16)

    early_came = send_rows(early, line)
    late_came = send_rows(after(late, early_came[1]), line)
    early_own = jnp.concatenate(early_came, axis=0)
    early_near = cross(early_own, 0)
    early_two = jnp.concatenate([early_own, early_near], axis=0)
    early_four = cross(early_two, 1)
    late_came[0] = after(late_came[0], early_near)
    late_own = jnp.concatenate(late_came, axis=0)
    late_near = cross(late_own, 0)
    sizes = (4 * early_own.shape[0],) * 2
    early_hidden = gate_up(after(pieces(early_two, early_four), late_own), w_gate, w_up)

    late_two = jnp.concatenate([after(late_own, early_hidden), late_near], axis=0)
    late_four = cross(late_two, 1)
    early_out = down(after(early_hidden, late_two), sizes, w_down, 0, width)
    late_four = after(late_four, early_out)
    early_kept, early_go = home_first(after(early_out, late_four))
    early_far = cross(early_go, 1)
    sizes = (4 * late_own.shape[0],) * 2
    late_hidden = gate_up(after(pieces(late_two, late_four), early_go), w_gate, w_up)

    early_kept, early_go = home_second(after(early_kept, late_hidden), early_far)
    early_far = cross(early_go, 0)
    out_left = down(after(late_hidden, early_go), sizes, w_down, 0, half)
    early_result = add_up(after(early_kept, out_left), early_far).astype(BF16)
    early_back = send_home(early_result, line)
    left = home_first(out_left)
    left_far = cross(left[1], 1)
    out_right = down(after(late_hidden, early_result, left[1]), sizes, w_down, half, half)
    left = home_second(after(left[0], out_right), left_far)
    left_far = cross(left[1], 0)
    right = home_first(out_right)
    right_far = cross(right[1], 1)
    right = home_second(after(right[0], left[1]), right_far)
    right_far = cross(right[1], 0)
    late_back = []
    for kept, far in ((left[0], left_far), (right[0], right_far)):
        late_back.append(send_home(add_up(kept, far).astype(BF16), line))
    return early_back, jnp.concatenate(late_back, axis=1)


def on_device(
    residual,
    x_raw,
    z_gate,
    conv_w,
    conv_b,
    xproj_w,
    dtproj_w,
    dt_bias,
    a_rate,
    skip_gain,
    out_w,
    norm_gain,
    route_ids,
    route_w,
    w_gate,
    w_up,
    w_down,
):
    owners, contexts, dps = (lax.axis_size(a) for a in ("expert", "context", "dp"))
    me = lax.axis_index("expert")
    place, half = me // 2, me % 2
    line = owners // 2
    length, channels = x_raw.shape[2:]
    width = residual.shape[3]
    row_count = residual.shape[2]

    values = x_raw[0, 0]
    prior_rim = from_behind(values[length - (CONV - 1) :], "context", 1)
    padded = jnp.concatenate([prior_rim, values], axis=0).astype(F32)
    conv_sum = conv_b[None, :] + sum(
        (
            conv_w[lag_index][None, :] * padded[lag_index : lag_index + length]
            for lag_index in range(CONV)
        )
    )
    mixed_in = jax.nn.silu(conv_sum).astype(BF16)
    projected = jnp.dot(mixed_in, xproj_w, preferred_element_type=F32).astype(BF16)
    shares = projected.reshape(line, length // line, -1)

    def share_of(s):
        return lax.dynamic_index_in_dim(shares, (place + s) % line, 0, keepdims=False)

    share = add_up(share_of(0), *[along_line(share_of(s), s) for s in range(1, line)]).astype(BF16)
    share = add_up(share, swap_pair(share)).astype(BF16)
    pieces = [share] + [along_line(share, s) for s in range(1, line)]

    neg = -a_rate.reshape(NSTATE, channels // LANES, LANES)
    neg = jnp.pad(neg, ((0, 0), (0, SUB - channels // LANES), (0, 0)))
    where = jnp.stack([place, half]).astype(jnp.int32)
    y, total, end, bc = run_scan(where, pieces, dtproj_w, dt_bias[None, :], neg, mixed_in)
    enter = from_behind(end, "context", 1)
    for step in range(contexts - 2):
        decay = jnp.exp(total[-SUB:][None] * neg)
        enter = from_behind(end + decay * enter, "context", 1)
    parts = 4
    part = width // parts
    cut = run_out(
        where, line, parts, y, total, enter, bc, neg, mixed_in, z_gate[0, 0], skip_gain[None, :], out_w
    )
    kept, sent = cut[:parts], cut[parts:]
    sums, got = [], [swap_pair(sent[k]) for k in range(2)]
    for k in range(parts):
        mine = kept[k] if k == 0 else after(kept[k], came[1])
        both = add_up(mine, got[k]).astype(BF16).reshape(line, row_count, part)
        if k + 2 < parts:
            got.append(swap_pair(after(sent[k + 2], both)))
        came = [both[0]] + [along_line(both[s], s) for s in range(1, line)]
        sums.append(add_up(*came))
    mixer_out = jnp.concatenate(sums, axis=1)

    stream_f = (residual[0, 0].astype(F32) + mixer_out).astype(BF16).astype(F32)
    normed = (
        stream_f
        * lax.rsqrt(jnp.mean(stream_f * stream_f, axis=1, keepdims=True) + 1e-05)
        * norm_gain[None, :]
    ).astype(BF16)
    ids, weights = route_ids[0, 0], route_w[0, 0]
    capacity = min(row_count, 8 * ((3 * row_count * TOP + 16 * line - 1) // (16 * line)))
    cuts = (0, 8, capacity) if contexts == 2 and dps == 2 and capacity > 8 else (0, capacity)
    named = jnp.any(ids[:, :, None] == jnp.arange(line, dtype=jnp.int32), axis=1)
    rank = jnp.cumsum(named.astype(jnp.int32), axis=0) - 1
    chosen = ids[:, :, None] == jnp.arange(line, dtype=jnp.int32)
    rank_of = jnp.sum(jnp.where(chosen, rank[:, None, :], 0), axis=2)
    away = (ids - place + line) % line
    placing, weighting, packed = [], [], []
    for low, high in zip(cuts[:-1], cuts[1:]):
        inside = (rank_of >= low) & (rank_of < high)
        slot_of = jnp.where(inside, away * (high - low) + rank_of - low, -1)
        hits = slot_of[:, :, None] == jnp.arange(line * (high - low), dtype=jnp.int32)
        placing = jnp.any(hits, axis=1).astype(BF16)
        weighting.append(jnp.sum(jnp.where(hits, weights[:, :, None], 0.0), axis=1))
        rows = lax.dot_general(
            placing, normed, (((0,), (0,)), ((), ())), preferred_element_type=F32
        )
        packed.append(rows.astype(BF16))
    if len(packed) == 2:
        back = square_experts(*packed, line, w_gate[0], w_up[0], w_down[0])
    else:
        back = [plain_experts(packed[0], line, w_gate[0], w_up[0], w_down[0])]
    expert_sum = jnp.dot(
        jnp.concatenate(weighting, axis=1),
        jnp.concatenate(back, axis=0).astype(F32),
        precision=lax.Precision.HIGHEST,
        preferred_element_type=F32,
    )
    mixed = (stream_f + expert_sum).astype(BF16)
    return mixed.reshape(1, 1, row_count, width)


def solution(mesh):
    placed = (
        P("dp", "context", "expert", None),
        P("dp", "context", None, "expert"),
        P("dp", "context", None, "expert"),
        P(None, "expert"),
        P("expert"),
        P("expert", None),
        P(None, "expert"),
        P("expert"),
        P(None, "expert"),
        P("expert"),
        P("expert", None),
        P(),
        P("dp", "context", "expert", None),
        P("dp", "context", "expert", None),
        P("expert", None, ("context", "dp")),
        P("expert", None, ("context", "dp")),
        P("expert", ("context", "dp"), None),
    )
    return jax.shard_map(
        on_device,
        mesh=mesh,
        in_specs=placed,
        out_specs=P("dp", "context", "expert", None),
        check_vma=False,
    )
```

```python
import functools

import jax
import jax.numpy as jnp
from jax import lax
from jax.experimental import pallas as pl
from jax.experimental.pallas import tpu as pltpu
from jax.sharding import PartitionSpec as P

NSTATE = 16
DT_RANK = 256
CONV = 4
TOP = 2
LANES = 128
SUB = 8
F32 = jnp.float32
BF16 = jnp.bfloat16
MIB = 1 << 20


def from_behind(block, axis, distance):
    devices = range(lax.axis_size(axis))
    route = [(i - distance, i) for i in devices if i - distance in devices]
    return lax.ppermute(block, axis, route)


def shift(block, axis, distance):
    size = lax.axis_size(axis)
    return lax.ppermute(block, axis, [(i, (i + distance) % size) for i in range(size)])


def swap_pair(block):
    size = lax.axis_size("expert")
    return lax.ppermute(block, "expert", [(i, i ^ 1) for i in range(size)])


def cost(flops, bytes_accessed, transcendentals=0):
    return pl.CostEstimate(
        flops=int(flops), bytes_accessed=int(bytes_accessed), transcendentals=int(transcendentals)
    )


def spread_rows(values, wide_ref):
    length, count = values.shape
    col = lax.broadcasted_iota(jnp.int32, (count, count * LANES), 1)
    row = lax.broadcasted_iota(jnp.int32, (count, count * LANES), 0)
    ones = jnp.where((col >= row * LANES) & (col < (row + 1) * LANES), 1.0, 0.0).astype(BF16)
    out = jnp.dot(values, ones, preferred_element_type=F32)
    for n in range(count):
        wide_ref[pl.ds(n * length, length), :] = out[:, n * LANES : (n + 1) * LANES]


def scan_kernel(groups, line, place_ref, *refs):
    pieces, refs = refs[:line], refs[line:]
    w_ref, bias_ref, neg_ref, x_ref, y_ref, sum_ref, end_ref, bc_ref = refs[:8]
    low_ref, step_ref, drive_ref, wide_ref = refs[8:]
    length = x_ref.shape[0]
    share = length // line
    for s in range(line):
        start = pl.multiple_of((place_ref[0] + (line - s)) % line * share, share)
        low_ref[pl.ds(start, share), :] = pieces[s][:, :DT_RANK]
        bc_ref[pl.ds(start, share), :] = pieces[s][:, DT_RANK:]
    spread_rows(bc_ref[...], wide_ref)
    for g in range(SUB):
        rows = pl.ds(g, length, stride=SUB)
        if g >= groups:
            step_ref[rows, :] = jnp.zeros((length, LANES), F32)
            drive_ref[rows, :] = jnp.zeros((length, LANES), F32)
            continue
        cols = pl.ds(g * LANES, LANES)
        raw = jnp.dot(low_ref[...], w_ref[:, cols], preferred_element_type=F32) + bias_ref[:, cols]
        step = jnp.maximum(raw, 0.0) + jnp.log1p(jnp.exp(-jnp.abs(raw)))
        step_ref[rows, :] = step
        drive_ref[rows, :] = step * x_ref[:, cols].astype(F32)

    def block(k, carry):
        states, total = list(carry[0]), carry[1]
        for u in range(SUB):
            t = k * SUB + u
            here = pl.ds(pl.multiple_of(t * SUB, SUB), SUB)
            step, drive = step_ref[here, :], drive_ref[here, :]
            total = total + step
            out = jnp.zeros((SUB, LANES), F32)
            for n in range(NSTATE):
                decay = jnp.exp(step * neg_ref[n])
                b = wide_ref[pl.ds(n * length + t, 1), :]
                c = wide_ref[pl.ds((NSTATE + n) * length + t, 1), :]
                states[n] = states[n] * decay + drive * b
                out = out + states[n] * c
            y_ref[here, :] = out
            sum_ref[here, :] = total
        return tuple(states), total

    zero = jnp.zeros((SUB, LANES), F32)
    states, total = lax.fori_loop(0, length // SUB, block, ((zero,) * NSTATE, zero))
    for n in range(NSTATE):
        end_ref[n] = states[n]


def run_scan(place, pieces, w, bias, neg, x):
    length, channels = x.shape
    vmem = pl.BlockSpec(memory_space=pltpu.VMEM)
    tall = jax.ShapeDtypeStruct((length * SUB, LANES), F32)
    return pl.pallas_call(
        functools.partial(scan_kernel, channels // LANES, len(pieces)),
        out_shape=(
            tall,
            tall,
            jax.ShapeDtypeStruct((NSTATE, SUB, LANES), F32),
            jax.ShapeDtypeStruct((length, 2 * NSTATE), BF16),
        ),
        in_specs=[pl.BlockSpec(memory_space=pltpu.SMEM)] + [vmem] * (len(pieces) + 4),
        out_specs=(vmem,) * 4,
        scratch_shapes=[
            pltpu.VMEM((length, DT_RANK), BF16),
            pltpu.VMEM((length * SUB, LANES), F32),
            pltpu.VMEM((length * SUB, LANES), F32),
            pltpu.VMEM((2 * NSTATE * length, LANES), F32),
        ],
        compiler_params=pltpu.CompilerParams(vmem_limit_bytes=20 * MIB),
        cost_estimate=cost(2e8, 4 * MIB, NSTATE * length * channels),
        name="state_scan",
    )(place, *pieces, w, bias, neg, x)


def out_kernel(groups, line, parts, at_ref, y_ref, sum_ref, enter_ref, bc_ref, neg_ref, x_ref, z_ref,
               skip_ref, w_hbm, *refs):
    kept_refs, sent_refs = refs[:parts], refs[parts : 2 * parts]
    full_ref, wide_ref, gated_ref, order_ref, w_ref, sems = refs[2 * parts :]
    length = x_ref.shape[0]
    part = w_ref.shape[1] // parts

    def fetch(j):
        cols = pl.ds(j * part, part)
        return pltpu.make_async_copy(w_hbm.at[:, cols], w_ref.at[:, cols], sems.at[j])

    for j in range(parts):
        fetch(j).start()
    spread_rows(bc_ref[:, NSTATE:], wide_ref)

    def block(k, carry):
        for u in range(SUB):
            t = k * SUB + u
            here = pl.ds(pl.multiple_of(t * SUB, SUB), SUB)
            total = sum_ref[here, :]
            out = y_ref[here, :]
            for n in range(NSTATE):
                c = wide_ref[pl.ds(n * length + t, 1), :]
                out = out + jnp.exp(total * neg_ref[n]) * enter_ref[n] * c
            full_ref[here, :] = out
        return carry

    lax.fori_loop(0, length // SUB, block, 0)
    for g in range(groups):
        cols = pl.ds(g * LANES, LANES)
        mixed_in = x_ref[:, cols].astype(F32)
        read = full_ref[pl.ds(g, length, stride=SUB), :] + skip_ref[:, cols] * mixed_in
        z = z_ref[:, cols].astype(F32)
        gated_ref[:, cols] = (read * (z / (1.0 + jnp.exp(-z)))).astype(BF16)
    place, half = at_ref[0], at_ref[1]
    count = length // 2
    piece = count // line
    for k in range(line):
        for r in range(2):
            source = pl.multiple_of((2 * ((place + k) % line) + (half ^ r)) * piece, piece)
            order_ref[pl.ds(r * count + k * piece, piece), :] = gated_ref[pl.ds(source, piece), :]
    tile = min(256, part)
    for j in range(parts):
        fetch(j).wait()

        def step(i, carry):
            target = pl.ds(pl.multiple_of(i * tile, tile), tile)
            source = pl.ds(pl.multiple_of(j * part + i * tile, tile), tile)
            out = jnp.dot(order_ref[...], w_ref[:, source], preferred_element_type=F32).astype(BF16)
            kept_refs[j][:, target] = out[:count]
            sent_refs[j][:, target] = out[count:]
            return carry

        lax.fori_loop(0, part // tile, step, 0)


def run_out(at, line, parts, y, total, enter, bc, neg, x, z, skip, w):
    length, channels = x.shape
    wide = w.shape[1]
    vmem = pl.BlockSpec(memory_space=pltpu.VMEM)
    return pl.pallas_call(
        functools.partial(out_kernel, channels // LANES, line, parts),
        out_shape=(jax.ShapeDtypeStruct((length // 2, wide // parts), BF16),) * (2 * parts),
        in_specs=[pl.BlockSpec(memory_space=pltpu.SMEM)] + [vmem] * 8 + [pl.BlockSpec(memory_space=pl.ANY)],
        out_specs=(vmem,) * (2 * parts),
        scratch_shapes=[
            pltpu.VMEM((length * SUB, LANES), F32),
            pltpu.VMEM((NSTATE * length, LANES), F32),
            pltpu.VMEM((length, channels), BF16),
            pltpu.VMEM((length, channels), BF16),
            pltpu.VMEM((channels, wide), BF16),
            pltpu.SemaphoreType.DMA((parts,)),
        ],
        compiler_params=pltpu.CompilerParams(vmem_limit_bytes=48 * MIB),
        cost_estimate=cost(
            2 * length * channels * wide, 2 * channels * wide + 8 * MIB, NSTATE * length * channels
        ),
        name="readout_project",
    )(at, y, total, enter, bc, neg, x, z, skip, w)


def gate_up_kernel(count, tile, *refs):
    pieces, (gate_hbm, up_hbm, out_ref, rows_ref, gate_ref, up_ref, sems) = refs[:count], refs[count:]
    copies, at = [], 0
    for k, piece in enumerate(pieces):
        rows = pl.ds(at, piece.shape[0])
        copies.append(pltpu.make_async_copy(piece, rows_ref.at[rows, :], sems.at[k]))
        at += piece.shape[0]
    steps = out_ref.shape[1] // tile

    def fetch(j, k):
        cols = pl.ds(pl.multiple_of(j * tile, tile), tile)
        source, target = ((gate_hbm, gate_ref), (up_hbm, up_ref))[k]
        sem = sems.at[count + 2 * j + k]
        return pltpu.make_async_copy(source.at[:, cols], target.at[:, cols], sem)

    for copy in copies:
        copy.start()
    for j in range(steps):
        fetch(j, 0).start()
        fetch(j, 1).start()
    for copy in copies:
        copy.wait()

    def step(j, carry):
        cols = pl.ds(pl.multiple_of(j * tile, tile), tile)
        fetch(j, 0).wait()
        gate = jnp.dot(rows_ref[...], gate_ref[:, cols], preferred_element_type=F32)
        fetch(j, 1).wait()
        up = jnp.dot(rows_ref[...], up_ref[:, cols], preferred_element_type=F32)
        out_ref[:, cols] = (gate / (1.0 + jnp.exp(-gate)) * up).astype(BF16)
        return carry

    lax.fori_loop(0, steps, step, 0)


def gate_up(pieces, w_gate, w_up):
    depth, hidden = w_gate.shape
    rows = sum(p.shape[0] for p in pieces)
    tile = min(256, hidden)
    anywhere = pl.BlockSpec(memory_space=pl.ANY)
    return pl.pallas_call(
        functools.partial(gate_up_kernel, len(pieces), tile),
        out_shape=jax.ShapeDtypeStruct((rows, hidden), BF16),
        in_specs=[anywhere] * (len(pieces) + 2),
        out_specs=pl.BlockSpec(memory_space=pltpu.VMEM),
        scratch_shapes=[
            pltpu.VMEM((rows, depth), BF16),
            pltpu.VMEM((depth, hidden), BF16),
            pltpu.VMEM((depth, hidden), BF16),
            pltpu.SemaphoreType.DMA((len(pieces) + 2 * (hidden // tile),)),
        ],
        compiler_params=pltpu.CompilerParams(vmem_limit_bytes=52 * MIB),
        cost_estimate=cost(4 * rows * depth * hidden, 4 * depth * hidden + 2 * rows * depth),
        name="gate_up",
    )(*pieces, w_gate, w_up)


def down_kernel(first, tile, rows_ref, w_hbm, *refs):
    outs, (w_ref, sems) = refs[:-2], refs[-2:]
    width = w_ref.shape[1]

    def fetch(j):
        source = pl.ds(pl.multiple_of(first + j * tile, tile), tile)
        target = pl.ds(pl.multiple_of(j * tile, tile), tile)
        return pltpu.make_async_copy(w_hbm.at[:, source], w_ref.at[:, target], sems.at[j])

    for j in range(width // tile):
        fetch(j).start()

    def step(j, carry):
        cols = pl.ds(pl.multiple_of(j * tile, tile), tile)
        fetch(j).wait()
        out = jnp.dot(rows_ref[...], w_ref[:, cols], preferred_element_type=F32).astype(BF16)
        start = 0
        for ref in outs:
            ref[:, cols] = out[start : start + ref.shape[0]]
            start += ref.shape[0]
        return carry

    lax.fori_loop(0, width // tile, step, 0)


def down(rows, sizes, w_down, first, width):
    hidden = w_down.shape[0]
    tile = min(512, width)
    vmem = pl.BlockSpec(memory_space=pltpu.VMEM)
    return pl.pallas_call(
        functools.partial(down_kernel, first, tile),
        out_shape=tuple(jax.ShapeDtypeStruct((n, width), BF16) for n in sizes),
        in_specs=[vmem, pl.BlockSpec(memory_space=pl.ANY)],
        out_specs=(vmem,) * len(sizes),
        scratch_shapes=[pltpu.VMEM((hidden, width), BF16), pltpu.SemaphoreType.DMA((width // tile,))],
        compiler_params=pltpu.CompilerParams(vmem_limit_bytes=52 * MIB),
        cost_estimate=cost(
            2 * rows.shape[0] * hidden * width, 2 * hidden * width + 2 * rows.shape[0] * (hidden + width)
        ),
        name="down",
    )(rows, w_down)


def add_up(*parts):
    return sum(p.astype(F32) for p in parts)


def along_line(block, distance):
    size = lax.axis_size("expert")
    return lax.ppermute(block, "expert", [(e, (e + 2 * distance) % size) for e in range(size)])


def cross(block, turn):
    owners, dps = lax.axis_size("expert"), lax.axis_size("dp")
    route = []
    for e in range(owners):
        for core in range(2):
            for d in range(dps):
                to = (e ^ 1, core, d) if core == turn else (e, core, d ^ 1)
                route.append(((e * 2 + core) * dps + d, (to[0] * 2 + core) * dps + to[2]))
    return lax.ppermute(block, ("expert", "context", "dp"), route)


def after(blocks, *others):
    return lax.optimization_barrier((blocks, others))[0]


def send_rows(packed, line):
    size = packed.shape[0] // line
    parts = [packed[size * s : size * (s + 1)] for s in range(line)]
    return [parts[0]] + [along_line(parts[s], s) for s in range(1, line)]


def send_home(result, line):
    size = result.shape[0] // line
    parts = [result[size * s : size * (s + 1)] for s in range(line)]
    came = [parts[0]] + [along_line(parts[s], -s) for s in range(1, line)]
    return jnp.concatenate(came, axis=0)


def plain_experts(packed, line, w_gate, w_up, w_down):
    own = jnp.concatenate(send_rows(packed, line), axis=0)
    rows = jnp.concatenate([own, swap_pair(own)], axis=0)
    rows = lax.all_gather(rows, ("context", "dp"), axis=0, tiled=True)
    hidden = gate_up([rows], w_gate, w_up)
    out = down(hidden, (rows.shape[0],), w_down, 0, w_down.shape[1])[0]
    mine = lax.psum_scatter(out, ("context", "dp"), scatter_dimension=0, tiled=True)
    count = own.shape[0]
    return send_home(add_up(mine[:count], swap_pair(mine[count:])).astype(BF16), line)


def square_experts(early, late, line, w_gate, w_up, w_down):
    width = w_down.shape[1]
    half = width // 2

    def pieces(two, four):
        return [two, four, shift(two, "context", 1), shift(four, "context", 1)]

    def home_first(outs):
        rows = outs[0].shape[0] // 4
        both = add_up(outs[0], shift(outs[1], "context", 1))
        return both[: 2 * rows], both[2 * rows :].astype(BF16)

    def home_second(kept, far):
        rows = kept.shape[0] // 2
        two = add_up(kept, far)
        return two[:rows], two[rows:].astype(BF16)

    early_came = send_rows(early, line)
    late_came = send_rows(after(late, early_came[1]), line)
    early_own = jnp.concatenate(early_came, axis=0)
    early_near = cross(early_own, 0)
    early_two = jnp.concatenate([early_own, early_near], axis=0)
    early_four = cross(early_two, 1)
    late_came[0] = after(late_came[0], early_near)
    late_own = jnp.concatenate(late_came, axis=0)
    late_near = cross(late_own, 0)
    sizes = (4 * early_own.shape[0],) * 2
    early_hidden = gate_up(after(pieces(early_two, early_four), late_own), w_gate, w_up)

    late_two = jnp.concatenate([after(late_own, early_hidden), late_near], axis=0)
    late_four = cross(late_two, 1)
    early_out = down(after(early_hidden, late_two), sizes, w_down, 0, width)
    late_four = after(late_four, early_out)
    early_kept, early_go = home_first(after(early_out, late_four))
    early_far = cross(early_go, 1)
    sizes = (4 * late_own.shape[0],) * 2
    late_hidden = gate_up(after(pieces(late_two, late_four), early_go), w_gate, w_up)

    early_kept, early_go = home_second(after(early_kept, late_hidden), early_far)
    early_far = cross(early_go, 0)
    out_left = down(after(late_hidden, early_go), sizes, w_down, 0, half)
    early_result = add_up(after(early_kept, out_left), early_far).astype(BF16)
    early_back = send_home(early_result, line)
    left = home_first(out_left)
    left_far = cross(left[1], 1)
    out_right = down(after(late_hidden, early_result, left[1]), sizes, w_down, half, half)
    left = home_second(after(left[0], out_right), left_far)
    left_far = cross(left[1], 0)
    right = home_first(out_right)
    right_far = cross(right[1], 1)
    right = home_second(after(right[0], left[1]), right_far)
    right_far = cross(right[1], 0)
    late_back = []
    for kept, far in ((left[0], left_far), (right[0], right_far)):
        late_back.append(send_home(add_up(kept, far).astype(BF16), line))
    return early_back, jnp.concatenate(late_back, axis=1)


def on_device(
    residual,
    x_raw,
    z_gate,
    conv_w,
    conv_b,
    xproj_w,
    dtproj_w,
    dt_bias,
    a_rate,
    skip_gain,
    out_w,
    norm_gain,
    route_ids,
    route_w,
    w_gate,
    w_up,
    w_down,
):
    owners, contexts, dps = (lax.axis_size(a) for a in ("expert", "context", "dp"))
    me = lax.axis_index("expert")
    place, half = me // 2, me % 2
    line = owners // 2
    length, channels = x_raw.shape[2:]
    width = residual.shape[3]
    row_count = residual.shape[2]

    values = x_raw[0, 0]
    prior_rim = from_behind(values[length - (CONV - 1) :], "context", 1)
    padded = jnp.concatenate([prior_rim, values], axis=0).astype(F32)
    conv_sum = conv_b[None, :] + sum(
        (
            conv_w[lag_index][None, :] * padded[lag_index : lag_index + length]
            for lag_index in range(CONV)
        )
    )
    mixed_in = jax.nn.silu(conv_sum).astype(BF16)
    projected = jnp.dot(mixed_in, xproj_w, preferred_element_type=F32).astype(BF16)
    shares = projected.reshape(line, length // line, -1)

    def share_of(s):
        return lax.dynamic_index_in_dim(shares, (place + s) % line, 0, keepdims=False)

    share = add_up(share_of(0), *[along_line(share_of(s), s) for s in range(1, line)]).astype(BF16)
    share = add_up(share, swap_pair(share)).astype(BF16)
    pieces = [share] + [along_line(share, s) for s in range(1, line)]

    neg = -a_rate.reshape(NSTATE, channels // LANES, LANES)
    neg = jnp.pad(neg, ((0, 0), (0, SUB - channels // LANES), (0, 0)))
    where = jnp.stack([place, half]).astype(jnp.int32)
    y, total, end, bc = run_scan(where, pieces, dtproj_w, dt_bias[None, :], neg, mixed_in)
    enter = from_behind(end, "context", 1)
    for step in range(contexts - 2):
        decay = jnp.exp(total[-SUB:][None] * neg)
        enter = from_behind(end + decay * enter, "context", 1)
    parts = 4
    part = width // parts
    cut = run_out(
        where, line, parts, y, total, enter, bc, neg, mixed_in, z_gate[0, 0], skip_gain[None, :], out_w
    )
    kept, sent = cut[:parts], cut[parts:]
    sums, got = [], swap_pair(sent[0])
    for k in range(parts):
        both = add_up(kept[k], got).astype(BF16).reshape(line, row_count, part)
        if k + 1 < parts:
            got = swap_pair(after(sent[k + 1], got))
        sums.append(add_up(both[0], *[along_line(both[s], s) for s in range(1, line)]))
    mixer_out = jnp.concatenate(sums, axis=1)

    stream_f = (residual[0, 0].astype(F32) + mixer_out).astype(BF16).astype(F32)
    normed = (
        stream_f
        * lax.rsqrt(jnp.mean(stream_f * stream_f, axis=1, keepdims=True) + 1e-05)
        * norm_gain[None, :]
    ).astype(BF16)
    ids, weights = route_ids[0, 0], route_w[0, 0]
    capacity = min(row_count, 8 * ((3 * row_count * TOP + 16 * line - 1) // (16 * line)))
    cuts = (0, 8, capacity) if contexts == 2 and dps == 2 and capacity > 8 else (0, capacity)
    named = jnp.any(ids[:, :, None] == jnp.arange(line, dtype=jnp.int32), axis=1)
    rank = jnp.cumsum(named.astype(jnp.int32), axis=0) - 1
    chosen = ids[:, :, None] == jnp.arange(line, dtype=jnp.int32)
    rank_of = jnp.sum(jnp.where(chosen, rank[:, None, :], 0), axis=2)
    away = (ids - place + line) % line
    placing, weighting, packed = [], [], []
    for low, high in zip(cuts[:-1], cuts[1:]):
        inside = (rank_of >= low) & (rank_of < high)
        slot_of = jnp.where(inside, away * (high - low) + rank_of - low, -1)
        hits = slot_of[:, :, None] == jnp.arange(line * (high - low), dtype=jnp.int32)
        placing = jnp.any(hits, axis=1).astype(BF16)
        weighting.append(jnp.sum(jnp.where(hits, weights[:, :, None], 0.0), axis=1))
        rows = lax.dot_general(
            placing, normed, (((0,), (0,)), ((), ())), preferred_element_type=F32
        )
        packed.append(rows.astype(BF16))
    if len(packed) == 2:
        back = square_experts(*packed, line, w_gate[0], w_up[0], w_down[0])
    else:
        back = [plain_experts(packed[0], line, w_gate[0], w_up[0], w_down[0])]
    expert_sum = jnp.dot(
        jnp.concatenate(weighting, axis=1),
        jnp.concatenate(back, axis=0).astype(F32),
        precision=lax.Precision.HIGHEST,
        preferred_element_type=F32,
    )
    mixed = (stream_f + expert_sum).astype(BF16)
    return mixed.reshape(1, 1, row_count, width)


def solution(mesh):
    placed = (
        P("dp", "context", "expert", None),
        P("dp", "context", None, "expert"),
        P("dp", "context", None, "expert"),
        P(None, "expert"),
        P("expert"),
        P("expert", None),
        P(None, "expert"),
        P("expert"),
        P(None, "expert"),
        P("expert"),
        P("expert", None),
        P(),
        P("dp", "context", "expert", None),
        P("dp", "context", "expert", None),
        P("expert", None, ("context", "dp")),
        P("expert", None, ("context", "dp")),
        P("expert", ("context", "dp"), None),
    )
    return jax.shard_map(
        on_device,
        mesh=mesh,
        in_specs=placed,
        out_specs=P("dp", "context", "expert", None),
        check_vma=False,
    )
```

```python
import functools

import jax
import jax.numpy as jnp
from jax import lax
from jax.experimental import pallas as pl
from jax.experimental.pallas import tpu as pltpu
from jax.sharding import PartitionSpec as P

NSTATE = 16
DT_RANK = 256
CONV = 4
TOP = 2
LANES = 128
SUB = 8
F32 = jnp.float32
BF16 = jnp.bfloat16
MIB = 1 << 20


def from_behind(block, axis, distance):
    devices = range(lax.axis_size(axis))
    route = [(i - distance, i) for i in devices if i - distance in devices]
    return lax.ppermute(block, axis, route)


def shift(block, axis, distance):
    size = lax.axis_size(axis)
    return lax.ppermute(block, axis, [(i, (i + distance) % size) for i in range(size)])


def swap_pair(block):
    size = lax.axis_size("expert")
    return lax.ppermute(block, "expert", [(i, i ^ 1) for i in range(size)])


def cost(flops, bytes_accessed, transcendentals=0):
    return pl.CostEstimate(
        flops=int(flops), bytes_accessed=int(bytes_accessed), transcendentals=int(transcendentals)
    )


def spread_rows(values, wide_ref):
    length, count = values.shape
    col = lax.broadcasted_iota(jnp.int32, (count, count * LANES), 1)
    row = lax.broadcasted_iota(jnp.int32, (count, count * LANES), 0)
    ones = jnp.where((col >= row * LANES) & (col < (row + 1) * LANES), 1.0, 0.0).astype(BF16)
    out = jnp.dot(values, ones, preferred_element_type=F32)
    for n in range(count):
        wide_ref[pl.ds(n * length, length), :] = out[:, n * LANES : (n + 1) * LANES]


def scan_kernel(groups, line, place_ref, *refs):
    pieces, refs = refs[:line], refs[line:]
    w_ref, bias_ref, neg_ref, x_ref, y_ref, sum_ref, end_ref, bc_ref = refs[:8]
    low_ref, step_ref, drive_ref, wide_ref = refs[8:]
    length = x_ref.shape[0]
    share = length // line
    for s in range(line):
        start = pl.multiple_of((place_ref[0] + (line - s)) % line * share, share)
        low_ref[pl.ds(start, share), :] = pieces[s][:, :DT_RANK]
        bc_ref[pl.ds(start, share), :] = pieces[s][:, DT_RANK:]
    spread_rows(bc_ref[...], wide_ref)
    for g in range(SUB):
        rows = pl.ds(g, length, stride=SUB)
        if g >= groups:
            step_ref[rows, :] = jnp.zeros((length, LANES), F32)
            drive_ref[rows, :] = jnp.zeros((length, LANES), F32)
            continue
        cols = pl.ds(g * LANES, LANES)
        raw = jnp.dot(low_ref[...], w_ref[:, cols], preferred_element_type=F32) + bias_ref[:, cols]
        step = jnp.maximum(raw, 0.0) + jnp.log1p(jnp.exp(-jnp.abs(raw)))
        step_ref[rows, :] = step
        drive_ref[rows, :] = step * x_ref[:, cols].astype(F32)

    def block(k, carry):
        states, total = list(carry[0]), carry[1]
        for u in range(SUB):
            t = k * SUB + u
            here = pl.ds(pl.multiple_of(t * SUB, SUB), SUB)
            step, drive = step_ref[here, :], drive_ref[here, :]
            total = total + step
            out = jnp.zeros((SUB, LANES), F32)
            for n in range(NSTATE):
                decay = jnp.exp(step * neg_ref[n])
                b = wide_ref[pl.ds(n * length + t, 1), :]
                c = wide_ref[pl.ds((NSTATE + n) * length + t, 1), :]
                states[n] = states[n] * decay + drive * b
                out = out + states[n] * c
            y_ref[here, :] = out
            sum_ref[here, :] = total
        return tuple(states), total

    zero = jnp.zeros((SUB, LANES), F32)
    states, total = lax.fori_loop(0, length // SUB, block, ((zero,) * NSTATE, zero))
    for n in range(NSTATE):
        end_ref[n] = states[n]


def run_scan(place, pieces, w, bias, neg, x):
    length, channels = x.shape
    vmem = pl.BlockSpec(memory_space=pltpu.VMEM)
    tall = jax.ShapeDtypeStruct((length * SUB, LANES), F32)
    return pl.pallas_call(
        functools.partial(scan_kernel, channels // LANES, len(pieces)),
        out_shape=(
            tall,
            tall,
            jax.ShapeDtypeStruct((NSTATE, SUB, LANES), F32),
            jax.ShapeDtypeStruct((length, 2 * NSTATE), BF16),
        ),
        in_specs=[pl.BlockSpec(memory_space=pltpu.SMEM)] + [vmem] * (len(pieces) + 4),
        out_specs=(vmem,) * 4,
        scratch_shapes=[
            pltpu.VMEM((length, DT_RANK), BF16),
            pltpu.VMEM((length * SUB, LANES), F32),
            pltpu.VMEM((length * SUB, LANES), F32),
            pltpu.VMEM((2 * NSTATE * length, LANES), F32),
        ],
        compiler_params=pltpu.CompilerParams(vmem_limit_bytes=20 * MIB),
        cost_estimate=cost(2e8, 4 * MIB, NSTATE * length * channels),
        name="state_scan",
    )(place, *pieces, w, bias, neg, x)


def out_kernel(groups, line, parts, at_ref, y_ref, sum_ref, enter_ref, bc_ref, neg_ref, x_ref, z_ref,
               skip_ref, w_hbm, *refs):
    kept_refs, sent_refs = refs[:parts], refs[parts : 2 * parts]
    full_ref, wide_ref, gated_ref, order_ref, w_ref, sems = refs[2 * parts :]
    length = x_ref.shape[0]
    tiles, _, tile = w_ref.shape

    def fetch(j):
        cols = pl.ds(pl.multiple_of(j * tile, tile), tile)
        return pltpu.make_async_copy(w_hbm.at[:, cols], w_ref.at[j], sems.at[j])

    for j in range(tiles):
        fetch(j).start()
    spread_rows(bc_ref[:, NSTATE:], wide_ref)

    def block(k, carry):
        for u in range(SUB):
            t = k * SUB + u
            here = pl.ds(pl.multiple_of(t * SUB, SUB), SUB)
            total = sum_ref[here, :]
            out = y_ref[here, :]
            for n in range(NSTATE):
                c = wide_ref[pl.ds(n * length + t, 1), :]
                out = out + jnp.exp(total * neg_ref[n]) * enter_ref[n] * c
            full_ref[here, :] = out
        return carry

    lax.fori_loop(0, length // SUB, block, 0)
    for g in range(groups):
        cols = pl.ds(g * LANES, LANES)
        mixed_in = x_ref[:, cols].astype(F32)
        read = full_ref[pl.ds(g, length, stride=SUB), :] + skip_ref[:, cols] * mixed_in
        z = z_ref[:, cols].astype(F32)
        gated_ref[:, cols] = (read * (z / (1.0 + jnp.exp(-z)))).astype(BF16)
    place, half = at_ref[0], at_ref[1]
    count = length // 2
    piece = count // line
    for k in range(line):
        for r in range(2):
            source = pl.multiple_of((2 * ((place + k) % line) + (half ^ r)) * piece, piece)
            order_ref[pl.ds(r * count + k * piece, piece), :] = gated_ref[pl.ds(source, piece), :]
    for j in range(parts):

        def step(i, carry):
            at = j * (tiles // parts) + i
            fetch(at).wait()
            cols = pl.ds(pl.multiple_of(i * tile, tile), tile)
            out = jnp.dot(order_ref[...], w_ref[at], preferred_element_type=F32).astype(BF16)
            kept_refs[j][:, cols] = out[:count]
            sent_refs[j][:, cols] = out[count:]
            return carry

        lax.fori_loop(0, tiles // parts, step, 0)


def run_out(at, line, parts, y, total, enter, bc, neg, x, z, skip, w):
    length, channels = x.shape
    wide = w.shape[1]
    tile = min(256, wide // parts)
    vmem = pl.BlockSpec(memory_space=pltpu.VMEM)
    return pl.pallas_call(
        functools.partial(out_kernel, channels // LANES, line, parts),
        out_shape=(jax.ShapeDtypeStruct((length // 2, wide // parts), BF16),) * (2 * parts),
        in_specs=[pl.BlockSpec(memory_space=pltpu.SMEM)] + [vmem] * 8 + [pl.BlockSpec(memory_space=pl.ANY)],
        out_specs=(vmem,) * (2 * parts),
        scratch_shapes=[
            pltpu.VMEM((length * SUB, LANES), F32),
            pltpu.VMEM((NSTATE * length, LANES), F32),
            pltpu.VMEM((length, channels), BF16),
            pltpu.VMEM((length, channels), BF16),
            pltpu.VMEM((wide // tile, channels, tile), BF16),
            pltpu.SemaphoreType.DMA((wide // tile,)),
        ],
        compiler_params=pltpu.CompilerParams(vmem_limit_bytes=48 * MIB),
        cost_estimate=cost(
            2 * length * channels * wide, 2 * channels * wide + 8 * MIB, NSTATE * length * channels
        ),
        name="readout_project",
    )(at, y, total, enter, bc, neg, x, z, skip, w)


def gate_up_kernel(count, first, *refs):
    pieces, (gate_hbm, up_hbm, out_ref, rows_ref, gate_ref, up_ref, sems) = refs[:count], refs[count:]
    copies, at = [], 0
    for k, piece in enumerate(pieces):
        rows = pl.ds(at, piece.shape[0])
        copies.append(pltpu.make_async_copy(piece, rows_ref.at[rows, :], sems.at[k]))
        at += piece.shape[0]
    steps, tile = gate_ref.shape[0], gate_ref.shape[2]

    def fetch(j, k):
        cols = pl.ds(pl.multiple_of(first + j * tile, tile), tile)
        source, target = ((gate_hbm, gate_ref), (up_hbm, up_ref))[k]
        return pltpu.make_async_copy(source.at[:, cols], target.at[j], sems.at[count + 2 * j + k])

    for copy in copies:
        copy.start()
    for j in range(steps):
        fetch(j, 0).start()
        fetch(j, 1).start()
    for copy in copies:
        copy.wait()

    def step(j, carry):
        fetch(j, 0).wait()
        gate = jnp.dot(rows_ref[...], gate_ref[j], preferred_element_type=F32)
        fetch(j, 1).wait()
        up = jnp.dot(rows_ref[...], up_ref[j], preferred_element_type=F32)
        cols = pl.ds(pl.multiple_of(j * tile, tile), tile)
        out_ref[:, cols] = (gate / (1.0 + jnp.exp(-gate)) * up).astype(BF16)
        return carry

    lax.fori_loop(0, steps, step, 0)


def gate_up(pieces, w_gate, w_up, first, width):
    depth = w_gate.shape[0]
    rows = sum(p.shape[0] for p in pieces)
    tile = min(256, width)
    steps = width // tile
    anywhere = pl.BlockSpec(memory_space=pl.ANY)
    return pl.pallas_call(
        functools.partial(gate_up_kernel, len(pieces), first),
        out_shape=jax.ShapeDtypeStruct((rows, width), BF16),
        in_specs=[anywhere] * (len(pieces) + 2),
        out_specs=pl.BlockSpec(memory_space=pltpu.VMEM),
        scratch_shapes=[
            pltpu.VMEM((rows, depth), BF16),
            pltpu.VMEM((steps, depth, tile), BF16),
            pltpu.VMEM((steps, depth, tile), BF16),
            pltpu.SemaphoreType.DMA((len(pieces) + 2 * steps,)),
        ],
        compiler_params=pltpu.CompilerParams(vmem_limit_bytes=49 * MIB),
        cost_estimate=cost(4 * rows * depth * width, 4 * depth * width + 2 * rows * depth),
        name="gate_up",
    )(*pieces, w_gate, w_up)


def down_kernel(count, first, *refs):
    pieces, w_hbm, outs = refs[:count], refs[count], refs[count + 1 : -3]
    rows_ref, w_ref, sems = refs[-3:]
    tiles, _, tile = w_ref.shape

    def fetch(j):
        source = pl.ds(pl.multiple_of(first + j * tile, tile), tile)
        return pltpu.make_async_copy(w_hbm.at[:, source], w_ref.at[j], sems.at[j])

    for j in range(tiles):
        fetch(j).start()
    at = 0
    for piece in pieces:
        rows_ref[:, pl.ds(at, piece.shape[1])] = piece[...]
        at += piece.shape[1]

    def step(j, carry):
        fetch(j).wait()
        out = jnp.dot(rows_ref[...], w_ref[j], preferred_element_type=F32).astype(BF16)
        cols = pl.ds(pl.multiple_of(j * tile, tile), tile)
        start = 0
        for ref in outs:
            ref[:, cols] = out[start : start + ref.shape[0]]
            start += ref.shape[0]
        return carry

    lax.fori_loop(0, tiles, step, 0)


def down(pieces, sizes, w_down, first, width):
    hidden, rows = w_down.shape[0], pieces[0].shape[0]
    tile = min(256, width)
    vmem = pl.BlockSpec(memory_space=pltpu.VMEM)
    return pl.pallas_call(
        functools.partial(down_kernel, len(pieces), first),
        out_shape=tuple(jax.ShapeDtypeStruct((n, width), BF16) for n in sizes),
        in_specs=[vmem] * len(pieces) + [pl.BlockSpec(memory_space=pl.ANY)],
        out_specs=(vmem,) * len(sizes),
        scratch_shapes=[
            pltpu.VMEM((rows, hidden), BF16),
            pltpu.VMEM((width // tile, hidden, tile), BF16),
            pltpu.SemaphoreType.DMA((width // tile,)),
        ],
        compiler_params=pltpu.CompilerParams(vmem_limit_bytes=49 * MIB),
        cost_estimate=cost(2 * rows * hidden * width, 2 * hidden * width + 2 * rows * (hidden + width)),
        name="down",
    )(*pieces, w_down)


def add_up(*parts):
    return sum(p.astype(F32) for p in parts)


def along_line(block, distance):
    size = lax.axis_size("expert")
    return lax.ppermute(block, "expert", [(e, (e + 2 * distance) % size) for e in range(size)])


def cross(block, turn):
    owners, dps = lax.axis_size("expert"), lax.axis_size("dp")
    route = []
    for e in range(owners):
        for core in range(2):
            for d in range(dps):
                to = (e ^ 1, core, d) if core == turn else (e, core, d ^ 1)
                route.append(((e * 2 + core) * dps + d, (to[0] * 2 + core) * dps + to[2]))
    return lax.ppermute(block, ("expert", "context", "dp"), route)


def after(blocks, *others):
    return lax.optimization_barrier((blocks, others))[0]


def send_rows(packed, line):
    size = packed.shape[0] // line
    parts = [packed[size * s : size * (s + 1)] for s in range(line)]
    return [parts[0]] + [along_line(parts[s], s) for s in range(1, line)]


def send_home(result, line):
    size = result.shape[0] // line
    parts = [result[size * s : size * (s + 1)] for s in range(line)]
    came = [parts[0]] + [along_line(parts[s], -s) for s in range(1, line)]
    return jnp.concatenate(came, axis=0)


def plain_experts(packed, line, w_gate, w_up, w_down):
    own = jnp.concatenate(send_rows(packed, line), axis=0)
    rows = jnp.concatenate([own, swap_pair(own)], axis=0)
    rows = lax.all_gather(rows, ("context", "dp"), axis=0, tiled=True)
    hidden = gate_up([rows], w_gate, w_up, 0, w_gate.shape[1])
    out = down([hidden], (rows.shape[0],), w_down, 0, w_down.shape[1])[0]
    mine = lax.psum_scatter(out, ("context", "dp"), scatter_dimension=0, tiled=True)
    count = own.shape[0]
    return send_home(add_up(mine[:count], swap_pair(mine[count:])).astype(BF16), line)


def square_experts(early, late, line, w_gate, w_up, w_down):
    width = w_down.shape[1]
    half = width // 2
    hidden = w_down.shape[0]
    most = hidden * 2 // 3

    def pieces(two, four):
        return [two, four, shift(two, "context", 1), shift(four, "context", 1)]

    def home_first(outs):
        rows = outs[0].shape[0] // 4
        both = add_up(outs[0], shift(outs[1], "context", 1))
        return both[: 2 * rows], both[2 * rows :].astype(BF16)

    def home_second(kept, far):
        rows = kept.shape[0] // 2
        two = add_up(kept, far)
        return two[:rows], two[rows:].astype(BF16)

    early_came = send_rows(early, line)
    late_came = send_rows(after(late, early_came[1]), line)
    early_own = jnp.concatenate(early_came, axis=0)
    early_near = cross(early_own, 0)
    early_two = jnp.concatenate([early_own, early_near], axis=0)
    early_four = cross(early_two, 1)
    late_came[0] = after(late_came[0], early_near)
    late_own = jnp.concatenate(late_came, axis=0)
    late_near = cross(late_own, 0)
    sizes = (4 * early_own.shape[0],) * 2
    early_rows = after(pieces(early_two, early_four), late_own)
    early_first = gate_up(early_rows, w_gate, w_up, 0, most)

    late_two = jnp.concatenate([after(late_own, early_first), late_near], axis=0)
    late_four = cross(late_two, 1)
    early_second = gate_up(after(early_rows, late_two), w_gate, w_up, most, hidden - most)
    early_out = down([early_first, early_second], sizes, w_down, 0, width)
    late_four = after(late_four, early_out)
    early_kept, early_go = home_first(after(early_out, late_four))
    early_far = cross(early_go, 1)
    sizes = (4 * late_own.shape[0],) * 2
    late_rows = after(pieces(late_two, late_four), early_go)
    late_first = gate_up(late_rows, w_gate, w_up, 0, hidden // 2)
    early_kept, early_go = home_second(after(early_kept, late_first), early_far)
    early_far = cross(early_go, 0)
    late_second = gate_up(after(late_rows, early_go), w_gate, w_up, hidden // 2, hidden // 2)
    early_result = add_up(after(early_kept, late_second), early_far).astype(BF16)
    early_back = send_home(early_result, line)
    late_hidden = [late_first, late_second]
    out_left = down(after(late_hidden, early_result), sizes, w_down, 0, half)
    left = home_first(out_left)
    left_far = cross(left[1], 1)
    late_hidden, early_back = lax.optimization_barrier((late_hidden, early_back))
    out_right = down(after(late_hidden, left[1]), sizes, w_down, half, half)
    left = home_second(after(left[0], out_right), left_far)
    left_far = cross(left[1], 0)
    right = home_first(out_right)
    right_far = cross(right[1], 1)
    right = home_second(after(right[0], left[1]), right_far)
    right_far = cross(right[1], 0)
    late_back = []
    for kept, far in ((left[0], left_far), (right[0], right_far)):
        late_back.append(send_home(add_up(kept, far).astype(BF16), line))
    return early_back, jnp.concatenate(late_back, axis=1)


def on_device(
    residual,
    x_raw,
    z_gate,
    conv_w,
    conv_b,
    xproj_w,
    dtproj_w,
    dt_bias,
    a_rate,
    skip_gain,
    out_w,
    norm_gain,
    route_ids,
    route_w,
    w_gate,
    w_up,
    w_down,
):
    owners, contexts, dps = (lax.axis_size(a) for a in ("expert", "context", "dp"))
    me = lax.axis_index("expert")
    place, half = me // 2, me % 2
    line = owners // 2
    length, channels = x_raw.shape[2:]
    width = residual.shape[3]
    row_count = residual.shape[2]

    values = x_raw[0, 0]
    prior_rim = from_behind(values[length - (CONV - 1) :], "context", 1)
    padded = jnp.concatenate([prior_rim, values], axis=0).astype(F32)
    conv_sum = conv_b[None, :] + sum(
        (
            conv_w[lag_index][None, :] * padded[lag_index : lag_index + length]
            for lag_index in range(CONV)
        )
    )
    mixed_in = jax.nn.silu(conv_sum).astype(BF16)
    projected = jnp.dot(mixed_in, xproj_w, preferred_element_type=F32).astype(BF16)
    shares = projected.reshape(line, length // line, -1)

    def share_of(s):
        return lax.dynamic_index_in_dim(shares, (place + s) % line, 0, keepdims=False)

    share = add_up(share_of(0), *[along_line(share_of(s), s) for s in range(1, line)]).astype(BF16)
    share = add_up(share, swap_pair(share)).astype(BF16)
    pieces = [share] + [along_line(share, s) for s in range(1, line)]

    neg = -a_rate.reshape(NSTATE, channels // LANES, LANES)
    neg = jnp.pad(neg, ((0, 0), (0, SUB - channels // LANES), (0, 0)))
    where = jnp.stack([place, half]).astype(jnp.int32)
    y, total, end, bc = run_scan(where, pieces, dtproj_w, dt_bias[None, :], neg, mixed_in)
    enter = from_behind(end, "context", 1)
    for step in range(contexts - 2):
        decay = jnp.exp(total[-SUB:][None] * neg)
        enter = from_behind(end + decay * enter, "context", 1)
    parts = 4
    part = width // parts
    cut = run_out(
        where, line, parts, y, total, enter, bc, neg, mixed_in, z_gate[0, 0], skip_gain[None, :], out_w
    )
    kept, sent = cut[:parts], cut[parts:]
    sums, got = [], swap_pair(sent[0])
    for k in range(parts):
        both = add_up(kept[k], got).astype(BF16).reshape(line, row_count, part)
        if k + 1 < parts:
            got = swap_pair(after(sent[k + 1], got))
        sums.append(add_up(both[0], *[along_line(both[s], s) for s in range(1, line)]))
    mixer_out = jnp.concatenate(sums, axis=1)

    stream_f = (residual[0, 0].astype(F32) + mixer_out).astype(BF16).astype(F32)
    normed = (
        stream_f
        * lax.rsqrt(jnp.mean(stream_f * stream_f, axis=1, keepdims=True) + 1e-05)
        * norm_gain[None, :]
    ).astype(BF16)
    ids, weights = route_ids[0, 0], route_w[0, 0]
    capacity = min(row_count, 8 * ((3 * row_count * TOP + 16 * line - 1) // (16 * line)))
    cuts = (0, 8, capacity) if contexts == 2 and dps == 2 and capacity > 8 else (0, capacity)
    named = jnp.any(ids[:, :, None] == jnp.arange(line, dtype=jnp.int32), axis=1)
    rank = jnp.cumsum(named.astype(jnp.int32), axis=0) - 1
    chosen = ids[:, :, None] == jnp.arange(line, dtype=jnp.int32)
    rank_of = jnp.sum(jnp.where(chosen, rank[:, None, :], 0), axis=2)
    away = (ids - place + line) % line
    placing, weighting, packed = [], [], []
    for low, high in zip(cuts[:-1], cuts[1:]):
        inside = (rank_of >= low) & (rank_of < high)
        slot_of = jnp.where(inside, away * (high - low) + rank_of - low, -1)
        hits = slot_of[:, :, None] == jnp.arange(line * (high - low), dtype=jnp.int32)
        placing = jnp.any(hits, axis=1).astype(BF16)
        weighting.append(jnp.sum(jnp.where(hits, weights[:, :, None], 0.0), axis=1))
        rows = lax.dot_general(
            placing, normed, (((0,), (0,)), ((), ())), preferred_element_type=F32
        )
        packed.append(rows.astype(BF16))
    if len(packed) == 2:
        back = square_experts(*packed, line, w_gate[0], w_up[0], w_down[0])
    else:
        back = [plain_experts(packed[0], line, w_gate[0], w_up[0], w_down[0])]
    expert_sum = jnp.dot(
        jnp.concatenate(weighting, axis=1),
        jnp.concatenate(back, axis=0).astype(F32),
        precision=lax.Precision.HIGHEST,
        preferred_element_type=F32,
    )
    mixed = (stream_f + expert_sum).astype(BF16)
    return mixed.reshape(1, 1, row_count, width)


def solution(mesh):
    placed = (
        P("dp", "context", "expert", None),
        P("dp", "context", None, "expert"),
        P("dp", "context", None, "expert"),
        P(None, "expert"),
        P("expert"),
        P("expert", None),
        P(None, "expert"),
        P("expert"),
        P(None, "expert"),
        P("expert"),
        P("expert", None),
        P(),
        P("dp", "context", "expert", None),
        P("dp", "context", "expert", None),
        P("expert", None, ("context", "dp")),
        P("expert", None, ("context", "dp")),
        P("expert", ("context", "dp"), None),
    )
    return jax.shard_map(
        on_device,
        mesh=mesh,
        in_specs=placed,
        out_specs=P("dp", "context", "expert", None),
        check_vma=False,
    )
```

```python
import functools

import jax
import jax.numpy as jnp
from jax import lax
from jax.experimental import pallas as pl
from jax.experimental.pallas import tpu as pltpu
from jax.sharding import PartitionSpec as P

NSTATE = 16
DT_RANK = 256
CONV = 4
TOP = 2
LANES = 128
SUB = 8
F32 = jnp.float32
BF16 = jnp.bfloat16
MIB = 1 << 20


def from_behind(block, axis, distance):
    devices = range(lax.axis_size(axis))
    route = [(i - distance, i) for i in devices if i - distance in devices]
    return lax.ppermute(block, axis, route)


def shift(block, axis, distance):
    size = lax.axis_size(axis)
    return lax.ppermute(block, axis, [(i, (i + distance) % size) for i in range(size)])


def swap_pair(block):
    size = lax.axis_size("expert")
    return lax.ppermute(block, "expert", [(i, i ^ 1) for i in range(size)])


def cost(flops, bytes_accessed, transcendentals=0):
    return pl.CostEstimate(
        flops=int(flops), bytes_accessed=int(bytes_accessed), transcendentals=int(transcendentals)
    )


def spread_rows(values, wide_ref):
    length, count = values.shape
    col = lax.broadcasted_iota(jnp.int32, (count, count * LANES), 1)
    row = lax.broadcasted_iota(jnp.int32, (count, count * LANES), 0)
    ones = jnp.where((col >= row * LANES) & (col < (row + 1) * LANES), 1.0, 0.0).astype(BF16)
    out = jnp.dot(values, ones, preferred_element_type=F32)
    for n in range(count):
        wide_ref[pl.ds(n * length, length), :] = out[:, n * LANES : (n + 1) * LANES]


def scan_kernel(groups, line, place_ref, *refs):
    pieces, refs = refs[:line], refs[line:]
    w_ref, bias_ref, neg_ref, x_ref, y_ref, sum_ref, end_ref, bc_ref = refs[:8]
    low_ref, step_ref, drive_ref, wide_ref = refs[8:]
    length = x_ref.shape[0]
    share = length // line
    for s in range(line):
        start = pl.multiple_of((place_ref[0] + (line - s)) % line * share, share)
        low_ref[pl.ds(start, share), :] = pieces[s][:, :DT_RANK]
        bc_ref[pl.ds(start, share), :] = pieces[s][:, DT_RANK:]
    spread_rows(bc_ref[...], wide_ref)
    for g in range(SUB):
        rows = pl.ds(g, length, stride=SUB)
        if g >= groups:
            step_ref[rows, :] = jnp.zeros((length, LANES), F32)
            drive_ref[rows, :] = jnp.zeros((length, LANES), F32)
            continue
        cols = pl.ds(g * LANES, LANES)
        raw = jnp.dot(low_ref[...], w_ref[:, cols], preferred_element_type=F32) + bias_ref[:, cols]
        step = jnp.maximum(raw, 0.0) + jnp.log1p(jnp.exp(-jnp.abs(raw)))
        step_ref[rows, :] = step
        drive_ref[rows, :] = step * x_ref[:, cols].astype(F32)

    def block(k, carry):
        states, total = list(carry[0]), carry[1]
        for u in range(SUB):
            t = k * SUB + u
            here = pl.ds(pl.multiple_of(t * SUB, SUB), SUB)
            step, drive = step_ref[here, :], drive_ref[here, :]
            total = total + step
            out = jnp.zeros((SUB, LANES), F32)
            for n in range(NSTATE):
                decay = jnp.exp(step * neg_ref[n])
                b = wide_ref[pl.ds(n * length + t, 1), :]
                c = wide_ref[pl.ds((NSTATE + n) * length + t, 1), :]
                states[n] = states[n] * decay + drive * b
                out = out + states[n] * c
            y_ref[here, :] = out
            sum_ref[here, :] = total
        return tuple(states), total

    zero = jnp.zeros((SUB, LANES), F32)
    states, total = lax.fori_loop(0, length // SUB, block, ((zero,) * NSTATE, zero))
    for n in range(NSTATE):
        end_ref[n] = states[n]


def run_scan(place, pieces, w, bias, neg, x):
    length, channels = x.shape
    vmem = pl.BlockSpec(memory_space=pltpu.VMEM)
    tall = jax.ShapeDtypeStruct((length * SUB, LANES), F32)
    return pl.pallas_call(
        functools.partial(scan_kernel, channels // LANES, len(pieces)),
        out_shape=(
            tall,
            tall,
            jax.ShapeDtypeStruct((NSTATE, SUB, LANES), F32),
            jax.ShapeDtypeStruct((length, 2 * NSTATE), BF16),
        ),
        in_specs=[pl.BlockSpec(memory_space=pltpu.SMEM)] + [vmem] * (len(pieces) + 4),
        out_specs=(vmem,) * 4,
        scratch_shapes=[
            pltpu.VMEM((length, DT_RANK), BF16),
            pltpu.VMEM((length * SUB, LANES), F32),
            pltpu.VMEM((length * SUB, LANES), F32),
            pltpu.VMEM((2 * NSTATE * length, LANES), F32),
        ],
        compiler_params=pltpu.CompilerParams(vmem_limit_bytes=20 * MIB),
        cost_estimate=cost(2e8, 4 * MIB, NSTATE * length * channels),
        name="state_scan",
    )(place, *pieces, w, bias, neg, x)


def out_kernel(groups, line, first, at_ref, y_ref, sum_ref, enter_ref, bc_ref, neg_ref, x_ref, z_ref,
               skip_ref, w_hbm, *refs):
    kept_ref, sent_ref, blocks_ref, full_ref, wide_ref, gated_ref, order_ref, w_ref, sems = refs
    length = x_ref.shape[0]
    tiles, _, tile = w_ref.shape

    def fetch(j):
        cols = pl.ds(pl.multiple_of(j * tile, tile), tile)
        return pltpu.make_async_copy(w_hbm.at[:, cols], w_ref.at[j], sems.at[j])

    for j in range(tiles):
        fetch(j).start()
    spread_rows(bc_ref[:, NSTATE:], wide_ref)

    def block(k, carry):
        for u in range(SUB):
            t = k * SUB + u
            here = pl.ds(pl.multiple_of(t * SUB, SUB), SUB)
            total = sum_ref[here, :]
            out = y_ref[here, :]
            for n in range(NSTATE):
                c = wide_ref[pl.ds(n * length + t, 1), :]
                out = out + jnp.exp(total * neg_ref[n]) * enter_ref[n] * c
            full_ref[here, :] = out
        return carry

    lax.fori_loop(0, length // SUB, block, 0)
    for g in range(groups):
        cols = pl.ds(g * LANES, LANES)
        mixed_in = x_ref[:, cols].astype(F32)
        read = full_ref[pl.ds(g, length, stride=SUB), :] + skip_ref[:, cols] * mixed_in
        z = z_ref[:, cols].astype(F32)
        gated_ref[:, cols] = (read * (z / (1.0 + jnp.exp(-z)))).astype(BF16)
    place, half = at_ref[0], at_ref[1]
    count = length // 2
    piece = count // line
    for k in range(line):
        for r in range(2):
            source = pl.multiple_of((2 * ((place + k) % line) + (half ^ r)) * piece, piece)
            order_ref[pl.ds(r * count + k * piece, piece), :] = gated_ref[pl.ds(source, piece), :]
    def project(j):
        fetch(j).wait()
        return jnp.dot(order_ref[...], w_ref[j], preferred_element_type=F32).astype(BF16)

    def step(j, carry):
        cols = pl.ds(pl.multiple_of(j * tile, tile), tile)
        out = project(j)
        kept_ref[:, cols] = out[:count]
        sent_ref[:, cols] = out[count:]
        return carry

    def block_step(j, carry):
        cols = pl.ds(pl.multiple_of((j - first) * tile, tile), tile)
        out = project(j)
        for k in range(line):
            for r in range(2):
                start = r * count + k * piece
                blocks_ref[k, pl.ds(r * piece, piece), cols] = out[start : start + piece]
        return carry

    lax.fori_loop(0, first, step, 0)
    lax.fori_loop(first, tiles, block_step, 0)


def run_out(at, line, y, total, enter, bc, neg, x, z, skip, w):
    length, channels = x.shape
    wide = w.shape[1]
    tile = min(512, wide)
    first = (wide // tile * 5 + 4) // 8
    vmem = pl.BlockSpec(memory_space=pltpu.VMEM)
    part = jax.ShapeDtypeStruct((length // 2, first * tile), BF16)
    blocks = jax.ShapeDtypeStruct((line, length // line, wide - first * tile), BF16)
    return pl.pallas_call(
        functools.partial(out_kernel, channels // LANES, line, first),
        out_shape=(part, part, blocks),
        in_specs=[pl.BlockSpec(memory_space=pltpu.SMEM)] + [vmem] * 8 + [pl.BlockSpec(memory_space=pl.ANY)],
        out_specs=(vmem,) * 3,
        scratch_shapes=[
            pltpu.VMEM((length * SUB, LANES), F32),
            pltpu.VMEM((NSTATE * length, LANES), F32),
            pltpu.VMEM((length, channels), BF16),
            pltpu.VMEM((length, channels), BF16),
            pltpu.VMEM((wide // tile, channels, tile), BF16),
            pltpu.SemaphoreType.DMA((wide // tile,)),
        ],
        compiler_params=pltpu.CompilerParams(vmem_limit_bytes=48 * MIB),
        cost_estimate=cost(
            2 * length * channels * wide, 2 * channels * wide + 8 * MIB, NSTATE * length * channels
        ),
        name="readout_project",
    )(at, y, total, enter, bc, neg, x, z, skip, w)


def gate_up_kernel(count, first, *refs):
    pieces, (gate_hbm, up_hbm, out_ref, rows_ref, gate_ref, up_ref, sems) = refs[:count], refs[count:]
    copies, at = [], 0
    for k, piece in enumerate(pieces):
        rows = pl.ds(at, piece.shape[0])
        copies.append(pltpu.make_async_copy(piece, rows_ref.at[rows, :], sems.at[k]))
        at += piece.shape[0]
    steps, tile = gate_ref.shape[0], gate_ref.shape[2]

    def fetch(j, k):
        cols = pl.ds(pl.multiple_of(first + j * tile, tile), tile)
        source, target = ((gate_hbm, gate_ref), (up_hbm, up_ref))[k]
        return pltpu.make_async_copy(source.at[:, cols], target.at[j], sems.at[count + 2 * j + k])

    for copy in copies:
        copy.start()
    for j in range(steps):
        fetch(j, 0).start()
        fetch(j, 1).start()
    for copy in copies:
        copy.wait()

    def step(j, carry):
        fetch(j, 0).wait()
        fetch(j, 1).wait()
        gate = jnp.dot(rows_ref[...], gate_ref[j], preferred_element_type=F32)
        up = jnp.dot(rows_ref[...], up_ref[j], preferred_element_type=F32)
        cols = pl.ds(pl.multiple_of(j * tile, tile), tile)
        out_ref[:, cols] = (gate / (1.0 + jnp.exp(-gate)) * up).astype(BF16)
        return carry

    lax.fori_loop(0, steps, step, 0)


def gate_up(pieces, w_gate, w_up, first, width):
    depth = w_gate.shape[0]
    rows = sum(p.shape[0] for p in pieces)
    tile = min(256, width)
    steps = width // tile
    anywhere = pl.BlockSpec(memory_space=pl.ANY)
    return pl.pallas_call(
        functools.partial(gate_up_kernel, len(pieces), first),
        out_shape=jax.ShapeDtypeStruct((rows, width), BF16),
        in_specs=[anywhere] * (len(pieces) + 2),
        out_specs=pl.BlockSpec(memory_space=pltpu.VMEM),
        scratch_shapes=[
            pltpu.VMEM((rows, depth), BF16),
            pltpu.VMEM((steps, depth, tile), BF16),
            pltpu.VMEM((steps, depth, tile), BF16),
            pltpu.SemaphoreType.DMA((len(pieces) + 2 * steps,)),
        ],
        compiler_params=pltpu.CompilerParams(vmem_limit_bytes=49 * MIB),
        cost_estimate=cost(4 * rows * depth * width, 4 * depth * width + 2 * rows * depth),
        name="gate_up",
    )(*pieces, w_gate, w_up)


def down_kernel(count, first, *refs):
    pieces, w_hbm, outs = refs[:count], refs[count], refs[count + 1 : -3]
    rows_ref, w_ref, sems = refs[-3:]
    tiles, _, tile = w_ref.shape

    def fetch(j):
        source = pl.ds(pl.multiple_of(first + j * tile, tile), tile)
        return pltpu.make_async_copy(w_hbm.at[:, source], w_ref.at[j], sems.at[j])

    for j in range(tiles):
        fetch(j).start()
    at = 0
    for piece in pieces:
        rows_ref[:, pl.ds(at, piece.shape[1])] = piece[...]
        at += piece.shape[1]

    def step(j, carry):
        fetch(j).wait()
        out = jnp.dot(rows_ref[...], w_ref[j], preferred_element_type=F32).astype(BF16)
        cols = pl.ds(pl.multiple_of(j * tile, tile), tile)
        start = 0
        for ref in outs:
            ref[:, cols] = out[start : start + ref.shape[0]]
            start += ref.shape[0]
        return carry

    lax.fori_loop(0, tiles, step, 0)


def down(pieces, sizes, w_down, first, width):
    hidden, rows = w_down.shape[0], pieces[0].shape[0]
    tile = min(512, width)
    vmem = pl.BlockSpec(memory_space=pltpu.VMEM)
    return pl.pallas_call(
        functools.partial(down_kernel, len(pieces), first),
        out_shape=tuple(jax.ShapeDtypeStruct((n, width), BF16) for n in sizes),
        in_specs=[vmem] * len(pieces) + [pl.BlockSpec(memory_space=pl.ANY)],
        out_specs=(vmem,) * len(sizes),
        scratch_shapes=[
            pltpu.VMEM((rows, hidden), BF16),
            pltpu.VMEM((width // tile, hidden, tile), BF16),
            pltpu.SemaphoreType.DMA((width // tile,)),
        ],
        compiler_params=pltpu.CompilerParams(vmem_limit_bytes=49 * MIB),
        cost_estimate=cost(2 * rows * hidden * width, 2 * hidden * width + 2 * rows * (hidden + width)),
        name="down",
    )(*pieces, w_down)


def add_up(*parts):
    return sum(p.astype(F32) for p in parts)


def along_line(block, distance):
    size = lax.axis_size("expert")
    return lax.ppermute(block, "expert", [(e, (e + 2 * distance) % size) for e in range(size)])


def cross(block, turn):
    owners, dps = lax.axis_size("expert"), lax.axis_size("dp")
    route = []
    for e in range(owners):
        for core in range(2):
            for d in range(dps):
                to = (e ^ 1, core, d) if core == turn else (e, core, d ^ 1)
                route.append(((e * 2 + core) * dps + d, (to[0] * 2 + core) * dps + to[2]))
    return lax.ppermute(block, ("expert", "context", "dp"), route)


def after(blocks, *others):
    return lax.optimization_barrier((blocks, others))[0]


def send_rows(packed, line):
    size = packed.shape[0] // line
    parts = [packed[size * s : size * (s + 1)] for s in range(line)]
    return [parts[0]] + [along_line(parts[s], s) for s in range(1, line)]


def send_home(result, line):
    size = result.shape[0] // line
    parts = [result[size * s : size * (s + 1)] for s in range(line)]
    came = [parts[0]] + [along_line(parts[s], -s) for s in range(1, line)]
    return jnp.concatenate(came, axis=0)


def plain_experts(packed, line, w_gate, w_up, w_down):
    own = jnp.concatenate(send_rows(packed, line), axis=0)
    rows = jnp.concatenate([own, swap_pair(own)], axis=0)
    rows = lax.all_gather(rows, ("context", "dp"), axis=0, tiled=True)
    hidden = gate_up([rows], w_gate, w_up, 0, w_gate.shape[1])
    out = down([hidden], (rows.shape[0],), w_down, 0, w_down.shape[1])[0]
    mine = lax.psum_scatter(out, ("context", "dp"), scatter_dimension=0, tiled=True)
    count = own.shape[0]
    return send_home(add_up(mine[:count], swap_pair(mine[count:])).astype(BF16), line)


def square_experts(early, late, line, w_gate, w_up, w_down):
    width = w_down.shape[1]
    half = width // 2
    hidden = w_down.shape[0]
    most = hidden * 2 // 3

    def pieces(two, four):
        return [two, four, shift(two, "context", 1), shift(four, "context", 1)]

    def home_first(outs):
        rows = outs[0].shape[0] // 4
        both = add_up(outs[0], shift(outs[1], "context", 1))
        return both[: 2 * rows], both[2 * rows :].astype(BF16)

    def home_second(kept, far):
        rows = kept.shape[0] // 2
        two = add_up(kept, far)
        return two[:rows], two[rows:].astype(BF16)

    early_came = send_rows(early, line)
    late_came = send_rows(after(late, early_came[1]), line)
    early_own = jnp.concatenate(early_came, axis=0)
    early_near = cross(early_own, 0)
    early_two = jnp.concatenate([early_own, early_near], axis=0)
    early_four = cross(early_two, 1)
    late_came[0] = after(late_came[0], early_near)
    late_own = jnp.concatenate(late_came, axis=0)
    late_near = cross(late_own, 0)
    sizes = (4 * early_own.shape[0],) * 2
    early_rows = after(pieces(early_two, early_four), late_own)
    early_first = gate_up(early_rows, w_gate, w_up, 0, most)

    late_two = jnp.concatenate([after(late_own, early_first), late_near], axis=0)
    late_four = cross(late_two, 1)
    early_second = gate_up(after(early_rows, late_two), w_gate, w_up, most, hidden - most)
    early_out = down([early_first, early_second], sizes, w_down, 0, width)
    late_four = after(late_four, early_out)
    early_kept, early_go = home_first(after(early_out, late_four))
    early_far = cross(early_go, 1)
    sizes = (4 * late_own.shape[0],) * 2
    late_rows = after(pieces(late_two, late_four), early_go)
    late_first = gate_up(late_rows, w_gate, w_up, 0, hidden // 2)
    early_kept, early_go = home_second(after(early_kept, late_first), early_far)
    early_far = cross(early_go, 0)
    late_second = gate_up(after(late_rows, early_go), w_gate, w_up, hidden // 2, hidden // 2)
    early_result = add_up(after(early_kept, late_second), early_far).astype(BF16)
    late_hidden = [late_first, late_second]
    out_left = down(after(late_hidden, early_result), sizes, w_down, 0, half)
    left = home_first(out_left)
    left_far = cross(left[1], 1)
    out_right = down(after(late_hidden, early_result, left[1]), sizes, w_down, half, half)
    left = home_second(after(left[0], out_right), left_far)
    left_far = cross(left[1], 0)
    right = home_first(out_right)
    early_back = send_home(after(early_result, right[1]), line)
    right_far = cross(right[1], 1)
    right = home_second(after(right[0], left[1]), right_far)
    right_far = cross(right[1], 0)
    late_back = []
    for kept, far in ((left[0], left_far), (right[0], right_far)):
        late_back.append(send_home(add_up(kept, far).astype(BF16), line))
    return early_back, jnp.concatenate(late_back, axis=1)


def on_device(
    residual,
    x_raw,
    z_gate,
    conv_w,
    conv_b,
    xproj_w,
    dtproj_w,
    dt_bias,
    a_rate,
    skip_gain,
    out_w,
    norm_gain,
    route_ids,
    route_w,
    w_gate,
    w_up,
    w_down,
):
    owners, contexts, dps = (lax.axis_size(a) for a in ("expert", "context", "dp"))
    me = lax.axis_index("expert")
    place, half = me // 2, me % 2
    line = owners // 2
    length, channels = x_raw.shape[2:]
    width = residual.shape[3]
    row_count = residual.shape[2]

    values = x_raw[0, 0]
    prior_rim = from_behind(values[length - (CONV - 1) :], "context", 1)
    padded = jnp.concatenate([prior_rim, values], axis=0).astype(F32)
    conv_sum = conv_b[None, :] + sum(
        (
            conv_w[lag_index][None, :] * padded[lag_index : lag_index + length]
            for lag_index in range(CONV)
        )
    )
    mixed_in = jax.nn.silu(conv_sum).astype(BF16)
    projected = jnp.dot(mixed_in, xproj_w, preferred_element_type=F32).astype(BF16)
    shares = projected.reshape(line, length // line, -1)

    def share_of(s):
        return lax.dynamic_index_in_dim(shares, (place + s) % line, 0, keepdims=False)

    share = add_up(share_of(0), *[along_line(share_of(s), s) for s in range(1, line)]).astype(BF16)
    share = add_up(share, swap_pair(share)).astype(BF16)
    pieces = [share] + [along_line(share, s) for s in range(1, line)]

    neg = -a_rate.reshape(NSTATE, channels // LANES, LANES)
    neg = jnp.pad(neg, ((0, 0), (0, SUB - channels // LANES), (0, 0)))
    where = jnp.stack([place, half]).astype(jnp.int32)
    y, total, end, bc = run_scan(where, pieces, dtproj_w, dt_bias[None, :], neg, mixed_in)
    enter = from_behind(end, "context", 1)
    for step in range(contexts - 2):
        decay = jnp.exp(total[-SUB:][None] * neg)
        enter = from_behind(end + decay * enter, "context", 1)
    kept, sent, blocks = run_out(
        where, line, y, total, enter, bc, neg, mixed_in, z_gate[0, 0], skip_gain[None, :], out_w
    )
    got = swap_pair(sent)
    over_z = add_up(blocks[0], *[along_line(blocks[s], s) for s in range(1, line)])
    both = add_up(kept, got).astype(BF16).reshape(line, row_count, -1)
    other = swap_pair(over_z[row_count:].astype(BF16))
    sums = [
        add_up(both[0], *[along_line(both[s], s) for s in range(1, line)]),
        add_up(over_z[:row_count], other),
    ]
    mixer_out = jnp.concatenate(sums, axis=1)

    stream_f = (residual[0, 0].astype(F32) + mixer_out).astype(BF16).astype(F32)
    normed = (
        stream_f
        * lax.rsqrt(jnp.mean(stream_f * stream_f, axis=1, keepdims=True) + 1e-05)
        * norm_gain[None, :]
    ).astype(BF16)
    ids, weights = route_ids[0, 0], route_w[0, 0]
    capacity = min(row_count, 8 * ((3 * row_count * TOP + 16 * line - 1) // (16 * line)))
    cuts = (0, 8, capacity) if contexts == 2 and dps == 2 and capacity > 8 else (0, capacity)
    named = jnp.any(ids[:, :, None] == jnp.arange(line, dtype=jnp.int32), axis=1)
    rank = jnp.cumsum(named.astype(jnp.int32), axis=0) - 1
    chosen = ids[:, :, None] == jnp.arange(line, dtype=jnp.int32)
    rank_of = jnp.sum(jnp.where(chosen, rank[:, None, :], 0), axis=2)
    away = (ids - place + line) % line
    placing, weighting, packed = [], [], []
    for low, high in zip(cuts[:-1], cuts[1:]):
        inside = (rank_of >= low) & (rank_of < high)
        slot_of = jnp.where(inside, away * (high - low) + rank_of - low, -1)
        hits = slot_of[:, :, None] == jnp.arange(line * (high - low), dtype=jnp.int32)
        placing = jnp.any(hits, axis=1).astype(BF16)
        weighting.append(jnp.sum(jnp.where(hits, weights[:, :, None], 0.0), axis=1))
        rows = lax.dot_general(
            placing, normed, (((0,), (0,)), ((), ())), preferred_element_type=F32
        )
        packed.append(rows.astype(BF16))
    if len(packed) == 2:
        back = square_experts(*packed, line, w_gate[0], w_up[0], w_down[0])
    else:
        back = [plain_experts(packed[0], line, w_gate[0], w_up[0], w_down[0])]
    expert_sum = jnp.dot(
        jnp.concatenate(weighting, axis=1),
        jnp.concatenate(back, axis=0).astype(F32),
        precision=lax.Precision.HIGHEST,
        preferred_element_type=F32,
    )
    mixed = (stream_f + expert_sum).astype(BF16)
    return mixed.reshape(1, 1, row_count, width)


def solution(mesh):
    placed = (
        P("dp", "context", "expert", None),
        P("dp", "context", None, "expert"),
        P("dp", "context", None, "expert"),
        P(None, "expert"),
        P("expert"),
        P("expert", None),
        P(None, "expert"),
        P("expert"),
        P(None, "expert"),
        P("expert"),
        P("expert", None),
        P(),
        P("dp", "context", "expert", None),
        P("dp", "context", "expert", None),
        P("expert", None, ("context", "dp")),
        P("expert", None, ("context", "dp")),
        P("expert", ("context", "dp"), None),
    )
    return jax.shard_map(
        on_device,
        mesh=mesh,
        in_specs=placed,
        out_specs=P("dp", "context", "expert", None),
        check_vma=False,
    )
```

```python
import functools

import jax
import jax.numpy as jnp
from jax import lax
from jax.experimental import pallas as pl
from jax.experimental.pallas import tpu as pltpu
from jax.sharding import PartitionSpec as P

NSTATE = 16
DT_RANK = 256
CONV = 4
TOP = 2
LANES = 128
SUB = 8
F32 = jnp.float32
BF16 = jnp.bfloat16
MIB = 1 << 20


def from_behind(block, axis, distance):
    devices = range(lax.axis_size(axis))
    route = [(i - distance, i) for i in devices if i - distance in devices]
    return lax.ppermute(block, axis, route)


def shift(block, axis, distance):
    size = lax.axis_size(axis)
    return lax.ppermute(block, axis, [(i, (i + distance) % size) for i in range(size)])


def swap_pair(block):
    size = lax.axis_size("expert")
    return lax.ppermute(block, "expert", [(i, i ^ 1) for i in range(size)])


def cost(flops, bytes_accessed, transcendentals=0):
    return pl.CostEstimate(
        flops=int(flops), bytes_accessed=int(bytes_accessed), transcendentals=int(transcendentals)
    )


def spread_rows(values, wide_ref):
    length, count = values.shape
    col = lax.broadcasted_iota(jnp.int32, (count, count * LANES), 1)
    row = lax.broadcasted_iota(jnp.int32, (count, count * LANES), 0)
    ones = jnp.where((col >= row * LANES) & (col < (row + 1) * LANES), 1.0, 0.0).astype(BF16)
    out = jnp.dot(values, ones, preferred_element_type=F32)
    for n in range(count):
        wide_ref[pl.ds(n * length, length), :] = out[:, n * LANES : (n + 1) * LANES]


def scan_kernel(groups, line, place_ref, *refs):
    pieces, refs = refs[:line], refs[line:]
    w_ref, bias_ref, neg_ref, x_ref, y_ref, sum_ref, end_ref, bc_ref = refs[:8]
    low_ref, step_ref, drive_ref, wide_ref = refs[8:]
    length = x_ref.shape[0]
    share = length // line
    for s in range(line):
        start = pl.multiple_of((place_ref[0] + (line - s)) % line * share, share)
        low_ref[pl.ds(start, share), :] = pieces[s][:, :DT_RANK]
        bc_ref[pl.ds(start, share), :] = pieces[s][:, DT_RANK:]
    spread_rows(bc_ref[...], wide_ref)
    for g in range(SUB):
        rows = pl.ds(g, length, stride=SUB)
        if g >= groups:
            step_ref[rows, :] = jnp.zeros((length, LANES), F32)
            drive_ref[rows, :] = jnp.zeros((length, LANES), F32)
            continue
        cols = pl.ds(g * LANES, LANES)
        raw = jnp.dot(low_ref[...], w_ref[:, cols], preferred_element_type=F32) + bias_ref[:, cols]
        step = jnp.maximum(raw, 0.0) + jnp.log1p(jnp.exp(-jnp.abs(raw)))
        step_ref[rows, :] = step
        drive_ref[rows, :] = step * x_ref[:, cols].astype(F32)

    def block(k, carry):
        states, total = list(carry[0]), carry[1]
        for u in range(SUB):
            t = k * SUB + u
            here = pl.ds(pl.multiple_of(t * SUB, SUB), SUB)
            step, drive = step_ref[here, :], drive_ref[here, :]
            total = total + step
            out = jnp.zeros((SUB, LANES), F32)
            for n in range(NSTATE):
                decay = jnp.exp(step * neg_ref[n])
                b = wide_ref[pl.ds(n * length + t, 1), :]
                c = wide_ref[pl.ds((NSTATE + n) * length + t, 1), :]
                states[n] = states[n] * decay + drive * b
                out = out + states[n] * c
            y_ref[here, :] = out
            sum_ref[here, :] = total
        return tuple(states), total

    zero = jnp.zeros((SUB, LANES), F32)
    states, total = lax.fori_loop(0, length // SUB, block, ((zero,) * NSTATE, zero))
    for n in range(NSTATE):
        end_ref[n] = states[n]


def run_scan(place, pieces, w, bias, neg, x):
    length, channels = x.shape
    vmem = pl.BlockSpec(memory_space=pltpu.VMEM)
    tall = jax.ShapeDtypeStruct((length * SUB, LANES), F32)
    return pl.pallas_call(
        functools.partial(scan_kernel, channels // LANES, len(pieces)),
        out_shape=(
            tall,
            tall,
            jax.ShapeDtypeStruct((NSTATE, SUB, LANES), F32),
            jax.ShapeDtypeStruct((length, 2 * NSTATE), BF16),
        ),
        in_specs=[pl.BlockSpec(memory_space=pltpu.SMEM)] + [vmem] * (len(pieces) + 4),
        out_specs=(vmem,) * 4,
        scratch_shapes=[
            pltpu.VMEM((length, DT_RANK), BF16),
            pltpu.VMEM((length * SUB, LANES), F32),
            pltpu.VMEM((length * SUB, LANES), F32),
            pltpu.VMEM((2 * NSTATE * length, LANES), F32),
        ],
        compiler_params=pltpu.CompilerParams(vmem_limit_bytes=20 * MIB),
        cost_estimate=cost(2e8, 4 * MIB, NSTATE * length * channels),
        name="state_scan",
    )(place, *pieces, w, bias, neg, x)


def out_kernel(groups, line, first, at_ref, y_ref, sum_ref, enter_ref, bc_ref, neg_ref, x_ref, z_ref,
               skip_ref, w_hbm, *refs):
    kept_ref, sent_ref, blocks_ref, full_ref, wide_ref, gated_ref, order_ref, w_ref, sems = refs
    length = x_ref.shape[0]
    tiles, _, tile = w_ref.shape

    def fetch(j):
        cols = pl.ds(pl.multiple_of(j * tile, tile), tile)
        return pltpu.make_async_copy(w_hbm.at[:, cols], w_ref.at[j], sems.at[j])

    for j in range(tiles):
        fetch(j).start()
    spread_rows(bc_ref[:, NSTATE:], wide_ref)

    def block(k, carry):
        for u in range(SUB):
            t = k * SUB + u
            here = pl.ds(pl.multiple_of(t * SUB, SUB), SUB)
            total = sum_ref[here, :]
            out = y_ref[here, :]
            for n in range(NSTATE):
                c = wide_ref[pl.ds(n * length + t, 1), :]
                out = out + jnp.exp(total * neg_ref[n]) * enter_ref[n] * c
            full_ref[here, :] = out
        return carry

    lax.fori_loop(0, length // SUB, block, 0)
    for g in range(groups):
        cols = pl.ds(g * LANES, LANES)
        mixed_in = x_ref[:, cols].astype(F32)
        read = full_ref[pl.ds(g, length, stride=SUB), :] + skip_ref[:, cols] * mixed_in
        z = z_ref[:, cols].astype(F32)
        gated_ref[:, cols] = (read * (z / (1.0 + jnp.exp(-z)))).astype(BF16)
    place, half = at_ref[0], at_ref[1]
    count = length // 2
    piece = count // line
    for k in range(line):
        for r in range(2):
            source = pl.multiple_of((2 * ((place + k) % line) + (half ^ r)) * piece, piece)
            order_ref[pl.ds(r * count + k * piece, piece), :] = gated_ref[pl.ds(source, piece), :]
    def project(j):
        fetch(j).wait()
        return jnp.dot(order_ref[...], w_ref[j], preferred_element_type=F32).astype(BF16)

    def step(j, carry):
        cols = pl.ds(pl.multiple_of(j * tile, tile), tile)
        out = project(j)
        kept_ref[:, cols] = out[:count]
        sent_ref[:, cols] = out[count:]
        return carry

    def block_step(j, carry):
        cols = pl.ds(pl.multiple_of((j - first) * tile, tile), tile)
        out = project(j)
        for k in range(line):
            for r in range(2):
                start = r * count + k * piece
                blocks_ref[k, pl.ds(r * piece, piece), cols] = out[start : start + piece]
        return carry

    lax.fori_loop(0, first, step, 0)
    lax.fori_loop(first, tiles, block_step, 0)


def run_out(at, line, y, total, enter, bc, neg, x, z, skip, w):
    length, channels = x.shape
    wide = w.shape[1]
    tile = min(512, wide)
    first = (wide // tile * 5 + 4) // 8
    vmem = pl.BlockSpec(memory_space=pltpu.VMEM)
    part = jax.ShapeDtypeStruct((length // 2, first * tile), BF16)
    blocks = jax.ShapeDtypeStruct((line, length // line, wide - first * tile), BF16)
    return pl.pallas_call(
        functools.partial(out_kernel, channels // LANES, line, first),
        out_shape=(part, part, blocks),
        in_specs=[pl.BlockSpec(memory_space=pltpu.SMEM)] + [vmem] * 8 + [pl.BlockSpec(memory_space=pl.ANY)],
        out_specs=(vmem,) * 3,
        scratch_shapes=[
            pltpu.VMEM((length * SUB, LANES), F32),
            pltpu.VMEM((NSTATE * length, LANES), F32),
            pltpu.VMEM((length, channels), BF16),
            pltpu.VMEM((length, channels), BF16),
            pltpu.VMEM((wide // tile, channels, tile), BF16),
            pltpu.SemaphoreType.DMA((wide // tile,)),
        ],
        compiler_params=pltpu.CompilerParams(vmem_limit_bytes=48 * MIB),
        cost_estimate=cost(
            2 * length * channels * wide, 2 * channels * wide + 8 * MIB, NSTATE * length * channels
        ),
        name="readout_project",
    )(at, y, total, enter, bc, neg, x, z, skip, w)


def gate_up_kernel(count, first, *refs):
    pieces, (gate_hbm, up_hbm, out_ref, rows_ref, gate_ref, up_ref, sems) = refs[:count], refs[count:]
    copies, at = [], 0
    for k, piece in enumerate(pieces):
        rows = pl.ds(at, piece.shape[0])
        copies.append(pltpu.make_async_copy(piece, rows_ref.at[rows, :], sems.at[k]))
        at += piece.shape[0]
    steps, tile = gate_ref.shape[0], gate_ref.shape[2]

    def fetch(j, k):
        cols = pl.ds(pl.multiple_of(first + j * tile, tile), tile)
        source, target = ((gate_hbm, gate_ref), (up_hbm, up_ref))[k]
        return pltpu.make_async_copy(source.at[:, cols], target.at[j], sems.at[count + 2 * j + k])

    for copy in copies:
        copy.start()
    for j in range(steps):
        fetch(j, 0).start()
        fetch(j, 1).start()
    for copy in copies:
        copy.wait()

    def step(j, carry):
        fetch(j, 0).wait()
        fetch(j, 1).wait()
        gate = jnp.dot(rows_ref[...], gate_ref[j], preferred_element_type=F32)
        up = jnp.dot(rows_ref[...], up_ref[j], preferred_element_type=F32)
        cols = pl.ds(pl.multiple_of(j * tile, tile), tile)
        out_ref[:, cols] = (gate / (1.0 + jnp.exp(-gate)) * up).astype(BF16)
        return carry

    lax.fori_loop(0, steps, step, 0)


def gate_up(pieces, w_gate, w_up, first, width):
    depth = w_gate.shape[0]
    rows = sum(p.shape[0] for p in pieces)
    tile = min(256, width)
    steps = width // tile
    anywhere = pl.BlockSpec(memory_space=pl.ANY)
    return pl.pallas_call(
        functools.partial(gate_up_kernel, len(pieces), first),
        out_shape=jax.ShapeDtypeStruct((rows, width), BF16),
        in_specs=[anywhere] * (len(pieces) + 2),
        out_specs=pl.BlockSpec(memory_space=pltpu.VMEM),
        scratch_shapes=[
            pltpu.VMEM((rows, depth), BF16),
            pltpu.VMEM((steps, depth, tile), BF16),
            pltpu.VMEM((steps, depth, tile), BF16),
            pltpu.SemaphoreType.DMA((len(pieces) + 2 * steps,)),
        ],
        compiler_params=pltpu.CompilerParams(vmem_limit_bytes=49 * MIB),
        cost_estimate=cost(4 * rows * depth * width, 4 * depth * width + 2 * rows * depth),
        name="gate_up",
    )(*pieces, w_gate, w_up)


def down_kernel(count, first, *refs):
    pieces, w_hbm, outs = refs[:count], refs[count], refs[count + 1 : -3]
    rows_ref, w_ref, sems = refs[-3:]
    tiles, _, tile = w_ref.shape

    def fetch(j):
        source = pl.ds(pl.multiple_of(first + j * tile, tile), tile)
        return pltpu.make_async_copy(w_hbm.at[:, source], w_ref.at[j], sems.at[j])

    for j in range(tiles):
        fetch(j).start()
    at = 0
    for piece in pieces:
        rows_ref[:, pl.ds(at, piece.shape[1])] = piece[...]
        at += piece.shape[1]

    def step(j, carry):
        fetch(j).wait()
        out = jnp.dot(rows_ref[...], w_ref[j], preferred_element_type=F32).astype(BF16)
        cols = pl.ds(pl.multiple_of(j * tile, tile), tile)
        start = 0
        for ref in outs:
            ref[:, cols] = out[start : start + ref.shape[0]]
            start += ref.shape[0]
        return carry

    lax.fori_loop(0, tiles, step, 0)


def down(pieces, sizes, w_down, first, width):
    hidden, rows = w_down.shape[0], pieces[0].shape[0]
    tile = min(512, width)
    vmem = pl.BlockSpec(memory_space=pltpu.VMEM)
    return pl.pallas_call(
        functools.partial(down_kernel, len(pieces), first),
        out_shape=tuple(jax.ShapeDtypeStruct((n, width), BF16) for n in sizes),
        in_specs=[vmem] * len(pieces) + [pl.BlockSpec(memory_space=pl.ANY)],
        out_specs=(vmem,) * len(sizes),
        scratch_shapes=[
            pltpu.VMEM((rows, hidden), BF16),
            pltpu.VMEM((width // tile, hidden, tile), BF16),
            pltpu.SemaphoreType.DMA((width // tile,)),
        ],
        compiler_params=pltpu.CompilerParams(vmem_limit_bytes=49 * MIB),
        cost_estimate=cost(2 * rows * hidden * width, 2 * hidden * width + 2 * rows * (hidden + width)),
        name="down",
    )(*pieces, w_down)


def add_up(*parts):
    return sum(p.astype(F32) for p in parts)


def along_line(block, distance):
    size = lax.axis_size("expert")
    return lax.ppermute(block, "expert", [(e, (e + 2 * distance) % size) for e in range(size)])


def cross(block, turn):
    owners, dps = lax.axis_size("expert"), lax.axis_size("dp")
    route = []
    for e in range(owners):
        for core in range(2):
            for d in range(dps):
                to = (e ^ 1, core, d) if core == turn else (e, core, d ^ 1)
                route.append(((e * 2 + core) * dps + d, (to[0] * 2 + core) * dps + to[2]))
    return lax.ppermute(block, ("expert", "context", "dp"), route)


def after(blocks, *others):
    return lax.optimization_barrier((blocks, others))[0]


def send_rows(packed, line):
    size = packed.shape[0] // line
    parts = [packed[size * s : size * (s + 1)] for s in range(line)]
    return [parts[0]] + [along_line(parts[s], s) for s in range(1, line)]


def send_home(result, line):
    size = result.shape[0] // line
    parts = [result[size * s : size * (s + 1)] for s in range(line)]
    came = [parts[0]] + [along_line(parts[s], -s) for s in range(1, line)]
    return jnp.concatenate(came, axis=0)


def plain_experts(packed, line, w_gate, w_up, w_down):
    own = jnp.concatenate(send_rows(packed, line), axis=0)
    rows = jnp.concatenate([own, swap_pair(own)], axis=0)
    rows = lax.all_gather(rows, ("context", "dp"), axis=0, tiled=True)
    hidden = gate_up([rows], w_gate, w_up, 0, w_gate.shape[1])
    out = down([hidden], (rows.shape[0],), w_down, 0, w_down.shape[1])[0]
    mine = lax.psum_scatter(out, ("context", "dp"), scatter_dimension=0, tiled=True)
    count = own.shape[0]
    return send_home(add_up(mine[:count], swap_pair(mine[count:])).astype(BF16), line)


def square_experts(early, late, line, w_gate, w_up, w_down):
    width = w_down.shape[1]
    half = width // 2
    hidden = w_down.shape[0]
    most = hidden // 2

    def pieces(two, four):
        return [two, four, shift(two, "context", 1), shift(four, "context", 1)]

    def part(terms, start, stop):
        return add_up(*[t[start:stop] for t in terms]).astype(BF16)

    def home_first(outs, *others):
        terms = [after(outs[0], *others), shift(outs[1], "context", 1)]
        rows = outs[0].shape[0]
        return terms, part(terms, rows // 2, rows)

    def home_second(terms, far):
        terms = terms + [far]
        rows = far.shape[0]
        return terms, part(terms, rows // 2, rows)

    def home_third(terms, far):
        return part(terms + [far], 0, far.shape[0])

    early_came = send_rows(early, line)
    early_own = jnp.concatenate(early_came, axis=0)
    late_came = send_rows(after(late, early_own), line)
    early_near = cross(early_own, 0)
    early_two = jnp.concatenate([early_own, early_near], axis=0)
    early_four = cross(early_two, 1)
    late_came[0] = after(late_came[0], early_near)
    late_own = jnp.concatenate(late_came, axis=0)
    late_near = cross(late_own, 0)
    sizes = (4 * early_own.shape[0],) * 2
    early_rows = after(pieces(early_two, early_four), late_own)
    early_first = gate_up(early_rows, w_gate, w_up, 0, most)

    late_two = jnp.concatenate([after(late_own, early_first), late_near], axis=0)
    late_four = cross(late_two, 1)
    early_second = gate_up(after(early_rows, late_two), w_gate, w_up, most, hidden - most)
    early_out = down([early_first, early_second], sizes, w_down, 0, width)
    late_four = after(late_four, early_out)
    early_kept, early_go = home_first(early_out, late_four)
    early_far = cross(early_go, 1)
    sizes = (4 * late_own.shape[0],) * 2
    late_rows = after(pieces(late_two, late_four), early_go)
    late_first = gate_up(late_rows, w_gate, w_up, 0, hidden // 2)
    early_kept, early_go = home_second(after(early_kept, late_first), early_far)
    early_far = cross(early_go, 0)
    late_second = gate_up(after(late_rows, early_go), w_gate, w_up, hidden // 2, hidden // 2)
    early_result = home_third(after(early_kept, late_second), early_far)
    late_hidden = [late_first, late_second]
    out_left = down(after(late_hidden, early_result), sizes, w_down, 0, half)
    left = home_first(out_left)
    left_far = cross(left[1], 1)
    out_right = down(after(late_hidden, early_result, left[1]), sizes, w_down, half, half)
    left = home_second(after(left[0], out_right), left_far)
    left_far = cross(left[1], 0)
    right = home_first(after(out_right, left[1]))
    right_far = cross(right[1], 1)
    early_back = send_home(after(early_result, right[1]), line)
    left_kept, early_back = lax.optimization_barrier((left[0], early_back))
    left_result = home_third(left_kept, left_far)
    left_back = send_home(left_result, line)
    right = home_second(after(right[0], left_result), right_far)
    right_far = cross(right[1], 0)
    late_back = [left_back, send_home(home_third(right[0], right_far), line)]
    return early_back, jnp.concatenate(late_back, axis=1)


def on_device(
    residual,
    x_raw,
    z_gate,
    conv_w,
    conv_b,
    xproj_w,
    dtproj_w,
    dt_bias,
    a_rate,
    skip_gain,
    out_w,
    norm_gain,
    route_ids,
    route_w,
    w_gate,
    w_up,
    w_down,
):
    owners, contexts, dps = (lax.axis_size(a) for a in ("expert", "context", "dp"))
    me = lax.axis_index("expert")
    place, half = me // 2, me % 2
    line = owners // 2
    length, channels = x_raw.shape[2:]
    width = residual.shape[3]
    row_count = residual.shape[2]

    values = x_raw[0, 0]
    prior_rim = from_behind(values[length - (CONV - 1) :], "context", 1)
    padded = jnp.concatenate([prior_rim, values], axis=0).astype(F32)
    conv_sum = conv_b[None, :] + sum(
        (
            conv_w[lag_index][None, :] * padded[lag_index : lag_index + length]
            for lag_index in range(CONV)
        )
    )
    mixed_in = jax.nn.silu(conv_sum).astype(BF16)
    projected = jnp.dot(mixed_in, xproj_w, preferred_element_type=F32).astype(BF16)
    shares = projected.reshape(line, length // line, -1)

    def share_of(s):
        return lax.dynamic_index_in_dim(shares, (place + s) % line, 0, keepdims=False)

    share = add_up(share_of(0), *[along_line(share_of(s), s) for s in range(1, line)]).astype(BF16)
    share = add_up(share, swap_pair(share)).astype(BF16)
    pieces = [share] + [along_line(share, s) for s in range(1, line)]

    neg = -a_rate.reshape(NSTATE, channels // LANES, LANES)
    neg = jnp.pad(neg, ((0, 0), (0, SUB - channels // LANES), (0, 0)))
    where = jnp.stack([place, half]).astype(jnp.int32)
    y, total, end, bc = run_scan(where, pieces, dtproj_w, dt_bias[None, :], neg, mixed_in)
    enter = from_behind(end, "context", 1)
    for step in range(contexts - 2):
        decay = jnp.exp(total[-SUB:][None] * neg)
        enter = from_behind(end + decay * enter, "context", 1)
    kept, sent, blocks = run_out(
        where, line, y, total, enter, bc, neg, mixed_in, z_gate[0, 0], skip_gain[None, :], out_w
    )
    got = swap_pair(sent)
    over_z = add_up(blocks[0], *[along_line(blocks[s], s) for s in range(1, line)])
    both = add_up(kept, got).astype(BF16).reshape(line, row_count, -1)
    other = swap_pair(over_z[row_count:].astype(BF16))
    sums = [
        add_up(both[0], *[along_line(both[s], s) for s in range(1, line)]),
        add_up(over_z[:row_count], other),
    ]
    mixer_out = jnp.concatenate(sums, axis=1)

    stream_f = (residual[0, 0].astype(F32) + mixer_out).astype(BF16).astype(F32)
    normed = (
        stream_f
        * lax.rsqrt(jnp.mean(stream_f * stream_f, axis=1, keepdims=True) + 1e-05)
        * norm_gain[None, :]
    ).astype(BF16)
    ids, weights = route_ids[0, 0], route_w[0, 0]
    capacity = min(row_count, 8 * ((3 * row_count * TOP + 16 * line - 1) // (16 * line)))
    cuts = (0, 8, capacity) if contexts == 2 and dps == 2 and capacity > 8 else (0, capacity)
    named = jnp.any(ids[:, :, None] == jnp.arange(line, dtype=jnp.int32), axis=1)
    rank = jnp.cumsum(named.astype(jnp.int32), axis=0) - 1
    chosen = ids[:, :, None] == jnp.arange(line, dtype=jnp.int32)
    rank_of = jnp.sum(jnp.where(chosen, rank[:, None, :], 0), axis=2)
    away = (ids - place + line) % line
    placing, weighting, packed = [], [], []
    for low, high in zip(cuts[:-1], cuts[1:]):
        inside = (rank_of >= low) & (rank_of < high)
        slot_of = jnp.where(inside, away * (high - low) + rank_of - low, -1)
        hits = slot_of[:, :, None] == jnp.arange(line * (high - low), dtype=jnp.int32)
        placing = jnp.any(hits, axis=1).astype(BF16)
        weighting.append(jnp.sum(jnp.where(hits, weights[:, :, None], 0.0), axis=1))
        rows = lax.dot_general(
            placing, normed, (((0,), (0,)), ((), ())), preferred_element_type=F32
        )
        packed.append(rows.astype(BF16))
    if len(packed) == 2:
        back = square_experts(*packed, line, w_gate[0], w_up[0], w_down[0])
    else:
        back = [plain_experts(packed[0], line, w_gate[0], w_up[0], w_down[0])]
    expert_sum = jnp.dot(
        jnp.concatenate(weighting, axis=1),
        jnp.concatenate(back, axis=0).astype(F32),
        precision=lax.Precision.HIGHEST,
        preferred_element_type=F32,
    )
    mixed = (stream_f + expert_sum).astype(BF16)
    return mixed.reshape(1, 1, row_count, width)


def solution(mesh):
    placed = (
        P("dp", "context", "expert", None),
        P("dp", "context", None, "expert"),
        P("dp", "context", None, "expert"),
        P(None, "expert"),
        P("expert"),
        P("expert", None),
        P(None, "expert"),
        P("expert"),
        P(None, "expert"),
        P("expert"),
        P("expert", None),
        P(),
        P("dp", "context", "expert", None),
        P("dp", "context", "expert", None),
        P("expert", None, ("context", "dp")),
        P("expert", None, ("context", "dp")),
        P("expert", ("context", "dp"), None),
    )
    return jax.shard_map(
        on_device,
        mesh=mesh,
        in_specs=placed,
        out_specs=P("dp", "context", "expert", None),
        check_vma=False,
    )
```

```python
import functools

import jax
import jax.numpy as jnp
from jax import lax
from jax.experimental import pallas as pl
from jax.experimental.pallas import tpu as pltpu
from jax.sharding import PartitionSpec as P

NSTATE = 16
DT_RANK = 256
CONV = 4
TOP = 2
LANES = 128
SUB = 8
F32 = jnp.float32
BF16 = jnp.bfloat16
MIB = 1 << 20


def from_behind(block, axis, distance):
    devices = range(lax.axis_size(axis))
    route = [(i - distance, i) for i in devices if i - distance in devices]
    return lax.ppermute(block, axis, route)


def shift(block, axis, distance):
    size = lax.axis_size(axis)
    return lax.ppermute(block, axis, [(i, (i + distance) % size) for i in range(size)])


def swap_pair(block):
    size = lax.axis_size("expert")
    return lax.ppermute(block, "expert", [(i, i ^ 1) for i in range(size)])


def cost(flops, bytes_accessed, transcendentals=0):
    return pl.CostEstimate(
        flops=int(flops), bytes_accessed=int(bytes_accessed), transcendentals=int(transcendentals)
    )


def spread_rows(values, wide_ref):
    length, count = values.shape
    col = lax.broadcasted_iota(jnp.int32, (count, count * LANES), 1)
    row = lax.broadcasted_iota(jnp.int32, (count, count * LANES), 0)
    ones = jnp.where((col >= row * LANES) & (col < (row + 1) * LANES), 1.0, 0.0).astype(BF16)
    out = jnp.dot(values, ones, preferred_element_type=F32)
    for n in range(count):
        wide_ref[pl.ds(n * length, length), :] = out[:, n * LANES : (n + 1) * LANES]


def scan_kernel(groups, line, place_ref, *refs):
    pieces, refs = refs[:line], refs[line:]
    w_ref, bias_ref, neg_ref, x_ref, y_ref, sum_ref, end_ref, bc_ref = refs[:8]
    low_ref, step_ref, drive_ref, wide_ref = refs[8:]
    length = x_ref.shape[0]
    share = length // line
    for s in range(line):
        start = pl.multiple_of((place_ref[0] + (line - s)) % line * share, share)
        low_ref[pl.ds(start, share), :] = pieces[s][:, :DT_RANK]
        bc_ref[pl.ds(start, share), :] = pieces[s][:, DT_RANK:]
    spread_rows(bc_ref[...], wide_ref)
    for g in range(SUB):
        rows = pl.ds(g, length, stride=SUB)
        if g >= groups:
            step_ref[rows, :] = jnp.zeros((length, LANES), F32)
            drive_ref[rows, :] = jnp.zeros((length, LANES), F32)
            continue
        cols = pl.ds(g * LANES, LANES)
        raw = jnp.dot(low_ref[...], w_ref[:, cols], preferred_element_type=F32) + bias_ref[:, cols]
        step = jnp.maximum(raw, 0.0) + jnp.log1p(jnp.exp(-jnp.abs(raw)))
        step_ref[rows, :] = step
        drive_ref[rows, :] = step * x_ref[:, cols].astype(F32)

    def block(k, carry):
        states, total = list(carry[0]), carry[1]
        for u in range(SUB):
            t = k * SUB + u
            here = pl.ds(pl.multiple_of(t * SUB, SUB), SUB)
            step, drive = step_ref[here, :], drive_ref[here, :]
            total = total + step
            out = jnp.zeros((SUB, LANES), F32)
            for n in range(NSTATE):
                decay = jnp.exp(step * neg_ref[n])
                b = wide_ref[pl.ds(n * length + t, 1), :]
                c = wide_ref[pl.ds((NSTATE + n) * length + t, 1), :]
                states[n] = states[n] * decay + drive * b
                out = out + states[n] * c
            y_ref[here, :] = out
            sum_ref[here, :] = total
        return tuple(states), total

    zero = jnp.zeros((SUB, LANES), F32)
    states, total = lax.fori_loop(0, length // SUB, block, ((zero,) * NSTATE, zero))
    for n in range(NSTATE):
        end_ref[n] = states[n]


def run_scan(place, pieces, w, bias, neg, x):
    length, channels = x.shape
    vmem = pl.BlockSpec(memory_space=pltpu.VMEM)
    tall = jax.ShapeDtypeStruct((length * SUB, LANES), F32)
    return pl.pallas_call(
        functools.partial(scan_kernel, channels // LANES, len(pieces)),
        out_shape=(
            tall,
            tall,
            jax.ShapeDtypeStruct((NSTATE, SUB, LANES), F32),
            jax.ShapeDtypeStruct((length, 2 * NSTATE), BF16),
        ),
        in_specs=[pl.BlockSpec(memory_space=pltpu.SMEM)] + [vmem] * (len(pieces) + 4),
        out_specs=(vmem,) * 4,
        scratch_shapes=[
            pltpu.VMEM((length, DT_RANK), BF16),
            pltpu.VMEM((length * SUB, LANES), F32),
            pltpu.VMEM((length * SUB, LANES), F32),
            pltpu.VMEM((2 * NSTATE * length, LANES), F32),
        ],
        compiler_params=pltpu.CompilerParams(vmem_limit_bytes=20 * MIB),
        cost_estimate=cost(2e8, 4 * MIB, NSTATE * length * channels),
        name="state_scan",
    )(place, *pieces, w, bias, neg, x)


def out_kernel(groups, line, first, at_ref, y_ref, sum_ref, enter_ref, bc_ref, neg_ref, x_ref, z_ref,
               skip_ref, w_hbm, *refs):
    kept_ref, sent_ref, blocks_ref, full_ref, wide_ref, gated_ref, order_ref, w_ref, sems = refs
    length = x_ref.shape[0]
    tiles, _, tile = w_ref.shape

    def fetch(j):
        cols = pl.ds(pl.multiple_of(j * tile, tile), tile)
        return pltpu.make_async_copy(w_hbm.at[:, cols], w_ref.at[j], sems.at[j])

    for j in range(tiles):
        fetch(j).start()
    spread_rows(bc_ref[:, NSTATE:], wide_ref)

    def block(k, carry):
        for u in range(SUB):
            t = k * SUB + u
            here = pl.ds(pl.multiple_of(t * SUB, SUB), SUB)
            total = sum_ref[here, :]
            out = y_ref[here, :]
            for n in range(NSTATE):
                c = wide_ref[pl.ds(n * length + t, 1), :]
                out = out + jnp.exp(total * neg_ref[n]) * enter_ref[n] * c
            full_ref[here, :] = out
        return carry

    lax.fori_loop(0, length // SUB, block, 0)
    for g in range(groups):
        cols = pl.ds(g * LANES, LANES)
        mixed_in = x_ref[:, cols].astype(F32)
        read = full_ref[pl.ds(g, length, stride=SUB), :] + skip_ref[:, cols] * mixed_in
        z = z_ref[:, cols].astype(F32)
        gated_ref[:, cols] = (read * (z / (1.0 + jnp.exp(-z)))).astype(BF16)
    place, half = at_ref[0], at_ref[1]
    count = length // 2
    piece = count // line
    for k in range(line):
        for r in range(2):
            source = pl.multiple_of((2 * ((place + k) % line) + (half ^ r)) * piece, piece)
            order_ref[pl.ds(r * count + k * piece, piece), :] = gated_ref[pl.ds(source, piece), :]
    def project(j):
        fetch(j).wait()
        return jnp.dot(order_ref[...], w_ref[j], preferred_element_type=F32).astype(BF16)

    def step(j, carry):
        cols = pl.ds(pl.multiple_of(j * tile, tile), tile)
        out = project(j)
        kept_ref[:, cols] = out[:count]
        sent_ref[:, cols] = out[count:]
        return carry

    def block_step(j, carry):
        cols = pl.ds(pl.multiple_of((j - first) * tile, tile), tile)
        out = project(j)
        for k in range(line):
            for r in range(2):
                start = r * count + k * piece
                blocks_ref[k, pl.ds(r * piece, piece), cols] = out[start : start + piece]
        return carry

    lax.fori_loop(0, first, step, 0)
    lax.fori_loop(first, tiles, block_step, 0)


def run_out(at, line, y, total, enter, bc, neg, x, z, skip, w):
    length, channels = x.shape
    wide = w.shape[1]
    tile = min(512, wide)
    first = (wide // tile * 5 + 4) // 8
    vmem = pl.BlockSpec(memory_space=pltpu.VMEM)
    part = jax.ShapeDtypeStruct((length // 2, first * tile), BF16)
    blocks = jax.ShapeDtypeStruct((line, length // line, wide - first * tile), BF16)
    return pl.pallas_call(
        functools.partial(out_kernel, channels // LANES, line, first),
        out_shape=(part, part, blocks),
        in_specs=[pl.BlockSpec(memory_space=pltpu.SMEM)] + [vmem] * 8 + [pl.BlockSpec(memory_space=pl.ANY)],
        out_specs=(vmem,) * 3,
        scratch_shapes=[
            pltpu.VMEM((length * SUB, LANES), F32),
            pltpu.VMEM((NSTATE * length, LANES), F32),
            pltpu.VMEM((length, channels), BF16),
            pltpu.VMEM((length, channels), BF16),
            pltpu.VMEM((wide // tile, channels, tile), BF16),
            pltpu.SemaphoreType.DMA((wide // tile,)),
        ],
        compiler_params=pltpu.CompilerParams(vmem_limit_bytes=48 * MIB),
        cost_estimate=cost(
            2 * length * channels * wide, 2 * channels * wide + 8 * MIB, NSTATE * length * channels
        ),
        name="readout_project",
    )(at, y, total, enter, bc, neg, x, z, skip, w)


def gate_up_kernel(count, first, *refs):
    pieces, (gate_hbm, up_hbm, out_ref, rows_ref, gate_ref, up_ref, sems) = refs[:count], refs[count:]
    copies, at = [], 0
    for k, piece in enumerate(pieces):
        rows = pl.ds(at, piece.shape[0])
        copies.append(pltpu.make_async_copy(piece, rows_ref.at[rows, :], sems.at[k]))
        at += piece.shape[0]
    steps, tile = gate_ref.shape[0], gate_ref.shape[2]

    def fetch(j, k):
        cols = pl.ds(pl.multiple_of(first + j * tile, tile), tile)
        source, target = ((gate_hbm, gate_ref), (up_hbm, up_ref))[k]
        return pltpu.make_async_copy(source.at[:, cols], target.at[j], sems.at[count + 2 * j + k])

    for copy in copies:
        copy.start()
    for j in range(steps):
        fetch(j, 0).start()
        fetch(j, 1).start()
    for copy in copies:
        copy.wait()

    def step(j, carry):
        fetch(j, 0).wait()
        fetch(j, 1).wait()
        gate = jnp.dot(rows_ref[...], gate_ref[j], preferred_element_type=F32)
        up = jnp.dot(rows_ref[...], up_ref[j], preferred_element_type=F32)
        cols = pl.ds(pl.multiple_of(j * tile, tile), tile)
        out_ref[:, cols] = (gate / (1.0 + jnp.exp(-gate)) * up).astype(BF16)
        return carry

    lax.fori_loop(0, steps, step, 0)


def gate_up(pieces, w_gate, w_up, first, width):
    depth = w_gate.shape[0]
    rows = sum(p.shape[0] for p in pieces)
    tile = min(256, width)
    steps = width // tile
    anywhere = pl.BlockSpec(memory_space=pl.ANY)
    return pl.pallas_call(
        functools.partial(gate_up_kernel, len(pieces), first),
        out_shape=jax.ShapeDtypeStruct((rows, width), BF16),
        in_specs=[anywhere] * (len(pieces) + 2),
        out_specs=pl.BlockSpec(memory_space=pltpu.VMEM),
        scratch_shapes=[
            pltpu.VMEM((rows, depth), BF16),
            pltpu.VMEM((steps, depth, tile), BF16),
            pltpu.VMEM((steps, depth, tile), BF16),
            pltpu.SemaphoreType.DMA((len(pieces) + 2 * steps,)),
        ],
        compiler_params=pltpu.CompilerParams(vmem_limit_bytes=49 * MIB),
        cost_estimate=cost(4 * rows * depth * width, 4 * depth * width + 2 * rows * depth),
        name="gate_up",
    )(*pieces, w_gate, w_up)


def finish_kernel(count, first, *refs):
    pieces, (have_ref, gate_hbm, up_hbm, down_hbm) = refs[:count], refs[count : count + 4]
    hidden_ref, outs = refs[count + 4], refs[count + 5 : -5]
    rows_ref, gate_ref, up_ref, down_ref, sems = refs[-5:]
    done = have_ref.shape[1]
    steps, tile = gate_ref.shape[0], gate_ref.shape[2]
    last_steps, last_tile = down_ref.shape[0], down_ref.shape[2]

    def fetch(j, k):
        cols = pl.ds(pl.multiple_of(done + j * tile, tile), tile)
        source, target = ((gate_hbm, gate_ref), (up_hbm, up_ref))[k]
        return pltpu.make_async_copy(source.at[:, cols], target.at[j], sems.at[count + 2 * j + k])

    def last_fetch(j):
        cols = pl.ds(pl.multiple_of(first + j * last_tile, last_tile), last_tile)
        sem = sems.at[count + 2 * steps + j]
        return pltpu.make_async_copy(down_hbm.at[:, cols], down_ref.at[j], sem)

    copies, at = [], 0
    for k, piece in enumerate(pieces):
        rows = pl.ds(at, piece.shape[0])
        copies.append(pltpu.make_async_copy(piece, rows_ref.at[rows, :], sems.at[k]))
        at += piece.shape[0]
    for copy in copies:
        copy.start()
    for j in range(steps):
        fetch(j, 0).start()
        fetch(j, 1).start()
    for j in range(last_steps):
        last_fetch(j).start()
    hidden_ref[:, pl.ds(0, done)] = have_ref[...]
    for copy in copies:
        copy.wait()

    def step(j, carry):
        fetch(j, 0).wait()
        fetch(j, 1).wait()
        gate = jnp.dot(rows_ref[...], gate_ref[j], preferred_element_type=F32)
        up = jnp.dot(rows_ref[...], up_ref[j], preferred_element_type=F32)
        cols = pl.ds(pl.multiple_of(done + j * tile, tile), tile)
        hidden_ref[:, cols] = (gate / (1.0 + jnp.exp(-gate)) * up).astype(BF16)
        return carry

    def last_step(j, carry):
        last_fetch(j).wait()
        out = jnp.dot(hidden_ref[...], down_ref[j], preferred_element_type=F32).astype(BF16)
        cols = pl.ds(pl.multiple_of(j * last_tile, last_tile), last_tile)
        start = 0
        for ref in outs:
            ref[:, cols] = out[start : start + ref.shape[0]]
            start += ref.shape[0]
        return carry

    lax.fori_loop(0, steps, step, 0)
    lax.fori_loop(0, last_steps, last_step, 0)


def finish(pieces, have, sizes, w_gate, w_up, w_down, first, width):
    depth, hidden = w_gate.shape
    rows, done = have.shape
    tile, last_tile = min(256, hidden - done), min(512, width)
    steps, last_steps = (hidden - done) // tile, width // last_tile
    vmem, anywhere = pl.BlockSpec(memory_space=pltpu.VMEM), pl.BlockSpec(memory_space=pl.ANY)
    shapes = [(rows, hidden)] + [(n, width) for n in sizes]
    hidden_out, *outs = pl.pallas_call(
        functools.partial(finish_kernel, len(pieces), first),
        out_shape=tuple(jax.ShapeDtypeStruct(shape, BF16) for shape in shapes),
        in_specs=[anywhere] * len(pieces) + [vmem] + [anywhere] * 3,
        out_specs=(vmem,) * len(shapes),
        scratch_shapes=[
            pltpu.VMEM((rows, depth), BF16),
            pltpu.VMEM((steps, depth, tile), BF16),
            pltpu.VMEM((steps, depth, tile), BF16),
            pltpu.VMEM((last_steps, hidden, last_tile), BF16),
            pltpu.SemaphoreType.DMA((len(pieces) + 2 * steps + last_steps,)),
        ],
        compiler_params=pltpu.CompilerParams(vmem_limit_bytes=49 * MIB),
        cost_estimate=cost(
            4 * rows * depth * (hidden - done) + 2 * rows * hidden * width,
            4 * depth * (hidden - done) + 2 * hidden * width + 2 * rows * (depth + width),
        ),
        name="gate_up_down",
    )(*pieces, have, w_gate, w_up, w_down)
    return hidden_out, outs


def down_kernel(count, first, *refs):
    pieces, w_hbm, outs = refs[:count], refs[count], refs[count + 1 : -3]
    rows_ref, w_ref, sems = refs[-3:]
    tiles, _, tile = w_ref.shape

    def fetch(j):
        source = pl.ds(pl.multiple_of(first + j * tile, tile), tile)
        return pltpu.make_async_copy(w_hbm.at[:, source], w_ref.at[j], sems.at[j])

    for j in range(tiles):
        fetch(j).start()
    at = 0
    for piece in pieces:
        rows_ref[:, pl.ds(at, piece.shape[1])] = piece[...]
        at += piece.shape[1]

    def step(j, carry):
        fetch(j).wait()
        out = jnp.dot(rows_ref[...], w_ref[j], preferred_element_type=F32).astype(BF16)
        cols = pl.ds(pl.multiple_of(j * tile, tile), tile)
        start = 0
        for ref in outs:
            ref[:, cols] = out[start : start + ref.shape[0]]
            start += ref.shape[0]
        return carry

    lax.fori_loop(0, tiles, step, 0)


def down(pieces, sizes, w_down, first, width):
    hidden, rows = w_down.shape[0], pieces[0].shape[0]
    tile = min(512, width)
    vmem = pl.BlockSpec(memory_space=pltpu.VMEM)
    return pl.pallas_call(
        functools.partial(down_kernel, len(pieces), first),
        out_shape=tuple(jax.ShapeDtypeStruct((n, width), BF16) for n in sizes),
        in_specs=[vmem] * len(pieces) + [pl.BlockSpec(memory_space=pl.ANY)],
        out_specs=(vmem,) * len(sizes),
        scratch_shapes=[
            pltpu.VMEM((rows, hidden), BF16),
            pltpu.VMEM((width // tile, hidden, tile), BF16),
            pltpu.SemaphoreType.DMA((width // tile,)),
        ],
        compiler_params=pltpu.CompilerParams(vmem_limit_bytes=49 * MIB),
        cost_estimate=cost(2 * rows * hidden * width, 2 * hidden * width + 2 * rows * (hidden + width)),
        name="down",
    )(*pieces, w_down)


def add_up(*parts):
    return sum(p.astype(F32) for p in parts)


def along_line(block, distance):
    size = lax.axis_size("expert")
    return lax.ppermute(block, "expert", [(e, (e + 2 * distance) % size) for e in range(size)])


def cross(block, turn):
    owners, dps = lax.axis_size("expert"), lax.axis_size("dp")
    route = []
    for e in range(owners):
        for core in range(2):
            for d in range(dps):
                to = (e ^ 1, core, d) if core == turn else (e, core, d ^ 1)
                route.append(((e * 2 + core) * dps + d, (to[0] * 2 + core) * dps + to[2]))
    return lax.ppermute(block, ("expert", "context", "dp"), route)


def after(blocks, *others):
    return lax.optimization_barrier((blocks, others))[0]


def send_rows(packed, line, way=1):
    size = packed.shape[0] // line
    parts = [packed[size * s : size * (s + 1)] for s in range(line)]
    return [parts[0]] + [along_line(parts[s], way * s) for s in range(1, line)]


def plain_experts(packed, line, w_gate, w_up, w_down):
    own = jnp.concatenate(send_rows(packed, line), axis=0)
    rows = jnp.concatenate([own, swap_pair(own)], axis=0)
    rows = lax.all_gather(rows, ("context", "dp"), axis=0, tiled=True)
    hidden = gate_up([rows], w_gate, w_up, 0, w_gate.shape[1])
    out = down([hidden], (rows.shape[0],), w_down, 0, w_down.shape[1])[0]
    mine = lax.psum_scatter(out, ("context", "dp"), scatter_dimension=0, tiled=True)
    count = own.shape[0]
    result = add_up(mine[:count], swap_pair(mine[count:])).astype(BF16)
    return jnp.concatenate(send_rows(result, line, -1), axis=0)


def square_experts(early, late, line, w_gate, w_up, w_down):
    width = w_down.shape[1]
    half = width // 2
    hidden = w_down.shape[0]
    most = hidden // 2

    def pieces(two, four):
        return [two, four, shift(two, "context", 1), shift(four, "context", 1)]

    def part(terms, start, stop):
        return add_up(*[t[start:stop] for t in terms]).astype(BF16)

    def home_first(outs, *others):
        terms = [after(outs[0], *others), shift(outs[1], "context", 1)]
        rows = outs[0].shape[0]
        return terms, part(terms, rows // 2, rows)

    def home_second(terms, far):
        terms = terms + [far]
        rows = far.shape[0]
        return terms, part(terms, rows // 2, rows)

    def home_third(terms, far):
        return part(terms + [far], 0, far.shape[0])

    early_came = send_rows(early, line)
    early_own = jnp.concatenate(early_came, axis=0)
    late_came = send_rows(after(late, early_own), line)
    early_near = cross(early_own, 0)
    early_two = jnp.concatenate([early_own, early_near], axis=0)
    early_four = cross(early_two, 1)
    late_came[0] = after(late_came[0], early_near)
    late_own = jnp.concatenate(late_came, axis=0)
    late_near = cross(late_own, 0)
    sizes = (4 * early_own.shape[0],) * 2
    early_rows = after(pieces(early_two, early_four), late_own)
    early_first = gate_up(early_rows, w_gate, w_up, 0, most)

    late_two = jnp.concatenate([after(late_own, early_first), late_near], axis=0)
    late_four = cross(late_two, 1)
    early_rows = after(early_rows, late_two)
    early_out = finish(early_rows, early_first, sizes, w_gate, w_up, w_down, 0, width)[1]
    late_four = after(late_four, early_out)
    early_kept, early_go = home_first(early_out, late_four)
    early_far = cross(early_go, 1)
    sizes = (4 * late_own.shape[0],) * 2
    late_rows = after(pieces(late_two, late_four), early_go)
    late_first = gate_up(late_rows, w_gate, w_up, 0, hidden // 2)
    early_kept, early_go = home_second(after(early_kept, late_first), early_far)
    early_far = cross(early_go, 0)
    late_rows = after(late_rows, early_go)
    late_hidden, out_left = finish(late_rows, late_first, sizes, w_gate, w_up, w_down, 0, half)
    early_result = home_third(after(early_kept, out_left[0]), early_far)
    left = home_first(out_left)
    left_far = cross(left[1], 1)
    out_right = down([after(late_hidden, left[1])], sizes, w_down, half, half)
    left = home_second(after(left[0], out_right), left_far)
    left_far = cross(left[1], 0)
    right = home_first(after(out_right, left[1]))
    right_far = cross(right[1], 1)
    left_result = home_third(after(left[0], right[1]), left_far)
    right = home_second(after(right[0], left_result), right_far)
    right_far = cross(right[1], 0)
    few, many = early_result.shape[0] // line, left_result.shape[0] // line
    packed = []
    for s in range(line):
        mine = early_result[few * s : few * (s + 1)]
        packed += [mine[:, :half], mine[:, half:], left_result[many * s : many * (s + 1)]]
    left_came = send_rows(jnp.concatenate(packed, axis=0), line, -1)
    right_result = home_third(right[0], right_far)
    right_came = send_rows(right_result, line, -1)
    left_came = after(left_came, right_result)
    left_rows = [c[:few] for c in left_came] + [c[2 * few :] for c in left_came]
    right_rows = [c[few : 2 * few] for c in left_came] + right_came
    return [jnp.concatenate(rows, axis=0) for rows in (left_rows, right_rows)]


def on_device(
    residual,
    x_raw,
    z_gate,
    conv_w,
    conv_b,
    xproj_w,
    dtproj_w,
    dt_bias,
    a_rate,
    skip_gain,
    out_w,
    norm_gain,
    route_ids,
    route_w,
    w_gate,
    w_up,
    w_down,
):
    owners, contexts, dps = (lax.axis_size(a) for a in ("expert", "context", "dp"))
    me = lax.axis_index("expert")
    place, half = me // 2, me % 2
    line = owners // 2
    length, channels = x_raw.shape[2:]
    width = residual.shape[3]
    row_count = residual.shape[2]

    values = x_raw[0, 0]
    prior_rim = from_behind(values[length - (CONV - 1) :], "context", 1)
    padded = jnp.concatenate([prior_rim, values], axis=0).astype(F32)
    conv_sum = conv_b[None, :] + sum(
        (
            conv_w[lag_index][None, :] * padded[lag_index : lag_index + length]
            for lag_index in range(CONV)
        )
    )
    mixed_in = jax.nn.silu(conv_sum).astype(BF16)
    projected = jnp.dot(mixed_in, xproj_w, preferred_element_type=F32).astype(BF16)
    shares = projected.reshape(line, length // line, -1)

    def share_of(s):
        return lax.dynamic_index_in_dim(shares, (place + s) % line, 0, keepdims=False)

    share = add_up(share_of(0), *[along_line(share_of(s), s) for s in range(1, line)]).astype(BF16)
    share = add_up(share, swap_pair(share)).astype(BF16)
    pieces = [share] + [along_line(share, s) for s in range(1, line)]

    neg = -a_rate.reshape(NSTATE, channels // LANES, LANES)
    neg = jnp.pad(neg, ((0, 0), (0, SUB - channels // LANES), (0, 0)))
    where = jnp.stack([place, half]).astype(jnp.int32)
    y, total, end, bc = run_scan(where, pieces, dtproj_w, dt_bias[None, :], neg, mixed_in)
    enter = from_behind(end, "context", 1)
    for step in range(contexts - 2):
        decay = jnp.exp(total[-SUB:][None] * neg)
        enter = from_behind(end + decay * enter, "context", 1)
    kept, sent, blocks = run_out(
        where, line, y, total, enter, bc, neg, mixed_in, z_gate[0, 0], skip_gain[None, :], out_w
    )
    got = swap_pair(sent)
    over_z = add_up(blocks[0], *[along_line(blocks[s], s) for s in range(1, line)])
    both = add_up(kept, got).astype(BF16).reshape(line, row_count, -1)
    other = swap_pair(over_z[row_count:].astype(BF16))
    sums = [
        add_up(both[0], *[along_line(both[s], s) for s in range(1, line)]),
        add_up(over_z[:row_count], other),
    ]
    mixer_out = jnp.concatenate(sums, axis=1)

    stream_f = (residual[0, 0].astype(F32) + mixer_out).astype(BF16).astype(F32)
    normed = (
        stream_f
        * lax.rsqrt(jnp.mean(stream_f * stream_f, axis=1, keepdims=True) + 1e-05)
        * norm_gain[None, :]
    ).astype(BF16)
    ids, weights = route_ids[0, 0], route_w[0, 0]
    capacity = min(row_count, 8 * ((3 * row_count * TOP + 16 * line - 1) // (16 * line)))
    cuts = (0, 8, capacity) if contexts == 2 and dps == 2 and capacity > 8 else (0, capacity)
    named = jnp.any(ids[:, :, None] == jnp.arange(line, dtype=jnp.int32), axis=1)
    rank = jnp.cumsum(named.astype(jnp.int32), axis=0) - 1
    chosen = ids[:, :, None] == jnp.arange(line, dtype=jnp.int32)
    rank_of = jnp.sum(jnp.where(chosen, rank[:, None, :], 0), axis=2)
    away = (ids - place + line) % line
    placing, weighting, packed = [], [], []
    for low, high in zip(cuts[:-1], cuts[1:]):
        inside = (rank_of >= low) & (rank_of < high)
        slot_of = jnp.where(inside, away * (high - low) + rank_of - low, -1)
        hits = slot_of[:, :, None] == jnp.arange(line * (high - low), dtype=jnp.int32)
        placing = jnp.any(hits, axis=1).astype(BF16)
        weighting.append(jnp.sum(jnp.where(hits, weights[:, :, None], 0.0), axis=1))
        rows = lax.dot_general(
            placing, normed, (((0,), (0,)), ((), ())), preferred_element_type=F32
        )
        packed.append(rows.astype(BF16))
    if len(packed) == 2:
        back = square_experts(*packed, line, w_gate[0], w_up[0], w_down[0])
    else:
        back = [plain_experts(packed[0], line, w_gate[0], w_up[0], w_down[0])]
    weighting = jnp.concatenate(weighting, axis=1)
    expert_sum = jnp.concatenate(
        [
            jnp.dot(
                weighting,
                rows.astype(F32),
                precision=lax.Precision.HIGHEST,
                preferred_element_type=F32,
            )
            for rows in back
        ],
        axis=1,
    )
    mixed = (stream_f + expert_sum).astype(BF16)
    return mixed.reshape(1, 1, row_count, width)


def solution(mesh):
    placed = (
        P("dp", "context", "expert", None),
        P("dp", "context", None, "expert"),
        P("dp", "context", None, "expert"),
        P(None, "expert"),
        P("expert"),
        P("expert", None),
        P(None, "expert"),
        P("expert"),
        P(None, "expert"),
        P("expert"),
        P("expert", None),
        P(),
        P("dp", "context", "expert", None),
        P("dp", "context", "expert", None),
        P("expert", None, ("context", "dp")),
        P("expert", None, ("context", "dp")),
        P("expert", ("context", "dp"), None),
    )
    return jax.shard_map(
        on_device,
        mesh=mesh,
        in_specs=placed,
        out_specs=P("dp", "context", "expert", None),
        check_vma=False,
    )
```

```python
import functools

import jax
import jax.numpy as jnp
from jax import lax
from jax.experimental import pallas as pl
from jax.experimental.pallas import tpu as pltpu
from jax.sharding import PartitionSpec as P

NSTATE = 16
DT_RANK = 256
CONV = 4
TOP = 2
LANES = 128
SUB = 8
F32 = jnp.float32
BF16 = jnp.bfloat16
MIB = 1 << 20


def from_behind(block, axis, distance):
    devices = range(lax.axis_size(axis))
    route = [(i - distance, i) for i in devices if i - distance in devices]
    return lax.ppermute(block, axis, route)


def shift(block, axis, distance):
    size = lax.axis_size(axis)
    return lax.ppermute(block, axis, [(i, (i + distance) % size) for i in range(size)])


def swap_pair(block):
    size = lax.axis_size("expert")
    return lax.ppermute(block, "expert", [(i, i ^ 1) for i in range(size)])


def cost(flops, bytes_accessed, transcendentals=0):
    return pl.CostEstimate(
        flops=int(flops), bytes_accessed=int(bytes_accessed), transcendentals=int(transcendentals)
    )


def spread_rows(values, wide_ref):
    length, count = values.shape
    col = lax.broadcasted_iota(jnp.int32, (count, count * LANES), 1)
    row = lax.broadcasted_iota(jnp.int32, (count, count * LANES), 0)
    ones = jnp.where((col >= row * LANES) & (col < (row + 1) * LANES), 1.0, 0.0).astype(BF16)
    out = jnp.dot(values, ones, preferred_element_type=F32)
    for n in range(count):
        wide_ref[pl.ds(n * length, length), :] = out[:, n * LANES : (n + 1) * LANES]


def scan_kernel(groups, line, place_ref, *refs):
    pieces, refs = refs[:line], refs[line:]
    w_ref, bias_ref, neg_ref, x_ref, y_ref, sum_ref, end_ref, bc_ref = refs[:8]
    low_ref, step_ref, drive_ref, wide_ref = refs[8:]
    length = x_ref.shape[0]
    share = length // line
    for s in range(line):
        start = pl.multiple_of((place_ref[0] + (line - s)) % line * share, share)
        low_ref[pl.ds(start, share), :] = pieces[s][:, :DT_RANK]
        bc_ref[pl.ds(start, share), :] = pieces[s][:, DT_RANK:]
    spread_rows(bc_ref[...], wide_ref)
    for g in range(SUB):
        rows = pl.ds(g, length, stride=SUB)
        if g >= groups:
            step_ref[rows, :] = jnp.zeros((length, LANES), F32)
            drive_ref[rows, :] = jnp.zeros((length, LANES), F32)
            continue
        cols = pl.ds(g * LANES, LANES)
        raw = jnp.dot(low_ref[...], w_ref[:, cols], preferred_element_type=F32) + bias_ref[:, cols]
        step = jnp.maximum(raw, 0.0) + jnp.log1p(jnp.exp(-jnp.abs(raw)))
        step_ref[rows, :] = step
        drive_ref[rows, :] = step * x_ref[:, cols].astype(F32)

    def block(k, carry):
        states, total = list(carry[0]), carry[1]
        for u in range(SUB):
            t = k * SUB + u
            here = pl.ds(pl.multiple_of(t * SUB, SUB), SUB)
            step, drive = step_ref[here, :], drive_ref[here, :]
            total = total + step
            out = jnp.zeros((SUB, LANES), F32)
            for n in range(NSTATE):
                decay = jnp.exp(step * neg_ref[n])
                b = wide_ref[pl.ds(n * length + t, 1), :]
                c = wide_ref[pl.ds((NSTATE + n) * length + t, 1), :]
                states[n] = states[n] * decay + drive * b
                out = out + states[n] * c
            y_ref[here, :] = out
            sum_ref[here, :] = total
        return tuple(states), total

    zero = jnp.zeros((SUB, LANES), F32)
    states, total = lax.fori_loop(0, length // SUB, block, ((zero,) * NSTATE, zero))
    for n in range(NSTATE):
        end_ref[n] = states[n]


def run_scan(place, pieces, w, bias, neg, x):
    length, channels = x.shape
    vmem = pl.BlockSpec(memory_space=pltpu.VMEM)
    tall = jax.ShapeDtypeStruct((length * SUB, LANES), F32)
    return pl.pallas_call(
        functools.partial(scan_kernel, channels // LANES, len(pieces)),
        out_shape=(
            tall,
            tall,
            jax.ShapeDtypeStruct((NSTATE, SUB, LANES), F32),
            jax.ShapeDtypeStruct((length, 2 * NSTATE), BF16),
        ),
        in_specs=[pl.BlockSpec(memory_space=pltpu.SMEM)] + [vmem] * (len(pieces) + 4),
        out_specs=(vmem,) * 4,
        scratch_shapes=[
            pltpu.VMEM((length, DT_RANK), BF16),
            pltpu.VMEM((length * SUB, LANES), F32),
            pltpu.VMEM((length * SUB, LANES), F32),
            pltpu.VMEM((2 * NSTATE * length, LANES), F32),
        ],
        compiler_params=pltpu.CompilerParams(vmem_limit_bytes=20 * MIB),
        cost_estimate=cost(2e8, 4 * MIB, NSTATE * length * channels),
        name="state_scan",
    )(place, *pieces, w, bias, neg, x)


def out_kernel(groups, line, first, at_ref, y_ref, sum_ref, enter_ref, bc_ref, neg_ref, x_ref, z_ref,
               skip_ref, w_hbm, *refs):
    kept_ref, sent_ref, blocks_ref, full_ref, wide_ref, gated_ref, order_ref, w_ref, sems = refs
    length = x_ref.shape[0]
    tiles, _, tile = w_ref.shape

    def fetch(j):
        cols = pl.ds(pl.multiple_of(j * tile, tile), tile)
        return pltpu.make_async_copy(w_hbm.at[:, cols], w_ref.at[j], sems.at[j])

    for j in range(tiles):
        fetch(j).start()
    spread_rows(bc_ref[:, NSTATE:], wide_ref)

    def block(k, carry):
        for u in range(SUB):
            t = k * SUB + u
            here = pl.ds(pl.multiple_of(t * SUB, SUB), SUB)
            total = sum_ref[here, :]
            out = y_ref[here, :]
            for n in range(NSTATE):
                c = wide_ref[pl.ds(n * length + t, 1), :]
                out = out + jnp.exp(total * neg_ref[n]) * enter_ref[n] * c
            full_ref[here, :] = out
        return carry

    lax.fori_loop(0, length // SUB, block, 0)
    for g in range(groups):
        cols = pl.ds(g * LANES, LANES)
        mixed_in = x_ref[:, cols].astype(F32)
        read = full_ref[pl.ds(g, length, stride=SUB), :] + skip_ref[:, cols] * mixed_in
        z = z_ref[:, cols].astype(F32)
        gated_ref[:, cols] = (read * (z / (1.0 + jnp.exp(-z)))).astype(BF16)
    place, half = at_ref[0], at_ref[1]
    count = length // 2
    piece = count // line
    for k in range(line):
        for r in range(2):
            source = pl.multiple_of((2 * ((place + k) % line) + (half ^ r)) * piece, piece)
            order_ref[pl.ds(r * count + k * piece, piece), :] = gated_ref[pl.ds(source, piece), :]
    def project(j):
        fetch(j).wait()
        return jnp.dot(order_ref[...], w_ref[j], preferred_element_type=F32).astype(BF16)

    def step(j, carry):
        cols = pl.ds(pl.multiple_of(j * tile, tile), tile)
        out = project(j)
        kept_ref[:, cols] = out[:count]
        sent_ref[:, cols] = out[count:]
        return carry

    def block_step(j, carry):
        cols = pl.ds(pl.multiple_of((j - first) * tile, tile), tile)
        out = project(j)
        for k in range(line):
            for r in range(2):
                start = r * count + k * piece
                blocks_ref[k, pl.ds(r * piece, piece), cols] = out[start : start + piece]
        return carry

    lax.fori_loop(0, first, step, 0)
    lax.fori_loop(first, tiles, block_step, 0)


def run_out(at, line, y, total, enter, bc, neg, x, z, skip, w):
    length, channels = x.shape
    wide = w.shape[1]
    tile = min(512, wide)
    first = (wide // tile * 5 + 4) // 8
    vmem = pl.BlockSpec(memory_space=pltpu.VMEM)
    part = jax.ShapeDtypeStruct((length // 2, first * tile), BF16)
    blocks = jax.ShapeDtypeStruct((line, length // line, wide - first * tile), BF16)
    return pl.pallas_call(
        functools.partial(out_kernel, channels // LANES, line, first),
        out_shape=(part, part, blocks),
        in_specs=[pl.BlockSpec(memory_space=pltpu.SMEM)] + [vmem] * 8 + [pl.BlockSpec(memory_space=pl.ANY)],
        out_specs=(vmem,) * 3,
        scratch_shapes=[
            pltpu.VMEM((length * SUB, LANES), F32),
            pltpu.VMEM((NSTATE * length, LANES), F32),
            pltpu.VMEM((length, channels), BF16),
            pltpu.VMEM((length, channels), BF16),
            pltpu.VMEM((wide // tile, channels, tile), BF16),
            pltpu.SemaphoreType.DMA((wide // tile,)),
        ],
        compiler_params=pltpu.CompilerParams(vmem_limit_bytes=48 * MIB),
        cost_estimate=cost(
            2 * length * channels * wide, 2 * channels * wide + 8 * MIB, NSTATE * length * channels
        ),
        name="readout_project",
    )(at, y, total, enter, bc, neg, x, z, skip, w)


def gate_up_kernel(count, first, *refs):
    pieces, (gate_hbm, up_hbm, out_ref, rows_ref, gate_ref, up_ref, sems) = refs[:count], refs[count:]
    copies, at = [], 0
    for k, piece in enumerate(pieces):
        rows = pl.ds(at, piece.shape[0])
        copies.append(pltpu.make_async_copy(piece, rows_ref.at[rows, :], sems.at[k]))
        at += piece.shape[0]
    steps, tile = gate_ref.shape[0], gate_ref.shape[2]

    def fetch(j, k):
        cols = pl.ds(pl.multiple_of(first + j * tile, tile), tile)
        source, target = ((gate_hbm, gate_ref), (up_hbm, up_ref))[k]
        return pltpu.make_async_copy(source.at[:, cols], target.at[j], sems.at[count + 2 * j + k])

    for copy in copies:
        copy.start()
    fetch(0, 0).start()
    fetch(0, 1).start()
    for copy in copies:
        copy.wait()

    def step(j, carry):
        fetch(j, 0).wait()
        fetch(j, 1).wait()

        @pl.when(j + 1 < steps)
        def _():
            fetch(j + 1, 0).start()
            fetch(j + 1, 1).start()

        gate = jnp.dot(rows_ref[...], gate_ref[j], preferred_element_type=F32)
        up = jnp.dot(rows_ref[...], up_ref[j], preferred_element_type=F32)
        cols = pl.ds(pl.multiple_of(j * tile, tile), tile)
        out_ref[:, cols] = (gate / (1.0 + jnp.exp(-gate)) * up).astype(BF16)
        return carry

    lax.fori_loop(0, steps, step, 0)


def gate_up(pieces, w_gate, w_up, first, width):
    depth = w_gate.shape[0]
    rows = sum(p.shape[0] for p in pieces)
    tile = min(256, width)
    steps = width // tile
    anywhere = pl.BlockSpec(memory_space=pl.ANY)
    return pl.pallas_call(
        functools.partial(gate_up_kernel, len(pieces), first),
        out_shape=jax.ShapeDtypeStruct((rows, width), BF16),
        in_specs=[anywhere] * (len(pieces) + 2),
        out_specs=pl.BlockSpec(memory_space=pltpu.VMEM),
        scratch_shapes=[
            pltpu.VMEM((rows, depth), BF16),
            pltpu.VMEM((steps, depth, tile), BF16),
            pltpu.VMEM((steps, depth, tile), BF16),
            pltpu.SemaphoreType.DMA((len(pieces) + 2 * steps,)),
        ],
        compiler_params=pltpu.CompilerParams(vmem_limit_bytes=49 * MIB),
        cost_estimate=cost(4 * rows * depth * width, 4 * depth * width + 2 * rows * depth),
        name="gate_up",
    )(*pieces, w_gate, w_up)


def finish_kernel(count, first, *refs):
    pieces, (have_ref, gate_hbm, up_hbm, down_hbm) = refs[:count], refs[count : count + 4]
    hidden_ref, outs = refs[count + 4], refs[count + 5 : -5]
    rows_ref, gate_ref, up_ref, down_ref, sems = refs[-5:]
    done = have_ref.shape[1]
    steps, tile = gate_ref.shape[0], gate_ref.shape[2]
    last_steps, last_tile = down_ref.shape[0], down_ref.shape[2]

    def fetch(j, k):
        cols = pl.ds(pl.multiple_of(done + j * tile, tile), tile)
        source, target = ((gate_hbm, gate_ref), (up_hbm, up_ref))[k]
        return pltpu.make_async_copy(source.at[:, cols], target.at[j], sems.at[count + 2 * j + k])

    def last_fetch(j):
        cols = pl.ds(pl.multiple_of(first + j * last_tile, last_tile), last_tile)
        sem = sems.at[count + 2 * steps + j]
        return pltpu.make_async_copy(down_hbm.at[:, cols], down_ref.at[j], sem)

    copies, at = [], 0
    for k, piece in enumerate(pieces):
        rows = pl.ds(at, piece.shape[0])
        copies.append(pltpu.make_async_copy(piece, rows_ref.at[rows, :], sems.at[k]))
        at += piece.shape[0]
    for copy in copies:
        copy.start()
    fetch(0, 0).start()
    fetch(0, 1).start()
    hidden_ref[:, pl.ds(0, done)] = have_ref[...]
    for copy in copies:
        copy.wait()

    def step(j, carry):
        fetch(j, 0).wait()
        fetch(j, 1).wait()

        @pl.when(j + 1 < steps)
        def _():
            fetch(j + 1, 0).start()
            fetch(j + 1, 1).start()

        @pl.when(j + 1 == steps)
        def _():
            for k in range(last_steps):
                last_fetch(k).start()

        gate = jnp.dot(rows_ref[...], gate_ref[j], preferred_element_type=F32)
        up = jnp.dot(rows_ref[...], up_ref[j], preferred_element_type=F32)
        cols = pl.ds(pl.multiple_of(done + j * tile, tile), tile)
        hidden_ref[:, cols] = (gate / (1.0 + jnp.exp(-gate)) * up).astype(BF16)
        return carry

    def last_step(j, carry):
        last_fetch(j).wait()
        out = jnp.dot(hidden_ref[...], down_ref[j], preferred_element_type=F32).astype(BF16)
        cols = pl.ds(pl.multiple_of(j * last_tile, last_tile), last_tile)
        start = 0
        for ref in outs:
            ref[:, cols] = out[start : start + ref.shape[0]]
            start += ref.shape[0]
        return carry

    lax.fori_loop(0, steps, step, 0)
    lax.fori_loop(0, last_steps, last_step, 0)


def finish(pieces, have, sizes, w_gate, w_up, w_down, first, width):
    depth, hidden = w_gate.shape
    rows, done = have.shape
    tile, last_tile = min(256, hidden - done), min(512, width)
    steps, last_steps = (hidden - done) // tile, width // last_tile
    vmem, anywhere = pl.BlockSpec(memory_space=pltpu.VMEM), pl.BlockSpec(memory_space=pl.ANY)
    shapes = [(rows, hidden)] + [(n, width) for n in sizes]
    hidden_out, *outs = pl.pallas_call(
        functools.partial(finish_kernel, len(pieces), first),
        out_shape=tuple(jax.ShapeDtypeStruct(shape, BF16) for shape in shapes),
        in_specs=[anywhere] * len(pieces) + [vmem] + [anywhere] * 3,
        out_specs=(vmem,) * len(shapes),
        scratch_shapes=[
            pltpu.VMEM((rows, depth), BF16),
            pltpu.VMEM((steps, depth, tile), BF16),
            pltpu.VMEM((steps, depth, tile), BF16),
            pltpu.VMEM((last_steps, hidden, last_tile), BF16),
            pltpu.SemaphoreType.DMA((len(pieces) + 2 * steps + last_steps,)),
        ],
        compiler_params=pltpu.CompilerParams(vmem_limit_bytes=49 * MIB),
        cost_estimate=cost(
            4 * rows * depth * (hidden - done) + 2 * rows * hidden * width,
            4 * depth * (hidden - done) + 2 * hidden * width + 2 * rows * (depth + width),
        ),
        name="gate_up_down",
    )(*pieces, have, w_gate, w_up, w_down)
    return hidden_out, outs


def down_kernel(count, first, *refs):
    pieces, w_hbm, outs = refs[:count], refs[count], refs[count + 1 : -3]
    rows_ref, w_ref, sems = refs[-3:]
    tiles, _, tile = w_ref.shape

    def fetch(j):
        source = pl.ds(pl.multiple_of(first + j * tile, tile), tile)
        return pltpu.make_async_copy(w_hbm.at[:, source], w_ref.at[j], sems.at[j])

    for j in range(tiles):
        fetch(j).start()
    at = 0
    for piece in pieces:
        rows_ref[:, pl.ds(at, piece.shape[1])] = piece[...]
        at += piece.shape[1]

    def step(j, carry):
        fetch(j).wait()
        out = jnp.dot(rows_ref[...], w_ref[j], preferred_element_type=F32).astype(BF16)
        cols = pl.ds(pl.multiple_of(j * tile, tile), tile)
        start = 0
        for ref in outs:
            ref[:, cols] = out[start : start + ref.shape[0]]
            start += ref.shape[0]
        return carry

    lax.fori_loop(0, tiles, step, 0)


def down(pieces, sizes, w_down, first, width):
    hidden, rows = w_down.shape[0], pieces[0].shape[0]
    tile = min(512, width)
    vmem = pl.BlockSpec(memory_space=pltpu.VMEM)
    return pl.pallas_call(
        functools.partial(down_kernel, len(pieces), first),
        out_shape=tuple(jax.ShapeDtypeStruct((n, width), BF16) for n in sizes),
        in_specs=[vmem] * len(pieces) + [pl.BlockSpec(memory_space=pl.ANY)],
        out_specs=(vmem,) * len(sizes),
        scratch_shapes=[
            pltpu.VMEM((rows, hidden), BF16),
            pltpu.VMEM((width // tile, hidden, tile), BF16),
            pltpu.SemaphoreType.DMA((width // tile,)),
        ],
        compiler_params=pltpu.CompilerParams(vmem_limit_bytes=49 * MIB),
        cost_estimate=cost(2 * rows * hidden * width, 2 * hidden * width + 2 * rows * (hidden + width)),
        name="down",
    )(*pieces, w_down)


def add_up(*parts):
    return sum(p.astype(F32) for p in parts)


def along_line(block, distance):
    size = lax.axis_size("expert")
    return lax.ppermute(block, "expert", [(e, (e + 2 * distance) % size) for e in range(size)])


def cross(block, turn):
    owners, dps = lax.axis_size("expert"), lax.axis_size("dp")
    route = []
    for e in range(owners):
        for core in range(2):
            for d in range(dps):
                to = (e ^ 1, core, d) if core == turn else (e, core, d ^ 1)
                route.append(((e * 2 + core) * dps + d, (to[0] * 2 + core) * dps + to[2]))
    return lax.ppermute(block, ("expert", "context", "dp"), route)


def after(blocks, *others):
    return lax.optimization_barrier((blocks, others))[0]


def send_rows(packed, line, way=1):
    size = packed.shape[0] // line
    parts = [packed[size * s : size * (s + 1)] for s in range(line)]
    return [parts[0]] + [along_line(parts[s], way * s) for s in range(1, line)]


def plain_experts(packed, line, w_gate, w_up, w_down):
    own = jnp.concatenate(send_rows(packed, line), axis=0)
    rows = jnp.concatenate([own, swap_pair(own)], axis=0)
    rows = lax.all_gather(rows, ("context", "dp"), axis=0, tiled=True)
    hidden = gate_up([rows], w_gate, w_up, 0, w_gate.shape[1])
    out = down([hidden], (rows.shape[0],), w_down, 0, w_down.shape[1])[0]
    mine = lax.psum_scatter(out, ("context", "dp"), scatter_dimension=0, tiled=True)
    count = own.shape[0]
    result = add_up(mine[:count], swap_pair(mine[count:])).astype(BF16)
    return jnp.concatenate(send_rows(result, line, -1), axis=0)


def square_experts(early, late, line, w_gate, w_up, w_down):
    width = w_down.shape[1]
    half = width // 2
    hidden = w_down.shape[0]
    most = hidden // 2

    def pieces(two, four):
        return [two, four, shift(two, "context", 1), shift(four, "context", 1)]

    def part(terms, start, stop):
        return add_up(*[t[start:stop] for t in terms]).astype(BF16)

    def home_first(outs, *others):
        terms = [after(outs[0], *others), shift(outs[1], "context", 1)]
        rows = outs[0].shape[0]
        return terms, part(terms, rows // 2, rows)

    def home_second(terms, far):
        terms = terms + [far]
        rows = far.shape[0]
        return terms, part(terms, rows // 2, rows)

    def home_third(terms, far):
        return part(terms + [far], 0, far.shape[0])

    early_came = send_rows(early, line)
    early_own = jnp.concatenate(early_came, axis=0)
    late_came = send_rows(after(late, early_own), line)
    early_near = cross(early_own, 0)
    early_two = jnp.concatenate([early_own, early_near], axis=0)
    early_four = cross(early_two, 1)
    late_came[0] = after(late_came[0], early_near)
    late_own = jnp.concatenate(late_came, axis=0)
    late_near = cross(late_own, 0)
    sizes = (4 * early_own.shape[0],) * 2
    early_rows = after(pieces(early_two, early_four), late_own)
    early_first = gate_up(early_rows, w_gate, w_up, 0, most)

    late_two = jnp.concatenate([after(late_own, early_first), late_near], axis=0)
    late_four = cross(late_two, 1)
    early_rows = after(early_rows, late_two)
    early_out = finish(early_rows, early_first, sizes, w_gate, w_up, w_down, 0, width)[1]
    late_four = after(late_four, early_out)
    early_kept, early_go = home_first(early_out, late_four)
    early_far = cross(early_go, 1)
    sizes = (4 * late_own.shape[0],) * 2
    late_rows = after(pieces(late_two, late_four), early_go)
    late_first = gate_up(late_rows, w_gate, w_up, 0, hidden // 2)
    early_kept, early_go = home_second(after(early_kept, late_first), early_far)
    early_far = cross(early_go, 0)
    late_rows = after(late_rows, early_go)
    late_hidden, out_left = finish(late_rows, late_first, sizes, w_gate, w_up, w_down, 0, half)
    early_result = home_third(after(early_kept, out_left[0]), early_far)
    left = home_first(after(out_left, early_result))
    left_far = cross(left[1], 1)
    out_right = down([after(late_hidden, left[1])], sizes, w_down, half, half)
    left = home_second(after(left[0], out_right), left_far)
    left_far = cross(left[1], 0)
    right = home_first(after(out_right, left[1]))
    right_far = cross(right[1], 1)
    left_result = home_third(after(left[0], right[1]), left_far)
    right = home_second(after(right[0], left_result), right_far)
    right_far = cross(right[1], 0)
    few, many = early_result.shape[0] // line, left_result.shape[0] // line
    packed = []
    for s in range(line):
        mine = early_result[few * s : few * (s + 1)]
        packed += [mine[:, :half], mine[:, half:], left_result[many * s : many * (s + 1)]]
    left_came = send_rows(jnp.concatenate(packed, axis=0), line, -1)
    right_result = home_third(right[0], right_far)
    right_came = send_rows(right_result, line, -1)
    left_came = after(left_came, right_result)
    left_rows = [c[:few] for c in left_came] + [c[2 * few :] for c in left_came]
    right_rows = [c[few : 2 * few] for c in left_came] + right_came
    return [jnp.concatenate(rows, axis=0) for rows in (left_rows, right_rows)]


def on_device(
    residual,
    x_raw,
    z_gate,
    conv_w,
    conv_b,
    xproj_w,
    dtproj_w,
    dt_bias,
    a_rate,
    skip_gain,
    out_w,
    norm_gain,
    route_ids,
    route_w,
    w_gate,
    w_up,
    w_down,
):
    owners, contexts, dps = (lax.axis_size(a) for a in ("expert", "context", "dp"))
    me = lax.axis_index("expert")
    place, half = me // 2, me % 2
    line = owners // 2
    length, channels = x_raw.shape[2:]
    width = residual.shape[3]
    row_count = residual.shape[2]

    values = x_raw[0, 0]
    prior_rim = from_behind(values[length - (CONV - 1) :], "context", 1)
    padded = jnp.concatenate([prior_rim, values], axis=0).astype(F32)
    conv_sum = conv_b[None, :] + sum(
        (
            conv_w[lag_index][None, :] * padded[lag_index : lag_index + length]
            for lag_index in range(CONV)
        )
    )
    mixed_in = jax.nn.silu(conv_sum).astype(BF16)
    projected = jnp.dot(mixed_in, xproj_w, preferred_element_type=F32).astype(BF16)
    shares = projected.reshape(line, length // line, -1)

    def share_of(s):
        return lax.dynamic_index_in_dim(shares, (place + s) % line, 0, keepdims=False)

    share = add_up(share_of(0), *[along_line(share_of(s), s) for s in range(1, line)]).astype(BF16)
    share = add_up(share, swap_pair(share)).astype(BF16)
    pieces = [share] + [along_line(share, s) for s in range(1, line)]

    neg = -a_rate.reshape(NSTATE, channels // LANES, LANES)
    neg = jnp.pad(neg, ((0, 0), (0, SUB - channels // LANES), (0, 0)))
    where = jnp.stack([place, half]).astype(jnp.int32)
    y, total, end, bc = run_scan(where, pieces, dtproj_w, dt_bias[None, :], neg, mixed_in)
    enter = from_behind(end, "context", 1)
    for step in range(contexts - 2):
        decay = jnp.exp(total[-SUB:][None] * neg)
        enter = from_behind(end + decay * enter, "context", 1)
    kept, sent, blocks = run_out(
        where, line, y, total, enter, bc, neg, mixed_in, z_gate[0, 0], skip_gain[None, :], out_w
    )
    got = swap_pair(sent)
    over_z = add_up(blocks[0], *[along_line(blocks[s], s) for s in range(1, line)])
    both = add_up(kept, got).astype(BF16).reshape(line, row_count, -1)
    other = swap_pair(over_z[row_count:].astype(BF16))
    sums = [
        add_up(both[0], *[along_line(both[s], s) for s in range(1, line)]),
        add_up(over_z[:row_count], other),
    ]
    mixer_out = jnp.concatenate(sums, axis=1)

    stream_f = (residual[0, 0].astype(F32) + mixer_out).astype(BF16).astype(F32)
    normed = (
        stream_f
        * lax.rsqrt(jnp.mean(stream_f * stream_f, axis=1, keepdims=True) + 1e-05)
        * norm_gain[None, :]
    ).astype(BF16)
    ids, weights = route_ids[0, 0], route_w[0, 0]
    capacity = min(row_count, 8 * ((3 * row_count * TOP + 16 * line - 1) // (16 * line)))
    cuts = (0, 8, capacity) if contexts == 2 and dps == 2 and capacity > 8 else (0, capacity)
    named = jnp.any(ids[:, :, None] == jnp.arange(line, dtype=jnp.int32), axis=1)
    rank = jnp.cumsum(named.astype(jnp.int32), axis=0) - 1
    chosen = ids[:, :, None] == jnp.arange(line, dtype=jnp.int32)
    rank_of = jnp.sum(jnp.where(chosen, rank[:, None, :], 0), axis=2)
    away = (ids - place + line) % line
    placing, weighting, packed = [], [], []
    for low, high in zip(cuts[:-1], cuts[1:]):
        inside = (rank_of >= low) & (rank_of < high)
        slot_of = jnp.where(inside, away * (high - low) + rank_of - low, -1)
        hits = slot_of[:, :, None] == jnp.arange(line * (high - low), dtype=jnp.int32)
        placing = jnp.any(hits, axis=1).astype(BF16)
        weighting.append(jnp.sum(jnp.where(hits, weights[:, :, None], 0.0), axis=1))
        rows = lax.dot_general(
            placing, normed, (((0,), (0,)), ((), ())), preferred_element_type=F32
        )
        packed.append(rows.astype(BF16))
    if len(packed) == 2:
        back = square_experts(*packed, line, w_gate[0], w_up[0], w_down[0])
    else:
        back = [plain_experts(packed[0], line, w_gate[0], w_up[0], w_down[0])]
    weighting = jnp.concatenate(weighting, axis=1)
    expert_sum = jnp.concatenate(
        [
            jnp.dot(
                weighting,
                rows.astype(F32),
                precision=lax.Precision.HIGHEST,
                preferred_element_type=F32,
            )
            for rows in back
        ],
        axis=1,
    )
    mixed = (stream_f + expert_sum).astype(BF16)
    return mixed.reshape(1, 1, row_count, width)


def solution(mesh):
    placed = (
        P("dp", "context", "expert", None),
        P("dp", "context", None, "expert"),
        P("dp", "context", None, "expert"),
        P(None, "expert"),
        P("expert"),
        P("expert", None),
        P(None, "expert"),
        P("expert"),
        P(None, "expert"),
        P("expert"),
        P("expert", None),
        P(),
        P("dp", "context", "expert", None),
        P("dp", "context", "expert", None),
        P("expert", None, ("context", "dp")),
        P("expert", None, ("context", "dp")),
        P("expert", ("context", "dp"), None),
    )
    return jax.shard_map(
        on_device,
        mesh=mesh,
        in_specs=placed,
        out_specs=P("dp", "context", "expert", None),
        check_vma=False,
    )
```

```python
import functools

import jax
import jax.numpy as jnp
from jax import lax
from jax.experimental import pallas as pl
from jax.experimental.pallas import tpu as pltpu
from jax.sharding import PartitionSpec as P

NSTATE = 16
DT_RANK = 256
CONV = 4
TOP = 2
LANES = 128
SUB = 8
F32 = jnp.float32
BF16 = jnp.bfloat16
MIB = 1 << 20


def from_behind(block, axis, distance):
    devices = range(lax.axis_size(axis))
    route = [(i - distance, i) for i in devices if i - distance in devices]
    return lax.ppermute(block, axis, route)


def shift(block, axis, distance):
    size = lax.axis_size(axis)
    return lax.ppermute(block, axis, [(i, (i + distance) % size) for i in range(size)])


def swap_pair(block):
    size = lax.axis_size("expert")
    return lax.ppermute(block, "expert", [(i, i ^ 1) for i in range(size)])


def cost(flops, bytes_accessed, transcendentals=0):
    return pl.CostEstimate(
        flops=int(flops), bytes_accessed=int(bytes_accessed), transcendentals=int(transcendentals)
    )


def spread_rows(values, wide_ref):
    length, count = values.shape
    col = lax.broadcasted_iota(jnp.int32, (count, count * LANES), 1)
    row = lax.broadcasted_iota(jnp.int32, (count, count * LANES), 0)
    ones = jnp.where((col >= row * LANES) & (col < (row + 1) * LANES), 1.0, 0.0).astype(BF16)
    out = jnp.dot(values, ones, preferred_element_type=F32)
    for n in range(count):
        wide_ref[pl.ds(n * length, length), :] = out[:, n * LANES : (n + 1) * LANES]


def scan_kernel(groups, line, place_ref, *refs):
    pieces, refs = refs[:line], refs[line:]
    w_ref, bias_ref, rate_ref, x_ref, y_ref, sum_ref, end_ref, bc_ref, neg_ref = refs[:9]
    low_ref, step_ref, drive_ref, wide_ref = refs[9:]
    length = x_ref.shape[0]
    share = length // line
    for s in range(line):
        start = pl.multiple_of((place_ref[0] + (line - s)) % line * share, share)
        low_ref[pl.ds(start, share), :] = pieces[s][:, :DT_RANK]
        bc_ref[pl.ds(start, share), :] = pieces[s][:, DT_RANK:]
    spread_rows(bc_ref[...], wide_ref)
    for g in range(SUB):
        rows = pl.ds(g, length, stride=SUB)
        if g >= groups:
            step_ref[rows, :] = jnp.zeros((length, LANES), F32)
            drive_ref[rows, :] = jnp.zeros((length, LANES), F32)
            neg_ref[pl.ds(g, NSTATE, stride=SUB), :] = jnp.zeros((NSTATE, LANES), F32)
            continue
        cols = pl.ds(g * LANES, LANES)
        neg_ref[pl.ds(g, NSTATE, stride=SUB), :] = -rate_ref[:, cols]
        raw = jnp.dot(low_ref[...], w_ref[:, cols], preferred_element_type=F32) + bias_ref[:, cols]
        step = jnp.maximum(raw, 0.0) + jnp.log1p(jnp.exp(-jnp.abs(raw)))
        step_ref[rows, :] = step
        drive_ref[rows, :] = step * x_ref[:, cols].astype(F32)

    def block(k, carry):
        states, total = list(carry[0]), carry[1]
        for u in range(SUB):
            t = k * SUB + u
            here = pl.ds(pl.multiple_of(t * SUB, SUB), SUB)
            step, drive = step_ref[here, :], drive_ref[here, :]
            total = total + step
            out = jnp.zeros((SUB, LANES), F32)
            for n in range(NSTATE):
                decay = jnp.exp(step * neg_ref[pl.ds(n * SUB, SUB), :])
                b = wide_ref[pl.ds(n * length + t, 1), :]
                c = wide_ref[pl.ds((NSTATE + n) * length + t, 1), :]
                states[n] = states[n] * decay + drive * b
                out = out + states[n] * c
            y_ref[here, :] = out
            sum_ref[here, :] = total
        return tuple(states), total

    zero = jnp.zeros((SUB, LANES), F32)
    states, total = lax.fori_loop(0, length // SUB, block, ((zero,) * NSTATE, zero))
    for n in range(NSTATE):
        end_ref[n] = states[n]


def run_scan(place, pieces, w, bias, rate, x):
    length, channels = x.shape
    vmem = pl.BlockSpec(memory_space=pltpu.VMEM)
    tall = jax.ShapeDtypeStruct((length * SUB, LANES), F32)
    return pl.pallas_call(
        functools.partial(scan_kernel, channels // LANES, len(pieces)),
        out_shape=(
            tall,
            tall,
            jax.ShapeDtypeStruct((NSTATE, SUB, LANES), F32),
            jax.ShapeDtypeStruct((length, 2 * NSTATE), BF16),
            jax.ShapeDtypeStruct((NSTATE * SUB, LANES), F32),
        ),
        in_specs=[pl.BlockSpec(memory_space=pltpu.SMEM)] + [vmem] * (len(pieces) + 4),
        out_specs=(vmem,) * 5,
        scratch_shapes=[
            pltpu.VMEM((length, DT_RANK), BF16),
            pltpu.VMEM((length * SUB, LANES), F32),
            pltpu.VMEM((length * SUB, LANES), F32),
            pltpu.VMEM((2 * NSTATE * length, LANES), F32),
        ],
        compiler_params=pltpu.CompilerParams(vmem_limit_bytes=20 * MIB),
        cost_estimate=cost(2e8, 4 * MIB, NSTATE * length * channels),
        name="state_scan",
    )(place, *pieces, w, bias, rate, x)


def out_kernel(groups, line, first, at_ref, y_ref, sum_ref, enter_ref, bc_ref, neg_ref, x_ref, z_ref,
               skip_ref, w_hbm, *refs):
    kept_ref, sent_ref, blocks_ref, full_ref, wide_ref, gated_ref, order_ref, w_ref, sems = refs
    length = x_ref.shape[0]
    tiles, _, tile = w_ref.shape

    def fetch(j):
        cols = pl.ds(pl.multiple_of(j * tile, tile), tile)
        return pltpu.make_async_copy(w_hbm.at[:, cols], w_ref.at[j], sems.at[j])

    for j in range(tiles):
        fetch(j).start()
    spread_rows(bc_ref[:, NSTATE:], wide_ref)

    def block(k, carry):
        for u in range(SUB):
            t = k * SUB + u
            here = pl.ds(pl.multiple_of(t * SUB, SUB), SUB)
            total = sum_ref[here, :]
            out = y_ref[here, :]
            for n in range(NSTATE):
                c = wide_ref[pl.ds(n * length + t, 1), :]
                out = out + jnp.exp(total * neg_ref[pl.ds(n * SUB, SUB), :]) * enter_ref[n] * c
            full_ref[here, :] = out
        return carry

    lax.fori_loop(0, length // SUB, block, 0)
    for g in range(groups):
        cols = pl.ds(g * LANES, LANES)
        mixed_in = x_ref[:, cols].astype(F32)
        read = full_ref[pl.ds(g, length, stride=SUB), :] + skip_ref[:, cols] * mixed_in
        z = z_ref[:, cols].astype(F32)
        gated_ref[:, cols] = (read * (z / (1.0 + jnp.exp(-z)))).astype(BF16)
    place, half = at_ref[0], at_ref[1]
    count = length // 2
    piece = count // line
    for k in range(line):
        for r in range(2):
            source = pl.multiple_of((2 * ((place + k) % line) + (half ^ r)) * piece, piece)
            order_ref[pl.ds(r * count + k * piece, piece), :] = gated_ref[pl.ds(source, piece), :]
    def project(j):
        fetch(j).wait()
        return jnp.dot(order_ref[...], w_ref[j], preferred_element_type=F32).astype(BF16)

    def step(j, carry):
        cols = pl.ds(pl.multiple_of(j * tile, tile), tile)
        out = project(j)
        kept_ref[:, cols] = out[:count]
        sent_ref[:, cols] = out[count:]
        return carry

    def block_step(j, carry):
        cols = pl.ds(pl.multiple_of((j - first) * tile, tile), tile)
        out = project(j)
        for k in range(line):
            for r in range(2):
                start = r * count + k * piece
                blocks_ref[k, pl.ds(r * piece, piece), cols] = out[start : start + piece]
        return carry

    lax.fori_loop(0, first, step, 0)
    lax.fori_loop(first, tiles, block_step, 0)


def run_out(at, line, y, total, enter, bc, neg, x, z, skip, w):
    length, channels = x.shape
    wide = w.shape[1]
    tile = min(512, wide)
    first = (wide // tile * 5 + 4) // 8
    vmem = pl.BlockSpec(memory_space=pltpu.VMEM)
    part = jax.ShapeDtypeStruct((length // 2, first * tile), BF16)
    blocks = jax.ShapeDtypeStruct((line, length // line, wide - first * tile), BF16)
    return pl.pallas_call(
        functools.partial(out_kernel, channels // LANES, line, first),
        out_shape=(part, part, blocks),
        in_specs=[pl.BlockSpec(memory_space=pltpu.SMEM)] + [vmem] * 8 + [pl.BlockSpec(memory_space=pl.ANY)],
        out_specs=(vmem,) * 3,
        scratch_shapes=[
            pltpu.VMEM((length * SUB, LANES), F32),
            pltpu.VMEM((NSTATE * length, LANES), F32),
            pltpu.VMEM((length, channels), BF16),
            pltpu.VMEM((length, channels), BF16),
            pltpu.VMEM((wide // tile, channels, tile), BF16),
            pltpu.SemaphoreType.DMA((wide // tile,)),
        ],
        compiler_params=pltpu.CompilerParams(vmem_limit_bytes=48 * MIB),
        cost_estimate=cost(
            2 * length * channels * wide, 2 * channels * wide + 8 * MIB, NSTATE * length * channels
        ),
        name="readout_project",
    )(at, y, total, enter, bc, neg, x, z, skip, w)


def gate_up_kernel(count, first, *refs):
    pieces, (gate_hbm, up_hbm, out_ref, rows_ref, gate_ref, up_ref, sems) = refs[:count], refs[count:]
    copies, at = [], 0
    for k, piece in enumerate(pieces):
        rows = pl.ds(at, piece.shape[0])
        copies.append(pltpu.make_async_copy(piece, rows_ref.at[rows, :], sems.at[k]))
        at += piece.shape[0]
    steps, tile = gate_ref.shape[0], gate_ref.shape[2]

    def fetch(j, k):
        cols = pl.ds(pl.multiple_of(first + j * tile, tile), tile)
        source, target = ((gate_hbm, gate_ref), (up_hbm, up_ref))[k]
        return pltpu.make_async_copy(source.at[:, cols], target.at[j], sems.at[count + 2 * j + k])

    for copy in copies:
        copy.start()
    for j in range(steps):
        fetch(j, 0).start()
        fetch(j, 1).start()
    for copy in copies:
        copy.wait()

    def step(j, carry):
        fetch(j, 0).wait()
        fetch(j, 1).wait()
        gate = jnp.dot(rows_ref[...], gate_ref[j], preferred_element_type=F32)
        up = jnp.dot(rows_ref[...], up_ref[j], preferred_element_type=F32)
        cols = pl.ds(pl.multiple_of(j * tile, tile), tile)
        out_ref[:, cols] = (gate / (1.0 + jnp.exp(-gate)) * up).astype(BF16)
        return carry

    lax.fori_loop(0, steps, step, 0)


def gate_up(pieces, w_gate, w_up, first, width):
    depth = w_gate.shape[0]
    rows = sum(p.shape[0] for p in pieces)
    tile = min(256, width)
    steps = width // tile
    anywhere = pl.BlockSpec(memory_space=pl.ANY)
    return pl.pallas_call(
        functools.partial(gate_up_kernel, len(pieces), first),
        out_shape=jax.ShapeDtypeStruct((rows, width), BF16),
        in_specs=[anywhere] * (len(pieces) + 2),
        out_specs=pl.BlockSpec(memory_space=pltpu.VMEM),
        scratch_shapes=[
            pltpu.VMEM((rows, depth), BF16),
            pltpu.VMEM((steps, depth, tile), BF16),
            pltpu.VMEM((steps, depth, tile), BF16),
            pltpu.SemaphoreType.DMA((len(pieces) + 2 * steps,)),
        ],
        compiler_params=pltpu.CompilerParams(vmem_limit_bytes=49 * MIB),
        cost_estimate=cost(4 * rows * depth * width, 4 * depth * width + 2 * rows * depth),
        name="gate_up",
    )(*pieces, w_gate, w_up)


def finish_kernel(count, first, *refs):
    pieces, (have_ref, gate_hbm, up_hbm, down_hbm) = refs[:count], refs[count : count + 4]
    hidden_ref, outs = refs[count + 4], refs[count + 5 : -5]
    rows_ref, gate_ref, up_ref, down_ref, sems = refs[-5:]
    done = have_ref.shape[1]
    steps, tile = gate_ref.shape[0], gate_ref.shape[2]
    last_steps, last_tile = down_ref.shape[0], down_ref.shape[2]

    def fetch(j, k):
        cols = pl.ds(pl.multiple_of(done + j * tile, tile), tile)
        source, target = ((gate_hbm, gate_ref), (up_hbm, up_ref))[k]
        return pltpu.make_async_copy(source.at[:, cols], target.at[j], sems.at[count + 2 * j + k])

    def last_fetch(j):
        cols = pl.ds(pl.multiple_of(first + j * last_tile, last_tile), last_tile)
        sem = sems.at[count + 2 * steps + j]
        return pltpu.make_async_copy(down_hbm.at[:, cols], down_ref.at[j], sem)

    copies, at = [], 0
    for k, piece in enumerate(pieces):
        rows = pl.ds(at, piece.shape[0])
        copies.append(pltpu.make_async_copy(piece, rows_ref.at[rows, :], sems.at[k]))
        at += piece.shape[0]
    for copy in copies:
        copy.start()
    for j in range(steps):
        fetch(j, 0).start()
        fetch(j, 1).start()
    for j in range(last_steps):
        last_fetch(j).start()
    hidden_ref[:, pl.ds(0, done)] = have_ref[...]
    for copy in copies:
        copy.wait()

    def step(j, carry):
        fetch(j, 0).wait()
        fetch(j, 1).wait()
        gate = jnp.dot(rows_ref[...], gate_ref[j], preferred_element_type=F32)
        up = jnp.dot(rows_ref[...], up_ref[j], preferred_element_type=F32)
        cols = pl.ds(pl.multiple_of(done + j * tile, tile), tile)
        hidden_ref[:, cols] = (gate / (1.0 + jnp.exp(-gate)) * up).astype(BF16)
        return carry

    def last_step(j, carry):
        last_fetch(j).wait()
        out = jnp.dot(hidden_ref[...], down_ref[j], preferred_element_type=F32).astype(BF16)
        cols = pl.ds(pl.multiple_of(j * last_tile, last_tile), last_tile)
        start = 0
        for ref in outs:
            ref[:, cols] = out[start : start + ref.shape[0]]
            start += ref.shape[0]
        return carry

    lax.fori_loop(0, steps, step, 0)
    lax.fori_loop(0, last_steps, last_step, 0)


def finish(pieces, have, sizes, w_gate, w_up, w_down, first, width):
    depth, hidden = w_gate.shape
    rows, done = have.shape
    tile, last_tile = min(256, hidden - done), min(512, width)
    steps, last_steps = (hidden - done) // tile, width // last_tile
    vmem, anywhere = pl.BlockSpec(memory_space=pltpu.VMEM), pl.BlockSpec(memory_space=pl.ANY)
    shapes = [(rows, hidden)] + [(n, width) for n in sizes]
    hidden_out, *outs = pl.pallas_call(
        functools.partial(finish_kernel, len(pieces), first),
        out_shape=tuple(jax.ShapeDtypeStruct(shape, BF16) for shape in shapes),
        in_specs=[anywhere] * len(pieces) + [vmem] + [anywhere] * 3,
        out_specs=(vmem,) * len(shapes),
        scratch_shapes=[
            pltpu.VMEM((rows, depth), BF16),
            pltpu.VMEM((steps, depth, tile), BF16),
            pltpu.VMEM((steps, depth, tile), BF16),
            pltpu.VMEM((last_steps, hidden, last_tile), BF16),
            pltpu.SemaphoreType.DMA((len(pieces) + 2 * steps + last_steps,)),
        ],
        compiler_params=pltpu.CompilerParams(vmem_limit_bytes=49 * MIB),
        cost_estimate=cost(
            4 * rows * depth * (hidden - done) + 2 * rows * hidden * width,
            4 * depth * (hidden - done) + 2 * hidden * width + 2 * rows * (depth + width),
        ),
        name="gate_up_down",
    )(*pieces, have, w_gate, w_up, w_down)
    return hidden_out, outs


def down_kernel(count, first, *refs):
    pieces, w_hbm, outs = refs[:count], refs[count], refs[count + 1 : -3]
    rows_ref, w_ref, sems = refs[-3:]
    tiles, _, tile = w_ref.shape

    def fetch(j):
        source = pl.ds(pl.multiple_of(first + j * tile, tile), tile)
        return pltpu.make_async_copy(w_hbm.at[:, source], w_ref.at[j], sems.at[j])

    for j in range(tiles):
        fetch(j).start()
    at = 0
    for piece in pieces:
        rows_ref[:, pl.ds(at, piece.shape[1])] = piece[...]
        at += piece.shape[1]

    def step(j, carry):
        fetch(j).wait()
        out = jnp.dot(rows_ref[...], w_ref[j], preferred_element_type=F32).astype(BF16)
        cols = pl.ds(pl.multiple_of(j * tile, tile), tile)
        start = 0
        for ref in outs:
            ref[:, cols] = out[start : start + ref.shape[0]]
            start += ref.shape[0]
        return carry

    lax.fori_loop(0, tiles, step, 0)


def down(pieces, sizes, w_down, first, width):
    hidden, rows = w_down.shape[0], pieces[0].shape[0]
    tile = min(512, width)
    vmem = pl.BlockSpec(memory_space=pltpu.VMEM)
    return pl.pallas_call(
        functools.partial(down_kernel, len(pieces), first),
        out_shape=tuple(jax.ShapeDtypeStruct((n, width), BF16) for n in sizes),
        in_specs=[vmem] * len(pieces) + [pl.BlockSpec(memory_space=pl.ANY)],
        out_specs=(vmem,) * len(sizes),
        scratch_shapes=[
            pltpu.VMEM((rows, hidden), BF16),
            pltpu.VMEM((width // tile, hidden, tile), BF16),
            pltpu.SemaphoreType.DMA((width // tile,)),
        ],
        compiler_params=pltpu.CompilerParams(vmem_limit_bytes=49 * MIB),
        cost_estimate=cost(2 * rows * hidden * width, 2 * hidden * width + 2 * rows * (hidden + width)),
        name="down",
    )(*pieces, w_down)


def add_up(*parts):
    return sum(p.astype(F32) for p in parts)


def along_line(block, distance):
    size = lax.axis_size("expert")
    return lax.ppermute(block, "expert", [(e, (e + 2 * distance) % size) for e in range(size)])


def cross(block, turn):
    owners, dps = lax.axis_size("expert"), lax.axis_size("dp")
    route = []
    for e in range(owners):
        for core in range(2):
            for d in range(dps):
                to = (e ^ 1, core, d) if core == turn else (e, core, d ^ 1)
                route.append(((e * 2 + core) * dps + d, (to[0] * 2 + core) * dps + to[2]))
    return lax.ppermute(block, ("expert", "context", "dp"), route)


def after(blocks, *others):
    return lax.optimization_barrier((blocks, others))[0]


def send_rows(packed, line, way=1):
    size = packed.shape[0] // line
    parts = [packed[size * s : size * (s + 1)] for s in range(line)]
    return [parts[0]] + [along_line(parts[s], way * s) for s in range(1, line)]


def plain_experts(packed, line, w_gate, w_up, w_down):
    own = jnp.concatenate(send_rows(packed, line), axis=0)
    rows = jnp.concatenate([own, swap_pair(own)], axis=0)
    rows = lax.all_gather(rows, ("context", "dp"), axis=0, tiled=True)
    hidden = gate_up([rows], w_gate, w_up, 0, w_gate.shape[1])
    out = down([hidden], (rows.shape[0],), w_down, 0, w_down.shape[1])[0]
    mine = lax.psum_scatter(out, ("context", "dp"), scatter_dimension=0, tiled=True)
    count = own.shape[0]
    result = add_up(mine[:count], swap_pair(mine[count:])).astype(BF16)
    return jnp.concatenate(send_rows(result, line, -1), axis=0)


def square_experts(early, late, line, w_gate, w_up, w_down):
    width = w_down.shape[1]
    half = width // 2
    hidden = w_down.shape[0]
    most = hidden // 2

    def pieces(two, four):
        return [two, four, shift(two, "context", 1), shift(four, "context", 1)]

    def part(terms, start, stop):
        return add_up(*[t[start:stop] for t in terms]).astype(BF16)

    def home_first(outs, *others):
        terms = [after(outs[0], *others), shift(outs[1], "context", 1)]
        rows = outs[0].shape[0]
        return terms, part(terms, rows // 2, rows)

    def home_second(terms, far):
        terms = terms + [far]
        rows = far.shape[0]
        return terms, part(terms, rows // 2, rows)

    def home_third(terms, far):
        return part(terms + [far], 0, far.shape[0])

    early_came = send_rows(early, line)
    early_own = jnp.concatenate(early_came, axis=0)
    late_came = send_rows(after(late, early_own), line)
    early_near = cross(early_own, 0)
    early_two = jnp.concatenate([early_own, early_near], axis=0)
    early_four = cross(early_two, 1)
    late_came[0] = after(late_came[0], early_near)
    late_own = jnp.concatenate(late_came, axis=0)
    late_near = cross(late_own, 0)
    sizes = (4 * early_own.shape[0],) * 2
    early_rows = after(pieces(early_two, early_four), late_own)
    early_first = gate_up(early_rows, w_gate, w_up, 0, most)

    late_two = jnp.concatenate([after(late_own, early_first), late_near], axis=0)
    late_four = cross(late_two, 1)
    early_rows = after(early_rows, late_two)
    early_out = finish(early_rows, early_first, sizes, w_gate, w_up, w_down, 0, width)[1]
    late_four = after(late_four, early_out)
    early_kept, early_go = home_first(early_out, late_four)
    early_far = cross(early_go, 1)
    sizes = (4 * late_own.shape[0],) * 2
    late_rows = after(pieces(late_two, late_four), early_go)
    late_first = gate_up(late_rows, w_gate, w_up, 0, hidden // 2)
    early_kept, early_go = home_second(after(early_kept, late_first), early_far)
    early_far = cross(early_go, 0)
    late_rows = after(late_rows, early_go)
    late_hidden, out_left = finish(late_rows, late_first, sizes, w_gate, w_up, w_down, 0, half)
    early_result = home_third(after(early_kept, out_left[0]), early_far)
    left = home_first(after(out_left, early_result))
    left_far = cross(left[1], 1)
    out_right = down([after(late_hidden, left[1])], sizes, w_down, half, half)
    left = home_second(after(left[0], out_right), left_far)
    left_far = cross(left[1], 0)
    right = home_first(after(out_right, left[1]))
    right_far = cross(right[1], 1)
    left_result = home_third(after(left[0], right[1]), left_far)
    right = home_second(after(right[0], left_result), right_far)
    right_far = cross(right[1], 0)
    few, many = early_result.shape[0] // line, left_result.shape[0] // line
    packed = []
    for s in range(line):
        mine = early_result[few * s : few * (s + 1)]
        packed += [mine[:, :half], mine[:, half:], left_result[many * s : many * (s + 1)]]
    left_came = send_rows(jnp.concatenate(packed, axis=0), line, -1)
    right_result = home_third(right[0], right_far)
    right_came = send_rows(right_result, line, -1)
    left_came = after(left_came, right_result)
    left_rows = [c[:few] for c in left_came] + [c[2 * few :] for c in left_came]
    right_rows = [c[few : 2 * few] for c in left_came] + right_came
    return [jnp.concatenate(rows, axis=0) for rows in (left_rows, right_rows)]


def on_device(
    residual,
    x_raw,
    z_gate,
    conv_w,
    conv_b,
    xproj_w,
    dtproj_w,
    dt_bias,
    a_rate,
    skip_gain,
    out_w,
    norm_gain,
    route_ids,
    route_w,
    w_gate,
    w_up,
    w_down,
):
    owners, contexts, dps = (lax.axis_size(a) for a in ("expert", "context", "dp"))
    me = lax.axis_index("expert")
    place, half = me // 2, me % 2
    line = owners // 2
    length, channels = x_raw.shape[2:]
    width = residual.shape[3]
    row_count = residual.shape[2]

    values = x_raw[0, 0]
    prior_rim = from_behind(values[length - (CONV - 1) :], "context", 1)
    padded = jnp.concatenate([prior_rim, values], axis=0).astype(F32)
    conv_sum = conv_b[None, :] + sum(
        (
            conv_w[lag_index][None, :] * padded[lag_index : lag_index + length]
            for lag_index in range(CONV)
        )
    )
    mixed_in = jax.nn.silu(conv_sum).astype(BF16)
    projected = jnp.dot(mixed_in, xproj_w, preferred_element_type=F32).astype(BF16)
    shares = projected.reshape(line, length // line, -1)

    def share_of(s):
        return lax.dynamic_index_in_dim(shares, (place + s) % line, 0, keepdims=False)

    share = add_up(share_of(0), *[along_line(share_of(s), s) for s in range(1, line)]).astype(BF16)
    share = add_up(share, swap_pair(share)).astype(BF16)
    pieces = [share] + [along_line(share, s) for s in range(1, line)]

    where = jnp.stack([place, half]).astype(jnp.int32)
    y, total, end, bc, neg = run_scan(
        where, pieces, dtproj_w, dt_bias[None, :], a_rate, mixed_in
    )
    enter = from_behind(end, "context", 1)
    for step in range(contexts - 2):
        decay = jnp.exp(total[-SUB:][None] * neg.reshape(end.shape))
        enter = from_behind(end + decay * enter, "context", 1)
    kept, sent, blocks = run_out(
        where, line, y, total, enter, bc, neg, mixed_in, z_gate[0, 0], skip_gain[None, :], out_w
    )
    got = swap_pair(sent)
    over_z = add_up(blocks[0], *[along_line(blocks[s], s) for s in range(1, line)])
    both = add_up(kept, got).astype(BF16).reshape(line, row_count, -1)
    other = swap_pair(over_z[row_count:].astype(BF16))
    sums = [
        add_up(both[0], *[along_line(both[s], s) for s in range(1, line)]),
        add_up(over_z[:row_count], other),
    ]
    mixer_out = jnp.concatenate(sums, axis=1)

    stream_f = (residual[0, 0].astype(F32) + mixer_out).astype(BF16).astype(F32)
    normed = (
        stream_f
        * lax.rsqrt(jnp.mean(stream_f * stream_f, axis=1, keepdims=True) + 1e-05)
        * norm_gain[None, :]
    ).astype(BF16)
    ids, weights = after((route_ids[0, 0], route_w[0, 0]), kept)
    capacity = min(row_count, 8 * ((3 * row_count * TOP + 16 * line - 1) // (16 * line)))
    cuts = (0, 8, capacity) if contexts == 2 and dps == 2 and capacity > 8 else (0, capacity)
    named = jnp.any(ids[:, :, None] == jnp.arange(line, dtype=jnp.int32), axis=1)
    rank = jnp.cumsum(named.astype(jnp.int32), axis=0) - 1
    chosen = ids[:, :, None] == jnp.arange(line, dtype=jnp.int32)
    rank_of = jnp.sum(jnp.where(chosen, rank[:, None, :], 0), axis=2)
    away = (ids - place + line) % line
    placing, weighting, packed = [], [], []
    for low, high in zip(cuts[:-1], cuts[1:]):
        inside = (rank_of >= low) & (rank_of < high)
        slot_of = jnp.where(inside, away * (high - low) + rank_of - low, -1)
        hits = slot_of[:, :, None] == jnp.arange(line * (high - low), dtype=jnp.int32)
        placing = jnp.any(hits, axis=1).astype(BF16)
        weighting.append(jnp.sum(jnp.where(hits, weights[:, :, None], 0.0), axis=1))
        rows = lax.dot_general(
            placing, normed, (((0,), (0,)), ((), ())), preferred_element_type=F32
        )
        packed.append(rows.astype(BF16))
    if len(packed) == 2:
        back = square_experts(*packed, line, w_gate[0], w_up[0], w_down[0])
    else:
        back = [plain_experts(packed[0], line, w_gate[0], w_up[0], w_down[0])]
    weighting = jnp.concatenate(weighting, axis=1)
    expert_sum = jnp.concatenate(
        [
            jnp.dot(
                weighting,
                rows.astype(F32),
                precision=lax.Precision.HIGHEST,
                preferred_element_type=F32,
            )
            for rows in back
        ],
        axis=1,
    )
    mixed = (stream_f + expert_sum).astype(BF16)
    return mixed.reshape(1, 1, row_count, width)


def solution(mesh):
    placed = (
        P("dp", "context", "expert", None),
        P("dp", "context", None, "expert"),
        P("dp", "context", None, "expert"),
        P(None, "expert"),
        P("expert"),
        P("expert", None),
        P(None, "expert"),
        P("expert"),
        P(None, "expert"),
        P("expert"),
        P("expert", None),
        P(),
        P("dp", "context", "expert", None),
        P("dp", "context", "expert", None),
        P("expert", None, ("context", "dp")),
        P("expert", None, ("context", "dp")),
        P("expert", ("context", "dp"), None),
    )
    return jax.shard_map(
        on_device,
        mesh=mesh,
        in_specs=placed,
        out_specs=P("dp", "context", "expert", None),
        check_vma=False,
    )
```

```python
import functools

import jax
import jax.numpy as jnp
from jax import lax
from jax.experimental import pallas as pl
from jax.experimental.pallas import tpu as pltpu
from jax.sharding import PartitionSpec as P

NSTATE = 16
DT_RANK = 256
CONV = 4
TOP = 2
LANES = 128
SUB = 8
F32 = jnp.float32
BF16 = jnp.bfloat16
MIB = 1 << 20


def from_behind(block, axis, distance):
    devices = range(lax.axis_size(axis))
    route = [(i - distance, i) for i in devices if i - distance in devices]
    return lax.ppermute(block, axis, route)


def shift(block, axis, distance):
    size = lax.axis_size(axis)
    return lax.ppermute(block, axis, [(i, (i + distance) % size) for i in range(size)])


def swap_pair(block):
    size = lax.axis_size("expert")
    return lax.ppermute(block, "expert", [(i, i ^ 1) for i in range(size)])


def cost(flops, bytes_accessed, transcendentals=0):
    return pl.CostEstimate(
        flops=int(flops), bytes_accessed=int(bytes_accessed), transcendentals=int(transcendentals)
    )


def spread_rows(values, wide_ref):
    length, count = values.shape
    col = lax.broadcasted_iota(jnp.int32, (count, count * LANES), 1)
    row = lax.broadcasted_iota(jnp.int32, (count, count * LANES), 0)
    ones = jnp.where((col >= row * LANES) & (col < (row + 1) * LANES), 1.0, 0.0).astype(BF16)
    out = jnp.dot(values, ones, preferred_element_type=F32)
    for n in range(count):
        wide_ref[pl.ds(n * length, length), :] = out[:, n * LANES : (n + 1) * LANES]


def scan_kernel(groups, line, place_ref, *refs):
    pieces, refs = refs[:line], refs[line:]
    w_ref, bias_ref, rate_ref, x_ref, y_ref, sum_ref, end_ref, bc_ref, neg_ref = refs[:9]
    low_ref, step_ref, drive_ref, wide_ref = refs[9:]
    length = x_ref.shape[0]
    share = length // line
    for s in range(line):
        start = pl.multiple_of((place_ref[0] + (line - s)) % line * share, share)
        low_ref[pl.ds(start, share), :] = pieces[s][:, :DT_RANK]
        bc_ref[pl.ds(start, share), :] = pieces[s][:, DT_RANK:]
    spread_rows(bc_ref[...], wide_ref)
    for g in range(SUB):
        rows = pl.ds(g, length, stride=SUB)
        if g >= groups:
            step_ref[rows, :] = jnp.zeros((length, LANES), F32)
            drive_ref[rows, :] = jnp.zeros((length, LANES), F32)
            neg_ref[pl.ds(g, NSTATE, stride=SUB), :] = jnp.zeros((NSTATE, LANES), F32)
            continue
        cols = pl.ds(g * LANES, LANES)
        neg_ref[pl.ds(g, NSTATE, stride=SUB), :] = -rate_ref[:, cols]
        raw = jnp.dot(low_ref[...], w_ref[:, cols], preferred_element_type=F32) + bias_ref[:, cols]
        step = jnp.maximum(raw, 0.0) + jnp.log1p(jnp.exp(-jnp.abs(raw)))
        step_ref[rows, :] = step
        drive_ref[rows, :] = step * x_ref[:, cols].astype(F32)

    def block(k, carry):
        states, total = list(carry[0]), carry[1]
        for u in range(SUB):
            t = k * SUB + u
            here = pl.ds(pl.multiple_of(t * SUB, SUB), SUB)
            step, drive = step_ref[here, :], drive_ref[here, :]
            total = total + step
            out = jnp.zeros((SUB, LANES), F32)
            for n in range(NSTATE):
                decay = jnp.exp(step * neg_ref[pl.ds(n * SUB, SUB), :])
                b = wide_ref[pl.ds(n * length + t, 1), :]
                c = wide_ref[pl.ds((NSTATE + n) * length + t, 1), :]
                states[n] = states[n] * decay + drive * b
                out = out + states[n] * c
            y_ref[here, :] = out
            sum_ref[here, :] = total
        return tuple(states), total

    zero = jnp.zeros((SUB, LANES), F32)
    states, total = lax.fori_loop(0, length // SUB, block, ((zero,) * NSTATE, zero))
    for n in range(NSTATE):
        end_ref[n] = states[n]


def run_scan(place, pieces, w, bias, rate, x):
    length, channels = x.shape
    vmem = pl.BlockSpec(memory_space=pltpu.VMEM)
    tall = jax.ShapeDtypeStruct((length * SUB, LANES), F32)
    return pl.pallas_call(
        functools.partial(scan_kernel, channels // LANES, len(pieces)),
        out_shape=(
            tall,
            tall,
            jax.ShapeDtypeStruct((NSTATE, SUB, LANES), F32),
            jax.ShapeDtypeStruct((length, 2 * NSTATE), BF16),
            jax.ShapeDtypeStruct((NSTATE * SUB, LANES), F32),
        ),
        in_specs=[pl.BlockSpec(memory_space=pltpu.SMEM)] + [vmem] * (len(pieces) + 4),
        out_specs=(vmem,) * 5,
        scratch_shapes=[
            pltpu.VMEM((length, DT_RANK), BF16),
            pltpu.VMEM((length * SUB, LANES), F32),
            pltpu.VMEM((length * SUB, LANES), F32),
            pltpu.VMEM((2 * NSTATE * length, LANES), F32),
        ],
        compiler_params=pltpu.CompilerParams(vmem_limit_bytes=20 * MIB),
        cost_estimate=cost(2e8, 4 * MIB, NSTATE * length * channels),
        name="state_scan",
    )(place, *pieces, w, bias, rate, x)


def out_kernel(groups, line, first, at_ref, y_ref, sum_ref, enter_ref, bc_ref, neg_ref, x_ref, z_ref,
               skip_ref, w_hbm, *refs):
    kept_ref, sent_ref, blocks_ref, full_ref, wide_ref, gated_ref, order_ref, w_ref, sems = refs
    length = x_ref.shape[0]
    tiles, _, tile = w_ref.shape

    def fetch(j):
        cols = pl.ds(pl.multiple_of(j * tile, tile), tile)
        return pltpu.make_async_copy(w_hbm.at[:, cols], w_ref.at[j], sems.at[j])

    for j in range(tiles):
        fetch(j).start()
    spread_rows(bc_ref[:, NSTATE:], wide_ref)

    def block(k, carry):
        for u in range(SUB):
            t = k * SUB + u
            here = pl.ds(pl.multiple_of(t * SUB, SUB), SUB)
            total = sum_ref[here, :]
            out = y_ref[here, :]
            for n in range(NSTATE):
                c = wide_ref[pl.ds(n * length + t, 1), :]
                out = out + jnp.exp(total * neg_ref[pl.ds(n * SUB, SUB), :]) * enter_ref[n] * c
            full_ref[here, :] = out
        return carry

    lax.fori_loop(0, length // SUB, block, 0)
    for g in range(groups):
        cols = pl.ds(g * LANES, LANES)
        mixed_in = x_ref[:, cols].astype(F32)
        read = full_ref[pl.ds(g, length, stride=SUB), :] + skip_ref[:, cols] * mixed_in
        z = z_ref[:, cols].astype(F32)
        gated_ref[:, cols] = (read * (z / (1.0 + jnp.exp(-z)))).astype(BF16)
    place, half = at_ref[0], at_ref[1]
    count = length // 2
    piece = count // line
    for k in range(line):
        for r in range(2):
            source = pl.multiple_of((2 * ((place + k) % line) + (half ^ r)) * piece, piece)
            order_ref[pl.ds(r * count + k * piece, piece), :] = gated_ref[pl.ds(source, piece), :]
    def project(j):
        fetch(j).wait()
        return jnp.dot(order_ref[...], w_ref[j], preferred_element_type=F32).astype(BF16)

    def step(j, carry):
        cols = pl.ds(pl.multiple_of(j * tile, tile), tile)
        out = project(j)
        kept_ref[:, cols] = out[:count]
        sent_ref[:, cols] = out[count:]
        return carry

    def block_step(j, carry):
        cols = pl.ds(pl.multiple_of((j - first) * tile, tile), tile)
        out = project(j)
        for k in range(line):
            for r in range(2):
                start = r * count + k * piece
                blocks_ref[k, pl.ds(r * piece, piece), cols] = out[start : start + piece]
        return carry

    lax.fori_loop(0, first, step, 0)
    lax.fori_loop(first, tiles, block_step, 0)


def run_out(at, line, y, total, enter, bc, neg, x, z, skip, w):
    length, channels = x.shape
    wide = w.shape[1]
    tile = min(512, wide)
    first = (wide // tile * 5 + 4) // 8
    vmem = pl.BlockSpec(memory_space=pltpu.VMEM)
    part = jax.ShapeDtypeStruct((length // 2, first * tile), BF16)
    blocks = jax.ShapeDtypeStruct((line, length // line, wide - first * tile), BF16)
    return pl.pallas_call(
        functools.partial(out_kernel, channels // LANES, line, first),
        out_shape=(part, part, blocks),
        in_specs=[pl.BlockSpec(memory_space=pltpu.SMEM)] + [vmem] * 8 + [pl.BlockSpec(memory_space=pl.ANY)],
        out_specs=(vmem,) * 3,
        scratch_shapes=[
            pltpu.VMEM((length * SUB, LANES), F32),
            pltpu.VMEM((NSTATE * length, LANES), F32),
            pltpu.VMEM((length, channels), BF16),
            pltpu.VMEM((length, channels), BF16),
            pltpu.VMEM((wide // tile, channels, tile), BF16),
            pltpu.SemaphoreType.DMA((wide // tile,)),
        ],
        compiler_params=pltpu.CompilerParams(vmem_limit_bytes=48 * MIB),
        cost_estimate=cost(
            2 * length * channels * wide, 2 * channels * wide + 8 * MIB, NSTATE * length * channels
        ),
        name="readout_project",
    )(at, y, total, enter, bc, neg, x, z, skip, w)


def gate_up_kernel(count, first, *refs):
    pieces, (gate_hbm, up_hbm, out_ref, rows_ref, gate_ref, up_ref, sems) = refs[:count], refs[count:]
    copies, at = [], 0
    for k, piece in enumerate(pieces):
        rows = pl.ds(at, piece.shape[0])
        copies.append(pltpu.make_async_copy(piece, rows_ref.at[rows, :], sems.at[k]))
        at += piece.shape[0]
    steps, tile = gate_ref.shape[0], gate_ref.shape[2]

    def fetch(j, k):
        cols = pl.ds(pl.multiple_of(first + j * tile, tile), tile)
        source, target = ((gate_hbm, gate_ref), (up_hbm, up_ref))[k]
        return pltpu.make_async_copy(source.at[:, cols], target.at[j], sems.at[count + 2 * j + k])

    for copy in copies:
        copy.start()
    for j in range(steps):
        fetch(j, 0).start()
        fetch(j, 1).start()
    for copy in copies:
        copy.wait()

    def step(j, carry):
        fetch(j, 0).wait()
        fetch(j, 1).wait()
        gate = jnp.dot(rows_ref[...], gate_ref[j], preferred_element_type=F32)
        up = jnp.dot(rows_ref[...], up_ref[j], preferred_element_type=F32)
        cols = pl.ds(pl.multiple_of(j * tile, tile), tile)
        out_ref[:, cols] = (gate / (1.0 + jnp.exp(-gate)) * up).astype(BF16)
        return carry

    lax.fori_loop(0, steps, step, 0)


def gate_up(pieces, w_gate, w_up, first, width):
    depth = w_gate.shape[0]
    rows = sum(p.shape[0] for p in pieces)
    tile = min(256, width)
    steps = width // tile
    anywhere = pl.BlockSpec(memory_space=pl.ANY)
    return pl.pallas_call(
        functools.partial(gate_up_kernel, len(pieces), first),
        out_shape=jax.ShapeDtypeStruct((rows, width), BF16),
        in_specs=[anywhere] * (len(pieces) + 2),
        out_specs=pl.BlockSpec(memory_space=pltpu.VMEM),
        scratch_shapes=[
            pltpu.VMEM((rows, depth), BF16),
            pltpu.VMEM((steps, depth, tile), BF16),
            pltpu.VMEM((steps, depth, tile), BF16),
            pltpu.SemaphoreType.DMA((len(pieces) + 2 * steps,)),
        ],
        compiler_params=pltpu.CompilerParams(vmem_limit_bytes=49 * MIB),
        cost_estimate=cost(4 * rows * depth * width, 4 * depth * width + 2 * rows * depth),
        name="gate_up",
    )(*pieces, w_gate, w_up)


def finish_kernel(count, first, *refs):
    pieces, (have_ref, gate_hbm, up_hbm, down_hbm) = refs[:count], refs[count : count + 4]
    hidden_ref, outs = refs[count + 4], refs[count + 5 : -5]
    rows_ref, gate_ref, up_ref, down_ref, sems = refs[-5:]
    done = have_ref.shape[1]
    steps, tile = gate_ref.shape[0], gate_ref.shape[2]
    last_steps, last_tile = down_ref.shape[0], down_ref.shape[2]

    def fetch(j, k):
        cols = pl.ds(pl.multiple_of(done + j * tile, tile), tile)
        source, target = ((gate_hbm, gate_ref), (up_hbm, up_ref))[k]
        return pltpu.make_async_copy(source.at[:, cols], target.at[j], sems.at[count + 2 * j + k])

    def last_fetch(j):
        cols = pl.ds(pl.multiple_of(first + j * last_tile, last_tile), last_tile)
        sem = sems.at[count + 2 * steps + j]
        return pltpu.make_async_copy(down_hbm.at[:, cols], down_ref.at[j], sem)

    copies, at = [], 0
    for k, piece in enumerate(pieces):
        rows = pl.ds(at, piece.shape[0])
        copies.append(pltpu.make_async_copy(piece, rows_ref.at[rows, :], sems.at[k]))
        at += piece.shape[0]
    for copy in copies:
        copy.start()
    for j in range(steps):
        fetch(j, 0).start()
        fetch(j, 1).start()
    for j in range(last_steps):
        last_fetch(j).start()
    hidden_ref[:, pl.ds(0, done)] = have_ref[...]
    for copy in copies:
        copy.wait()

    def step(j, carry):
        fetch(j, 0).wait()
        fetch(j, 1).wait()
        gate = jnp.dot(rows_ref[...], gate_ref[j], preferred_element_type=F32)
        up = jnp.dot(rows_ref[...], up_ref[j], preferred_element_type=F32)
        cols = pl.ds(pl.multiple_of(done + j * tile, tile), tile)
        hidden_ref[:, cols] = (gate / (1.0 + jnp.exp(-gate)) * up).astype(BF16)
        return carry

    def last_step(j, carry):
        last_fetch(j).wait()
        out = jnp.dot(hidden_ref[...], down_ref[j], preferred_element_type=F32).astype(BF16)
        cols = pl.ds(pl.multiple_of(j * last_tile, last_tile), last_tile)
        start = 0
        for ref in outs:
            ref[:, cols] = out[start : start + ref.shape[0]]
            start += ref.shape[0]
        return carry

    lax.fori_loop(0, steps, step, 0)
    lax.fori_loop(0, last_steps, last_step, 0)


def finish(pieces, have, sizes, w_gate, w_up, w_down, first, width):
    depth, hidden = w_gate.shape
    rows, done = have.shape
    tile, last_tile = min(256, hidden - done), min(512, width)
    steps, last_steps = (hidden - done) // tile, width // last_tile
    vmem, anywhere = pl.BlockSpec(memory_space=pltpu.VMEM), pl.BlockSpec(memory_space=pl.ANY)
    shapes = [(rows, hidden)] + [(n, width) for n in sizes]
    hidden_out, *outs = pl.pallas_call(
        functools.partial(finish_kernel, len(pieces), first),
        out_shape=tuple(jax.ShapeDtypeStruct(shape, BF16) for shape in shapes),
        in_specs=[anywhere] * len(pieces) + [vmem] + [anywhere] * 3,
        out_specs=(vmem,) * len(shapes),
        scratch_shapes=[
            pltpu.VMEM((rows, depth), BF16),
            pltpu.VMEM((steps, depth, tile), BF16),
            pltpu.VMEM((steps, depth, tile), BF16),
            pltpu.VMEM((last_steps, hidden, last_tile), BF16),
            pltpu.SemaphoreType.DMA((len(pieces) + 2 * steps + last_steps,)),
        ],
        compiler_params=pltpu.CompilerParams(vmem_limit_bytes=49 * MIB),
        cost_estimate=cost(
            4 * rows * depth * (hidden - done) + 2 * rows * hidden * width,
            4 * depth * (hidden - done) + 2 * hidden * width + 2 * rows * (depth + width),
        ),
        name="gate_up_down",
    )(*pieces, have, w_gate, w_up, w_down)
    return hidden_out, outs


def down_kernel(count, first, *refs):
    pieces, w_hbm, outs = refs[:count], refs[count], refs[count + 1 : -3]
    rows_ref, w_ref, sems = refs[-3:]
    tiles, _, tile = w_ref.shape

    def fetch(j):
        source = pl.ds(pl.multiple_of(first + j * tile, tile), tile)
        return pltpu.make_async_copy(w_hbm.at[:, source], w_ref.at[j], sems.at[j])

    for j in range(tiles):
        fetch(j).start()
    at = 0
    for piece in pieces:
        rows_ref[:, pl.ds(at, piece.shape[1])] = piece[...]
        at += piece.shape[1]

    def step(j, carry):
        fetch(j).wait()
        out = jnp.dot(rows_ref[...], w_ref[j], preferred_element_type=F32).astype(BF16)
        cols = pl.ds(pl.multiple_of(j * tile, tile), tile)
        start = 0
        for ref in outs:
            ref[:, cols] = out[start : start + ref.shape[0]]
            start += ref.shape[0]
        return carry

    lax.fori_loop(0, tiles, step, 0)


def down(pieces, sizes, w_down, first, width):
    hidden, rows = w_down.shape[0], pieces[0].shape[0]
    tile = min(512, width)
    vmem = pl.BlockSpec(memory_space=pltpu.VMEM)
    return pl.pallas_call(
        functools.partial(down_kernel, len(pieces), first),
        out_shape=tuple(jax.ShapeDtypeStruct((n, width), BF16) for n in sizes),
        in_specs=[vmem] * len(pieces) + [pl.BlockSpec(memory_space=pl.ANY)],
        out_specs=(vmem,) * len(sizes),
        scratch_shapes=[
            pltpu.VMEM((rows, hidden), BF16),
            pltpu.VMEM((width // tile, hidden, tile), BF16),
            pltpu.SemaphoreType.DMA((width // tile,)),
        ],
        compiler_params=pltpu.CompilerParams(vmem_limit_bytes=49 * MIB),
        cost_estimate=cost(2 * rows * hidden * width, 2 * hidden * width + 2 * rows * (hidden + width)),
        name="down",
    )(*pieces, w_down)


def add_up(*parts):
    return sum(p.astype(F32) for p in parts)


def along_line(block, distance):
    size = lax.axis_size("expert")
    return lax.ppermute(block, "expert", [(e, (e + 2 * distance) % size) for e in range(size)])


def cross(block, turn):
    owners, dps = lax.axis_size("expert"), lax.axis_size("dp")
    route = []
    for e in range(owners):
        for core in range(2):
            for d in range(dps):
                to = (e ^ 1, core, d) if core == turn else (e, core, d ^ 1)
                route.append(((e * 2 + core) * dps + d, (to[0] * 2 + core) * dps + to[2]))
    return lax.ppermute(block, ("expert", "context", "dp"), route)


def after(blocks, *others):
    return lax.optimization_barrier((blocks, others))[0]


def send_rows(packed, line, way=1):
    size = packed.shape[0] // line
    parts = [packed[size * s : size * (s + 1)] for s in range(line)]
    return [parts[0]] + [along_line(parts[s], way * s) for s in range(1, line)]


def plain_experts(packed, line, w_gate, w_up, w_down):
    own = jnp.concatenate(send_rows(packed, line), axis=0)
    rows = jnp.concatenate([own, swap_pair(own)], axis=0)
    rows = lax.all_gather(rows, ("context", "dp"), axis=0, tiled=True)
    hidden = gate_up([rows], w_gate, w_up, 0, w_gate.shape[1])
    out = down([hidden], (rows.shape[0],), w_down, 0, w_down.shape[1])[0]
    mine = lax.psum_scatter(out, ("context", "dp"), scatter_dimension=0, tiled=True)
    count = own.shape[0]
    result = add_up(mine[:count], swap_pair(mine[count:])).astype(BF16)
    return jnp.concatenate(send_rows(result, line, -1), axis=0)


def square_experts(early, late, line, w_gate, w_up, w_down):
    width = w_down.shape[1]
    hidden = w_down.shape[0]

    def pieces(two, four):
        return [two, four, shift(two, "context", 1), shift(four, "context", 1)]

    def part(terms, start, stop):
        return add_up(*[t[start:stop] for t in terms]).astype(BF16)

    def home_first(outs, *others):
        terms = [after(outs[0], *others), shift(outs[1], "context", 1)]
        rows = outs[0].shape[0]
        return terms, part(terms, rows // 2, rows)

    def home_second(terms, far):
        terms = terms + [far]
        rows = far.shape[0]
        return terms, part(terms, rows // 2, rows)

    def home_third(terms, far):
        return part(terms + [far], 0, far.shape[0])

    early_came = send_rows(early, line)
    early_own = jnp.concatenate(early_came, axis=0)
    late_came = send_rows(after(late, early_own), line)
    early_near = cross(early_own, 0)
    early_two = jnp.concatenate([early_own, early_near], axis=0)
    early_four = cross(early_two, 1)
    late_came[0] = after(late_came[0], early_near)
    late_own = jnp.concatenate(late_came, axis=0)
    late_near = cross(late_own, 0)
    sizes = (4 * early_own.shape[0],) * 2
    early_rows = after(pieces(early_two, early_four), late_own)
    early_first = gate_up(early_rows, w_gate, w_up, 0, hidden // 2)

    late_two = jnp.concatenate([after(late_own, early_first), late_near], axis=0)
    late_four = cross(late_two, 1)
    early_rows = after(early_rows, late_two)
    early_out = finish(early_rows, early_first, sizes, w_gate, w_up, w_down, 0, width)[1]
    late_four = after(late_four, early_out)
    early_kept, early_go = home_first(after(early_out, late_four))
    early_far = cross(early_go, 1)
    sizes = (4 * late_own.shape[0],) * 2
    late_rows = after(pieces(late_two, late_four), early_go)
    late_hidden = gate_up(late_rows, w_gate, w_up, 0, hidden)
    early_kept, early_go = home_second(after(early_kept, late_hidden), early_far)
    early_far = cross(early_go, 0)
    late_out = down([after(late_hidden, early_go)], sizes, w_down, 0, width)
    early_result = home_third(after(early_kept, late_out), early_far)
    early_came = send_rows(early_result, line, -1)
    late_kept, late_go = home_first(after(late_out, early_result))
    late_far = cross(late_go, 1)
    late_kept, late_go = home_second(after(late_kept, early_came[1]), late_far)
    late_far = cross(late_go, 0)
    late_result = home_third(after(late_kept, early_came[2:]), late_far)
    late_came = send_rows(late_result, line, -1)
    return [jnp.concatenate(came, axis=0) for came in (early_came, late_came)]


def on_device(
    residual,
    x_raw,
    z_gate,
    conv_w,
    conv_b,
    xproj_w,
    dtproj_w,
    dt_bias,
    a_rate,
    skip_gain,
    out_w,
    norm_gain,
    route_ids,
    route_w,
    w_gate,
    w_up,
    w_down,
):
    owners, contexts, dps = (lax.axis_size(a) for a in ("expert", "context", "dp"))
    me = lax.axis_index("expert")
    place, half = me // 2, me % 2
    line = owners // 2
    length, channels = x_raw.shape[2:]
    width = residual.shape[3]
    row_count = residual.shape[2]

    values = x_raw[0, 0]
    prior_rim = from_behind(values[length - (CONV - 1) :], "context", 1)
    padded = jnp.concatenate([prior_rim, values], axis=0).astype(F32)
    conv_sum = conv_b[None, :] + sum(
        (
            conv_w[lag_index][None, :] * padded[lag_index : lag_index + length]
            for lag_index in range(CONV)
        )
    )
    mixed_in = jax.nn.silu(conv_sum).astype(BF16)
    projected = jnp.dot(mixed_in, xproj_w, preferred_element_type=F32).astype(BF16)
    shares = projected.reshape(line, length // line, -1)

    def share_of(s):
        return lax.dynamic_index_in_dim(shares, (place + s) % line, 0, keepdims=False)

    share = add_up(share_of(0), *[along_line(share_of(s), s) for s in range(1, line)]).astype(BF16)
    share = add_up(share, swap_pair(share)).astype(BF16)
    pieces = [share] + [along_line(share, s) for s in range(1, line)]

    where = jnp.stack([place, half]).astype(jnp.int32)
    y, total, end, bc, neg = run_scan(
        where, pieces, dtproj_w, dt_bias[None, :], a_rate, mixed_in
    )
    enter = from_behind(end, "context", 1)
    for step in range(contexts - 2):
        decay = jnp.exp(total[-SUB:][None] * neg.reshape(end.shape))
        enter = from_behind(end + decay * enter, "context", 1)
    kept, sent, blocks = run_out(
        where, line, y, total, enter, bc, neg, mixed_in, z_gate[0, 0], skip_gain[None, :], out_w
    )
    got = swap_pair(sent)
    over_z = add_up(blocks[0], *[along_line(blocks[s], s) for s in range(1, line)])
    both = add_up(kept, got).astype(BF16).reshape(line, row_count, -1)
    other = swap_pair(over_z[row_count:].astype(BF16))
    sums = [
        add_up(both[0], *[along_line(both[s], s) for s in range(1, line)]),
        add_up(over_z[:row_count], other),
    ]
    mixer_out = jnp.concatenate(sums, axis=1)

    stream_f = (residual[0, 0].astype(F32) + mixer_out).astype(BF16).astype(F32)
    normed = (
        stream_f
        * lax.rsqrt(jnp.mean(stream_f * stream_f, axis=1, keepdims=True) + 1e-05)
        * norm_gain[None, :]
    ).astype(BF16)
    ids, weights = after((route_ids[0, 0], route_w[0, 0]), kept)
    capacity = min(row_count, 8 * ((3 * row_count * TOP + 16 * line - 1) // (16 * line)))
    square = contexts == 2 and dps == 2 and capacity > 8
    cuts = (0, capacity - 8, capacity) if square else (0, capacity)
    named = jnp.any(ids[:, :, None] == jnp.arange(line, dtype=jnp.int32), axis=1)
    rank = jnp.cumsum(named.astype(jnp.int32), axis=0) - 1
    chosen = ids[:, :, None] == jnp.arange(line, dtype=jnp.int32)
    rank_of = jnp.sum(jnp.where(chosen, rank[:, None, :], 0), axis=2)
    away = (ids - place + line) % line
    placing, weighting, packed = [], [], []
    for low, high in zip(cuts[:-1], cuts[1:]):
        inside = (rank_of >= low) & (rank_of < high)
        slot_of = jnp.where(inside, away * (high - low) + rank_of - low, -1)
        hits = slot_of[:, :, None] == jnp.arange(line * (high - low), dtype=jnp.int32)
        placing = jnp.any(hits, axis=1).astype(BF16)
        weighting.append(jnp.sum(jnp.where(hits, weights[:, :, None], 0.0), axis=1))
        rows = lax.dot_general(
            placing, normed, (((0,), (0,)), ((), ())), preferred_element_type=F32
        )
        packed.append(rows.astype(BF16))
    if len(packed) == 2:
        back = square_experts(*packed, line, w_gate[0], w_up[0], w_down[0])
    else:
        back = [plain_experts(packed[0], line, w_gate[0], w_up[0], w_down[0])]
    expert_sum = sum(
        jnp.dot(
            w, rows.astype(F32), precision=lax.Precision.HIGHEST, preferred_element_type=F32
        )
        for w, rows in zip(weighting, back)
    )
    mixed = (stream_f + expert_sum).astype(BF16)
    return mixed.reshape(1, 1, row_count, width)


def solution(mesh):
    placed = (
        P("dp", "context", "expert", None),
        P("dp", "context", None, "expert"),
        P("dp", "context", None, "expert"),
        P(None, "expert"),
        P("expert"),
        P("expert", None),
        P(None, "expert"),
        P("expert"),
        P(None, "expert"),
        P("expert"),
        P("expert", None),
        P(),
        P("dp", "context", "expert", None),
        P("dp", "context", "expert", None),
        P("expert", None, ("context", "dp")),
        P("expert", None, ("context", "dp")),
        P("expert", ("context", "dp"), None),
    )
    return jax.shard_map(
        on_device,
        mesh=mesh,
        in_specs=placed,
        out_specs=P("dp", "context", "expert", None),
        check_vma=False,
    )
```

```python
import functools

import jax
import jax.numpy as jnp
from jax import lax
from jax.experimental import pallas as pl
from jax.experimental.pallas import tpu as pltpu
from jax.sharding import PartitionSpec as P

NSTATE = 16
DT_RANK = 256
CONV = 4
TOP = 2
LANES = 128
SUB = 8
F32 = jnp.float32
BF16 = jnp.bfloat16
MIB = 1 << 20


def from_behind(block, axis, distance):
    devices = range(lax.axis_size(axis))
    route = [(i - distance, i) for i in devices if i - distance in devices]
    return lax.ppermute(block, axis, route)


def shift(block, axis, distance):
    size = lax.axis_size(axis)
    return lax.ppermute(block, axis, [(i, (i + distance) % size) for i in range(size)])


def swap_pair(block):
    size = lax.axis_size("expert")
    return lax.ppermute(block, "expert", [(i, i ^ 1) for i in range(size)])


def cost(flops, bytes_accessed, transcendentals=0):
    return pl.CostEstimate(
        flops=int(flops), bytes_accessed=int(bytes_accessed), transcendentals=int(transcendentals)
    )


def spread_rows(values, wide_ref):
    length, count = values.shape
    col = lax.broadcasted_iota(jnp.int32, (count, count * LANES), 1)
    row = lax.broadcasted_iota(jnp.int32, (count, count * LANES), 0)
    ones = jnp.where((col >= row * LANES) & (col < (row + 1) * LANES), 1.0, 0.0).astype(BF16)
    out = jnp.dot(values, ones, preferred_element_type=F32)
    for n in range(count):
        wide_ref[pl.ds(n * length, length), :] = out[:, n * LANES : (n + 1) * LANES]


def scan_kernel(groups, line, place_ref, *refs):
    pieces, refs = refs[:line], refs[line:]
    w_ref, bias_ref, rate_ref, x_ref, y_ref, sum_ref, end_ref, bc_ref, neg_ref = refs[:9]
    low_ref, step_ref, drive_ref, wide_ref = refs[9:]
    length = x_ref.shape[0]
    share = length // line
    for s in range(line):
        start = pl.multiple_of((place_ref[0] + (line - s)) % line * share, share)
        low_ref[pl.ds(start, share), :] = pieces[s][:, :DT_RANK]
        bc_ref[pl.ds(start, share), :] = pieces[s][:, DT_RANK:]
    spread_rows(bc_ref[...], wide_ref)
    for g in range(SUB):
        rows = pl.ds(g, length, stride=SUB)
        if g >= groups:
            step_ref[rows, :] = jnp.zeros((length, LANES), F32)
            drive_ref[rows, :] = jnp.zeros((length, LANES), F32)
            neg_ref[pl.ds(g, NSTATE, stride=SUB), :] = jnp.zeros((NSTATE, LANES), F32)
            continue
        cols = pl.ds(g * LANES, LANES)
        neg_ref[pl.ds(g, NSTATE, stride=SUB), :] = -rate_ref[:, cols]
        raw = jnp.dot(low_ref[...], w_ref[:, cols], preferred_element_type=F32) + bias_ref[:, cols]
        step = jnp.maximum(raw, 0.0) + jnp.log1p(jnp.exp(-jnp.abs(raw)))
        step_ref[rows, :] = step
        drive_ref[rows, :] = step * x_ref[:, cols].astype(F32)

    def block(k, carry):
        states, total = list(carry[0]), carry[1]
        for u in range(SUB):
            t = k * SUB + u
            here = pl.ds(pl.multiple_of(t * SUB, SUB), SUB)
            step, drive = step_ref[here, :], drive_ref[here, :]
            total = total + step
            out = jnp.zeros((SUB, LANES), F32)
            for n in range(NSTATE):
                decay = jnp.exp(step * neg_ref[pl.ds(n * SUB, SUB), :])
                b = wide_ref[pl.ds(n * length + t, 1), :]
                c = wide_ref[pl.ds((NSTATE + n) * length + t, 1), :]
                states[n] = states[n] * decay + drive * b
                out = out + states[n] * c
            y_ref[here, :] = out
            sum_ref[here, :] = total
        return tuple(states), total

    zero = jnp.zeros((SUB, LANES), F32)
    states, total = lax.fori_loop(0, length // SUB, block, ((zero,) * NSTATE, zero))
    for n in range(NSTATE):
        end_ref[n] = states[n]


def run_scan(place, pieces, w, bias, rate, x):
    length, channels = x.shape
    vmem = pl.BlockSpec(memory_space=pltpu.VMEM)
    tall = jax.ShapeDtypeStruct((length * SUB, LANES), F32)
    return pl.pallas_call(
        functools.partial(scan_kernel, channels // LANES, len(pieces)),
        out_shape=(
            tall,
            tall,
            jax.ShapeDtypeStruct((NSTATE, SUB, LANES), F32),
            jax.ShapeDtypeStruct((length, 2 * NSTATE), BF16),
            jax.ShapeDtypeStruct((NSTATE * SUB, LANES), F32),
        ),
        in_specs=[pl.BlockSpec(memory_space=pltpu.SMEM)] + [vmem] * (len(pieces) + 4),
        out_specs=(vmem,) * 5,
        scratch_shapes=[
            pltpu.VMEM((length, DT_RANK), BF16),
            pltpu.VMEM((length * SUB, LANES), F32),
            pltpu.VMEM((length * SUB, LANES), F32),
            pltpu.VMEM((2 * NSTATE * length, LANES), F32),
        ],
        compiler_params=pltpu.CompilerParams(vmem_limit_bytes=20 * MIB),
        cost_estimate=cost(2e8, 4 * MIB, NSTATE * length * channels),
        name="state_scan",
    )(place, *pieces, w, bias, rate, x)


def out_kernel(groups, line, first, at_ref, y_ref, sum_ref, enter_ref, bc_ref, neg_ref, x_ref, z_ref,
               skip_ref, w_hbm, *refs):
    kept_ref, sent_ref, block_refs = refs[0], refs[1], refs[2 : 2 + line]
    full_ref, wide_ref, gated_ref, order_ref, w_ref, sems = refs[2 + line :]
    length = x_ref.shape[0]
    tiles, _, tile = w_ref.shape

    def fetch(j):
        cols = pl.ds(pl.multiple_of(j * tile, tile), tile)
        return pltpu.make_async_copy(w_hbm.at[:, cols], w_ref.at[j], sems.at[j])

    for j in range(tiles):
        fetch(j).start()
    spread_rows(bc_ref[:, NSTATE:], wide_ref)

    def block(k, carry):
        for u in range(SUB):
            t = k * SUB + u
            here = pl.ds(pl.multiple_of(t * SUB, SUB), SUB)
            total = sum_ref[here, :]
            out = y_ref[here, :]
            for n in range(NSTATE):
                c = wide_ref[pl.ds(n * length + t, 1), :]
                out = out + jnp.exp(total * neg_ref[pl.ds(n * SUB, SUB), :]) * enter_ref[n] * c
            full_ref[here, :] = out
        return carry

    lax.fori_loop(0, length // SUB, block, 0)
    for g in range(groups):
        cols = pl.ds(g * LANES, LANES)
        mixed_in = x_ref[:, cols].astype(F32)
        read = full_ref[pl.ds(g, length, stride=SUB), :] + skip_ref[:, cols] * mixed_in
        z = z_ref[:, cols].astype(F32)
        gated_ref[:, cols] = (read * (z / (1.0 + jnp.exp(-z)))).astype(BF16)
    place, half = at_ref[0], at_ref[1]
    count = length // 2
    piece = count // line
    for k in range(line):
        for r in range(2):
            source = pl.multiple_of((2 * ((place + k) % line) + (half ^ r)) * piece, piece)
            order_ref[pl.ds(r * count + k * piece, piece), :] = gated_ref[pl.ds(source, piece), :]
    def project(j):
        fetch(j).wait()
        return jnp.dot(order_ref[...], w_ref[j], preferred_element_type=F32).astype(BF16)

    def step(j, carry):
        cols = pl.ds(pl.multiple_of(j * tile, tile), tile)
        out = project(j)
        kept_ref[:, cols] = out[:count]
        sent_ref[:, cols] = out[count:]
        return carry

    def block_step(j, carry):
        cols = pl.ds(pl.multiple_of((j - first) * tile, tile), tile)
        out = project(j)
        for k in range(line):
            for r in range(2):
                start = r * count + k * piece
                block_refs[k][pl.ds(r * piece, piece), cols] = out[start : start + piece]
        return carry

    lax.fori_loop(0, first, step, 0)
    lax.fori_loop(first, tiles, block_step, 0)


def run_out(at, line, y, total, enter, bc, neg, x, z, skip, w):
    length, channels = x.shape
    wide = w.shape[1]
    tile = min(512, wide)
    first = (wide // tile * 5 + 4) // 8
    vmem = pl.BlockSpec(memory_space=pltpu.VMEM)
    part = jax.ShapeDtypeStruct((length // 2, first * tile), BF16)
    block = jax.ShapeDtypeStruct((length // line, wide - first * tile), BF16)
    return pl.pallas_call(
        functools.partial(out_kernel, channels // LANES, line, first),
        out_shape=(part, part) + (block,) * line,
        in_specs=[pl.BlockSpec(memory_space=pltpu.SMEM)] + [vmem] * 8 + [pl.BlockSpec(memory_space=pl.ANY)],
        out_specs=(vmem,) * (2 + line),
        scratch_shapes=[
            pltpu.VMEM((length * SUB, LANES), F32),
            pltpu.VMEM((NSTATE * length, LANES), F32),
            pltpu.VMEM((length, channels), BF16),
            pltpu.VMEM((length, channels), BF16),
            pltpu.VMEM((wide // tile, channels, tile), BF16),
            pltpu.SemaphoreType.DMA((wide // tile,)),
        ],
        compiler_params=pltpu.CompilerParams(vmem_limit_bytes=48 * MIB),
        cost_estimate=cost(
            2 * length * channels * wide, 2 * channels * wide + 8 * MIB, NSTATE * length * channels
        ),
        name="readout_project",
    )(at, y, total, enter, bc, neg, x, z, skip, w)


class Fetch:
    def __init__(self, source, cols, target, sems, first):
        rows = target.shape[0] // 2
        self.copies = [
            pltpu.make_async_copy(
                source.at[pl.ds(h * rows, rows), cols],
                target.at[pl.ds(h * rows, rows), :],
                sems.at[first + h],
            )
            for h in range(2)
        ]

    def start(self):
        for copy in self.copies:
            copy.start()

    def wait(self):
        for copy in self.copies:
            copy.wait()


def gate_up_kernel(count, first, *refs):
    pieces, (gate_hbm, up_hbm, out_ref, rows_ref, gate_ref, up_ref, sems) = refs[:count], refs[count:]
    copies, at = [], 0
    for k, piece in enumerate(pieces):
        rows = pl.ds(at, piece.shape[0])
        copies.append(pltpu.make_async_copy(piece, rows_ref.at[rows, :], sems.at[k]))
        at += piece.shape[0]
    steps, tile = gate_ref.shape[0], gate_ref.shape[2]

    def fetch(j, k):
        cols = pl.ds(pl.multiple_of(first + j * tile, tile), tile)
        source, target = ((gate_hbm, gate_ref), (up_hbm, up_ref))[k]
        return Fetch(source, cols, target.at[j], sems, count + 4 * j + 2 * k)

    for copy in copies:
        copy.start()
    for j in range(steps):
        fetch(j, 0).start()
        fetch(j, 1).start()
    for copy in copies:
        copy.wait()

    def step(j, carry):
        fetch(j, 0).wait()
        fetch(j, 1).wait()
        gate = jnp.dot(rows_ref[...], gate_ref[j], preferred_element_type=F32)
        up = jnp.dot(rows_ref[...], up_ref[j], preferred_element_type=F32)
        cols = pl.ds(pl.multiple_of(j * tile, tile), tile)
        out_ref[:, cols] = (gate / (1.0 + jnp.exp(-gate)) * up).astype(BF16)
        return carry

    lax.fori_loop(0, steps, step, 0)


def gate_up(pieces, w_gate, w_up, first, width):
    depth = w_gate.shape[0]
    rows = sum(p.shape[0] for p in pieces)
    tile = min(256, width)
    steps = width // tile
    anywhere = pl.BlockSpec(memory_space=pl.ANY)
    return pl.pallas_call(
        functools.partial(gate_up_kernel, len(pieces), first),
        out_shape=jax.ShapeDtypeStruct((rows, width), BF16),
        in_specs=[anywhere] * (len(pieces) + 2),
        out_specs=pl.BlockSpec(memory_space=pltpu.VMEM),
        scratch_shapes=[
            pltpu.VMEM((rows, depth), BF16),
            pltpu.VMEM((steps, depth, tile), BF16),
            pltpu.VMEM((steps, depth, tile), BF16),
            pltpu.SemaphoreType.DMA((len(pieces) + 4 * steps,)),
        ],
        compiler_params=pltpu.CompilerParams(vmem_limit_bytes=49 * MIB),
        cost_estimate=cost(4 * rows * depth * width, 4 * depth * width + 2 * rows * depth),
        name="gate_up",
    )(*pieces, w_gate, w_up)


def finish_kernel(count, first, *refs):
    pieces, (have_ref, gate_hbm, up_hbm, down_hbm) = refs[:count], refs[count : count + 4]
    hidden_ref, outs = refs[count + 4], refs[count + 5 : -5]
    rows_ref, gate_ref, up_ref, down_ref, sems = refs[-5:]
    done = have_ref.shape[1]
    steps, tile = gate_ref.shape[0], gate_ref.shape[2]
    last_steps, last_tile = down_ref.shape[0], down_ref.shape[2]

    def fetch(j, k):
        cols = pl.ds(pl.multiple_of(done + j * tile, tile), tile)
        source, target = ((gate_hbm, gate_ref), (up_hbm, up_ref))[k]
        return Fetch(source, cols, target.at[j], sems, count + 4 * j + 2 * k)

    def last_fetch(j):
        cols = pl.ds(pl.multiple_of(first + j * last_tile, last_tile), last_tile)
        return Fetch(down_hbm, cols, down_ref.at[j], sems, count + 4 * steps + 2 * j)

    copies, at = [], 0
    for k, piece in enumerate(pieces):
        rows = pl.ds(at, piece.shape[0])
        copies.append(pltpu.make_async_copy(piece, rows_ref.at[rows, :], sems.at[k]))
        at += piece.shape[0]
    for copy in copies:
        copy.start()
    for j in range(steps):
        fetch(j, 0).start()
        fetch(j, 1).start()
    for j in range(last_steps):
        last_fetch(j).start()
    hidden_ref[:, pl.ds(0, done)] = have_ref[...]
    for copy in copies:
        copy.wait()

    def step(j, carry):
        fetch(j, 0).wait()
        fetch(j, 1).wait()
        gate = jnp.dot(rows_ref[...], gate_ref[j], preferred_element_type=F32)
        up = jnp.dot(rows_ref[...], up_ref[j], preferred_element_type=F32)
        cols = pl.ds(pl.multiple_of(done + j * tile, tile), tile)
        hidden_ref[:, cols] = (gate / (1.0 + jnp.exp(-gate)) * up).astype(BF16)
        return carry

    def last_step(j, carry):
        last_fetch(j).wait()
        out = jnp.dot(hidden_ref[...], down_ref[j], preferred_element_type=F32).astype(BF16)
        cols = pl.ds(pl.multiple_of(j * last_tile, last_tile), last_tile)
        start = 0
        for ref in outs:
            ref[:, cols] = out[start : start + ref.shape[0]]
            start += ref.shape[0]
        return carry

    lax.fori_loop(0, steps, step, 0)
    lax.fori_loop(0, last_steps, last_step, 0)


def finish(pieces, have, sizes, w_gate, w_up, w_down, first, width):
    depth, hidden = w_gate.shape
    rows, done = have.shape
    tile, last_tile = min(256, hidden - done), min(512, width)
    steps, last_steps = (hidden - done) // tile, width // last_tile
    vmem, anywhere = pl.BlockSpec(memory_space=pltpu.VMEM), pl.BlockSpec(memory_space=pl.ANY)
    shapes = [(rows, hidden)] + [(n, width) for n in sizes]
    hidden_out, *outs = pl.pallas_call(
        functools.partial(finish_kernel, len(pieces), first),
        out_shape=tuple(jax.ShapeDtypeStruct(shape, BF16) for shape in shapes),
        in_specs=[anywhere] * len(pieces) + [vmem] + [anywhere] * 3,
        out_specs=(vmem,) * len(shapes),
        scratch_shapes=[
            pltpu.VMEM((rows, depth), BF16),
            pltpu.VMEM((steps, depth, tile), BF16),
            pltpu.VMEM((steps, depth, tile), BF16),
            pltpu.VMEM((last_steps, hidden, last_tile), BF16),
            pltpu.SemaphoreType.DMA((len(pieces) + 4 * steps + 2 * last_steps,)),
        ],
        compiler_params=pltpu.CompilerParams(vmem_limit_bytes=49 * MIB),
        cost_estimate=cost(
            4 * rows * depth * (hidden - done) + 2 * rows * hidden * width,
            4 * depth * (hidden - done) + 2 * hidden * width + 2 * rows * (depth + width),
        ),
        name="gate_up_down",
    )(*pieces, have, w_gate, w_up, w_down)
    return hidden_out, outs


def down_kernel(count, first, *refs):
    pieces, w_hbm, outs = refs[:count], refs[count], refs[count + 1 : -3]
    rows_ref, w_ref, sems = refs[-3:]
    tiles, _, tile = w_ref.shape

    def fetch(j):
        source = pl.ds(pl.multiple_of(first + j * tile, tile), tile)
        return Fetch(w_hbm, source, w_ref.at[j], sems, 2 * j)

    for j in range(tiles):
        fetch(j).start()
    at = 0
    for piece in pieces:
        rows_ref[:, pl.ds(at, piece.shape[1])] = piece[...]
        at += piece.shape[1]

    def step(j, carry):
        fetch(j).wait()
        out = jnp.dot(rows_ref[...], w_ref[j], preferred_element_type=F32).astype(BF16)
        cols = pl.ds(pl.multiple_of(j * tile, tile), tile)
        start = 0
        for ref in outs:
            ref[:, cols] = out[start : start + ref.shape[0]]
            start += ref.shape[0]
        return carry

    lax.fori_loop(0, tiles, step, 0)


def down(pieces, sizes, w_down, first, width):
    hidden, rows = w_down.shape[0], pieces[0].shape[0]
    tile = min(512, width)
    vmem = pl.BlockSpec(memory_space=pltpu.VMEM)
    return pl.pallas_call(
        functools.partial(down_kernel, len(pieces), first),
        out_shape=tuple(jax.ShapeDtypeStruct((n, width), BF16) for n in sizes),
        in_specs=[vmem] * len(pieces) + [pl.BlockSpec(memory_space=pl.ANY)],
        out_specs=(vmem,) * len(sizes),
        scratch_shapes=[
            pltpu.VMEM((rows, hidden), BF16),
            pltpu.VMEM((width // tile, hidden, tile), BF16),
            pltpu.SemaphoreType.DMA((2 * (width // tile),)),
        ],
        compiler_params=pltpu.CompilerParams(vmem_limit_bytes=49 * MIB),
        cost_estimate=cost(2 * rows * hidden * width, 2 * hidden * width + 2 * rows * (hidden + width)),
        name="down",
    )(*pieces, w_down)


def add_up(*parts):
    return sum(p.astype(F32) for p in parts)


def along_line(block, distance):
    size = lax.axis_size("expert")
    return lax.ppermute(block, "expert", [(e, (e + 2 * distance) % size) for e in range(size)])


def cross(block, turn):
    owners, dps = lax.axis_size("expert"), lax.axis_size("dp")
    route = []
    for e in range(owners):
        for core in range(2):
            for d in range(dps):
                to = (e ^ 1, core, d) if core == turn else (e, core, d ^ 1)
                route.append(((e * 2 + core) * dps + d, (to[0] * 2 + core) * dps + to[2]))
    return lax.ppermute(block, ("expert", "context", "dp"), route)


def after(blocks, *others):
    return lax.optimization_barrier((blocks, others))[0]


def send_rows(packed, line, way=1):
    size = packed.shape[0] // line
    parts = [packed[size * s : size * (s + 1)] for s in range(line)]
    return [parts[0]] + [along_line(parts[s], way * s) for s in range(1, line)]


def plain_experts(packed, line, w_gate, w_up, w_down):
    own = jnp.concatenate(send_rows(packed, line), axis=0)
    rows = jnp.concatenate([own, swap_pair(own)], axis=0)
    rows = lax.all_gather(rows, ("context", "dp"), axis=0, tiled=True)
    hidden = gate_up([rows], w_gate, w_up, 0, w_gate.shape[1])
    out = down([hidden], (rows.shape[0],), w_down, 0, w_down.shape[1])[0]
    mine = lax.psum_scatter(out, ("context", "dp"), scatter_dimension=0, tiled=True)
    count = own.shape[0]
    result = add_up(mine[:count], swap_pair(mine[count:])).astype(BF16)
    return jnp.concatenate(send_rows(result, line, -1), axis=0)


def square_experts(early, late, line, w_gate, w_up, w_down):
    width = w_down.shape[1]
    half = width // 2
    hidden = w_down.shape[0]
    most = hidden // 2

    def pieces(two, four):
        return [two, four, shift(two, "context", 1), shift(four, "context", 1)]

    def part(terms, start, stop):
        return add_up(*[t[start:stop] for t in terms]).astype(BF16)

    def home_first(outs, *others):
        terms = [after(outs[0], *others), shift(outs[1], "context", 1)]
        rows = outs[0].shape[0]
        return terms, part(terms, rows // 2, rows)

    def home_second(terms, far):
        terms = terms + [far]
        rows = far.shape[0]
        return terms, part(terms, rows // 2, rows)

    def home_third(terms, far):
        return part(terms + [far], 0, far.shape[0])

    early_came = send_rows(early, line)
    early_own = jnp.concatenate(early_came, axis=0)
    late_came = send_rows(after(late, early_own), line)
    early_near = cross(early_own, 0)
    early_two = jnp.concatenate([early_own, early_near], axis=0)
    early_four = cross(early_two, 1)
    late_came[0] = after(late_came[0], early_near)
    late_own = jnp.concatenate(late_came, axis=0)
    late_near = cross(late_own, 0)
    sizes = (4 * early_own.shape[0],) * 2
    early_rows = after(pieces(early_two, early_four), late_own)
    early_first = gate_up(early_rows, w_gate, w_up, 0, most)

    late_two = jnp.concatenate([after(late_own, early_first), late_near], axis=0)
    late_four = cross(late_two, 1)
    early_rows = after(early_rows, late_two)
    early_out = finish(early_rows, early_first, sizes, w_gate, w_up, w_down, 0, width)[1]
    late_four = after(late_four, early_out)
    early_kept, early_go = home_first(early_out, late_four)
    early_far = cross(early_go, 1)
    sizes = (4 * late_own.shape[0],) * 2
    late_rows = after(pieces(late_two, late_four), early_go)
    late_first = gate_up(late_rows, w_gate, w_up, 0, hidden // 2)
    early_kept, early_go = home_second(after(early_kept, late_first), early_far)
    early_far = cross(early_go, 0)
    late_rows = after(late_rows, early_go)
    late_hidden, out_left = finish(late_rows, late_first, sizes, w_gate, w_up, w_down, 0, half)
    early_result = home_third(after(early_kept, out_left[0]), early_far)
    left = home_first(after(out_left, early_result))
    left_far = cross(left[1], 1)
    out_right = down([after(late_hidden, left[1])], sizes, w_down, half, half)
    left = home_second(after(left[0], out_right), left_far)
    left_far = cross(left[1], 0)
    right = home_first(after(out_right, left[1]))
    right_far = cross(right[1], 1)
    left_result = home_third(after(left[0], right[1]), left_far)
    right = home_second(after(right[0], left_result), right_far)
    right_far = cross(right[1], 0)
    few, many = early_result.shape[0] // line, left_result.shape[0] // line
    packed = []
    for s in range(line):
        mine = early_result[few * s : few * (s + 1)]
        packed += [mine[:, :half], mine[:, half:], left_result[many * s : many * (s + 1)]]
    left_came = send_rows(jnp.concatenate(packed, axis=0), line, -1)
    right_result = home_third(right[0], right_far)
    right_came = send_rows(right_result, line, -1)
    left_came = after(left_came, right_result)
    left_rows = [c[:few] for c in left_came] + [c[2 * few :] for c in left_came]
    right_rows = [c[few : 2 * few] for c in left_came] + right_came
    return [jnp.concatenate(rows, axis=0) for rows in (left_rows, right_rows)]


def on_device(
    residual,
    x_raw,
    z_gate,
    conv_w,
    conv_b,
    xproj_w,
    dtproj_w,
    dt_bias,
    a_rate,
    skip_gain,
    out_w,
    norm_gain,
    route_ids,
    route_w,
    w_gate,
    w_up,
    w_down,
):
    owners, contexts, dps = (lax.axis_size(a) for a in ("expert", "context", "dp"))
    me = lax.axis_index("expert")
    place, half = me // 2, me % 2
    line = owners // 2
    length, channels = x_raw.shape[2:]
    width = residual.shape[3]
    row_count = residual.shape[2]

    values = x_raw[0, 0]
    prior_rim = from_behind(values[length - (CONV - 1) :], "context", 1)
    padded = jnp.concatenate([prior_rim, values], axis=0).astype(F32)
    conv_sum = conv_b[None, :] + sum(
        (
            conv_w[lag_index][None, :] * padded[lag_index : lag_index + length]
            for lag_index in range(CONV)
        )
    )
    mixed_in = jax.nn.silu(conv_sum).astype(BF16)
    projected = jnp.dot(mixed_in, xproj_w, preferred_element_type=F32).astype(BF16)
    ids, weights = after((route_ids[0, 0], route_w[0, 0]), projected)
    shares = projected.reshape(line, length // line, -1)

    def share_of(s):
        return lax.dynamic_index_in_dim(shares, (place + s) % line, 0, keepdims=False)

    share = add_up(share_of(0), *[along_line(share_of(s), s) for s in range(1, line)]).astype(BF16)
    share = add_up(share, swap_pair(share)).astype(BF16)
    pieces = [share] + [along_line(share, s) for s in range(1, line)]

    where = jnp.stack([place, half]).astype(jnp.int32)
    y, total, end, bc, neg = run_scan(
        where, pieces, dtproj_w, dt_bias[None, :], a_rate, mixed_in
    )
    enter = from_behind(end, "context", 1)
    for step in range(contexts - 2):
        decay = jnp.exp(total[-SUB:][None] * neg.reshape(end.shape))
        enter = from_behind(end + decay * enter, "context", 1)
    kept, sent, *blocks = run_out(
        where, line, y, total, enter, bc, neg, mixed_in, z_gate[0, 0], skip_gain[None, :], out_w
    )
    got = swap_pair(sent)
    over_z = add_up(blocks[0], *[along_line(blocks[s], s) for s in range(1, line)])
    both = add_up(kept, got).astype(BF16).reshape(line, row_count, -1)
    other = swap_pair(over_z[row_count:].astype(BF16))
    sums = [
        add_up(both[0], *[along_line(both[s], s) for s in range(1, line)]),
        add_up(over_z[:row_count], other),
    ]
    mixer_out = jnp.concatenate(sums, axis=1)

    stream_f = (residual[0, 0].astype(F32) + mixer_out).astype(BF16).astype(F32)
    normed = (
        stream_f
        * lax.rsqrt(jnp.mean(stream_f * stream_f, axis=1, keepdims=True) + 1e-05)
        * norm_gain[None, :]
    ).astype(BF16)
    capacity = min(row_count, 8 * ((3 * row_count * TOP + 16 * line - 1) // (16 * line)))
    cuts = (0, 8, capacity) if contexts == 2 and dps == 2 and capacity > 8 else (0, capacity)
    named = jnp.any(ids[:, :, None] == jnp.arange(line, dtype=jnp.int32), axis=1)
    rank = jnp.cumsum(named.astype(jnp.int32), axis=0) - 1
    chosen = ids[:, :, None] == jnp.arange(line, dtype=jnp.int32)
    rank_of = jnp.sum(jnp.where(chosen, rank[:, None, :], 0), axis=2)
    away = (ids - place + line) % line
    placing, weighting, packed = [], [], []
    for low, high in zip(cuts[:-1], cuts[1:]):
        inside = (rank_of >= low) & (rank_of < high)
        slot_of = jnp.where(inside, away * (high - low) + rank_of - low, -1)
        hits = slot_of[:, :, None] == jnp.arange(line * (high - low), dtype=jnp.int32)
        placing = jnp.any(hits, axis=1).astype(BF16)
        weighting.append(jnp.sum(jnp.where(hits, weights[:, :, None], 0.0), axis=1))
        rows = lax.dot_general(
            placing, normed, (((0,), (0,)), ((), ())), preferred_element_type=F32
        )
        packed.append(rows.astype(BF16))
    if len(packed) == 2:
        back = square_experts(*packed, line, w_gate[0], w_up[0], w_down[0])
    else:
        back = [plain_experts(packed[0], line, w_gate[0], w_up[0], w_down[0])]
    weighting = jnp.concatenate(weighting, axis=1)
    expert_sum = jnp.concatenate(
        [
            jnp.dot(
                weighting,
                rows.astype(F32),
                precision=lax.Precision.HIGHEST,
                preferred_element_type=F32,
            )
            for rows in back
        ],
        axis=1,
    )
    mixed = (stream_f + expert_sum).astype(BF16)
    return mixed.reshape(1, 1, row_count, width)


def solution(mesh):
    placed = (
        P("dp", "context", "expert", None),
        P("dp", "context", None, "expert"),
        P("dp", "context", None, "expert"),
        P(None, "expert"),
        P("expert"),
        P("expert", None),
        P(None, "expert"),
        P("expert"),
        P(None, "expert"),
        P("expert"),
        P("expert", None),
        P(),
        P("dp", "context", "expert", None),
        P("dp", "context", "expert", None),
        P("expert", None, ("context", "dp")),
        P("expert", None, ("context", "dp")),
        P("expert", ("context", "dp"), None),
    )
    return jax.shard_map(
        on_device,
        mesh=mesh,
        in_specs=placed,
        out_specs=P("dp", "context", "expert", None),
        check_vma=False,
    )
```

```python
import functools

import jax
import jax.numpy as jnp
from jax import lax
from jax.experimental import pallas as pl
from jax.experimental.pallas import tpu as pltpu
from jax.sharding import PartitionSpec as P

NSTATE = 16
DT_RANK = 256
CONV = 4
TOP = 2
LANES = 128
SUB = 8
F32 = jnp.float32
BF16 = jnp.bfloat16
MIB = 1 << 20


def from_behind(block, axis, distance):
    devices = range(lax.axis_size(axis))
    route = [(i - distance, i) for i in devices if i - distance in devices]
    return lax.ppermute(block, axis, route)


def shift(block, axis, distance):
    size = lax.axis_size(axis)
    return lax.ppermute(block, axis, [(i, (i + distance) % size) for i in range(size)])


def swap_pair(block):
    size = lax.axis_size("expert")
    return lax.ppermute(block, "expert", [(i, i ^ 1) for i in range(size)])


def cost(flops, bytes_accessed, transcendentals=0):
    return pl.CostEstimate(
        flops=int(flops), bytes_accessed=int(bytes_accessed), transcendentals=int(transcendentals)
    )


def spread_rows(values, wide_ref):
    length, count = values.shape
    col = lax.broadcasted_iota(jnp.int32, (count, count * LANES), 1)
    row = lax.broadcasted_iota(jnp.int32, (count, count * LANES), 0)
    ones = jnp.where((col >= row * LANES) & (col < (row + 1) * LANES), 1.0, 0.0).astype(BF16)
    out = jnp.dot(values, ones, preferred_element_type=F32)
    for n in range(count):
        wide_ref[pl.ds(n * length, length), :] = out[:, n * LANES : (n + 1) * LANES]


def scan_kernel(groups, line, place_ref, *refs):
    pieces, refs = refs[:line], refs[line:]
    w_ref, bias_ref, rate_ref, x_ref, y_ref, sum_ref, end_ref, bc_ref, neg_ref = refs[:9]
    low_ref, step_ref, drive_ref, wide_ref = refs[9:]
    length = x_ref.shape[0]
    share = length // line
    for s in range(line):
        start = pl.multiple_of((place_ref[0] + (line - s)) % line * share, share)
        low_ref[pl.ds(start, share), :] = pieces[s][:, :DT_RANK]
        bc_ref[pl.ds(start, share), :] = pieces[s][:, DT_RANK:]
    spread_rows(bc_ref[...], wide_ref)
    for g in range(SUB):
        rows = pl.ds(g, length, stride=SUB)
        if g >= groups:
            step_ref[rows, :] = jnp.zeros((length, LANES), F32)
            drive_ref[rows, :] = jnp.zeros((length, LANES), F32)
            neg_ref[pl.ds(g, NSTATE, stride=SUB), :] = jnp.zeros((NSTATE, LANES), F32)
            continue
        cols = pl.ds(g * LANES, LANES)
        neg_ref[pl.ds(g, NSTATE, stride=SUB), :] = -rate_ref[:, cols]
        raw = jnp.dot(low_ref[...], w_ref[:, cols], preferred_element_type=F32) + bias_ref[:, cols]
        step = jnp.maximum(raw, 0.0) + jnp.log1p(jnp.exp(-jnp.abs(raw)))
        step_ref[rows, :] = step
        drive_ref[rows, :] = step * x_ref[:, cols].astype(F32)

    def block(k, carry):
        states, total = list(carry[0]), carry[1]
        for u in range(SUB):
            t = k * SUB + u
            here = pl.ds(pl.multiple_of(t * SUB, SUB), SUB)
            step, drive = step_ref[here, :], drive_ref[here, :]
            total = total + step
            out = jnp.zeros((SUB, LANES), F32)
            for n in range(NSTATE):
                decay = jnp.exp(step * neg_ref[pl.ds(n * SUB, SUB), :])
                b = wide_ref[pl.ds(n * length + t, 1), :]
                c = wide_ref[pl.ds((NSTATE + n) * length + t, 1), :]
                states[n] = states[n] * decay + drive * b
                out = out + states[n] * c
            y_ref[here, :] = out
            sum_ref[here, :] = total
        return tuple(states), total

    zero = jnp.zeros((SUB, LANES), F32)
    states, total = lax.fori_loop(0, length // SUB, block, ((zero,) * NSTATE, zero))
    for n in range(NSTATE):
        end_ref[n] = states[n]


def run_scan(place, pieces, w, bias, rate, x):
    length, channels = x.shape
    vmem = pl.BlockSpec(memory_space=pltpu.VMEM)
    tall = jax.ShapeDtypeStruct((length * SUB, LANES), F32)
    return pl.pallas_call(
        functools.partial(scan_kernel, channels // LANES, len(pieces)),
        out_shape=(
            tall,
            tall,
            jax.ShapeDtypeStruct((NSTATE, SUB, LANES), F32),
            jax.ShapeDtypeStruct((length, 2 * NSTATE), BF16),
            jax.ShapeDtypeStruct((NSTATE * SUB, LANES), F32),
        ),
        in_specs=[pl.BlockSpec(memory_space=pltpu.SMEM)] + [vmem] * (len(pieces) + 4),
        out_specs=(vmem,) * 5,
        scratch_shapes=[
            pltpu.VMEM((length, DT_RANK), BF16),
            pltpu.VMEM((length * SUB, LANES), F32),
            pltpu.VMEM((length * SUB, LANES), F32),
            pltpu.VMEM((2 * NSTATE * length, LANES), F32),
        ],
        compiler_params=pltpu.CompilerParams(vmem_limit_bytes=20 * MIB),
        cost_estimate=cost(2e8, 4 * MIB, NSTATE * length * channels),
        name="state_scan",
    )(place, *pieces, w, bias, rate, x)


def out_kernel(groups, line, first, at_ref, y_ref, sum_ref, enter_ref, bc_ref, neg_ref, x_ref, z_ref,
               skip_ref, w_hbm, *refs):
    kept_ref, sent_ref, block_refs = refs[0], refs[1], refs[2 : 2 + line]
    full_ref, wide_ref, gated_ref, order_ref, w_ref, sems = refs[2 + line :]
    length = x_ref.shape[0]
    tiles, _, tile = w_ref.shape

    def fetch(j):
        cols = pl.ds(pl.multiple_of(j * tile, tile), tile)
        return pltpu.make_async_copy(w_hbm.at[:, cols], w_ref.at[j], sems.at[j])

    for j in range(tiles):
        fetch(j).start()
    spread_rows(bc_ref[:, NSTATE:], wide_ref)

    def block(k, carry):
        for u in range(SUB):
            t = k * SUB + u
            here = pl.ds(pl.multiple_of(t * SUB, SUB), SUB)
            total = sum_ref[here, :]
            out = y_ref[here, :]
            for n in range(NSTATE):
                c = wide_ref[pl.ds(n * length + t, 1), :]
                out = out + jnp.exp(total * neg_ref[pl.ds(n * SUB, SUB), :]) * enter_ref[n] * c
            full_ref[here, :] = out
        return carry

    lax.fori_loop(0, length // SUB, block, 0)
    for g in range(groups):
        cols = pl.ds(g * LANES, LANES)
        mixed_in = x_ref[:, cols].astype(F32)
        read = full_ref[pl.ds(g, length, stride=SUB), :] + skip_ref[:, cols] * mixed_in
        z = z_ref[:, cols].astype(F32)
        gated_ref[:, cols] = (read * (z / (1.0 + jnp.exp(-z)))).astype(BF16)
    place, half = at_ref[0], at_ref[1]
    count = length // 2
    piece = count // line
    for k in range(line):
        for r in range(2):
            source = pl.multiple_of((2 * ((place + k) % line) + (half ^ r)) * piece, piece)
            order_ref[pl.ds(r * count + k * piece, piece), :] = gated_ref[pl.ds(source, piece), :]
    def project(j):
        fetch(j).wait()
        return jnp.dot(order_ref[...], w_ref[j], preferred_element_type=F32).astype(BF16)

    def step(j, carry):
        cols = pl.ds(pl.multiple_of(j * tile, tile), tile)
        out = project(j)
        kept_ref[:, cols] = out[:count]
        sent_ref[:, cols] = out[count:]
        return carry

    def block_step(j, carry):
        cols = pl.ds(pl.multiple_of((j - first) * tile, tile), tile)
        out = project(j)
        for k in range(line):
            for r in range(2):
                start = r * count + k * piece
                block_refs[k][pl.ds(r * piece, piece), cols] = out[start : start + piece]
        return carry

    lax.fori_loop(0, first, step, 0)
    lax.fori_loop(first, tiles, block_step, 0)


def run_out(at, line, y, total, enter, bc, neg, x, z, skip, w):
    length, channels = x.shape
    wide = w.shape[1]
    tile = min(512, wide)
    first = (wide // tile * 5 + 4) // 8
    vmem = pl.BlockSpec(memory_space=pltpu.VMEM)
    part = jax.ShapeDtypeStruct((length // 2, first * tile), BF16)
    block = jax.ShapeDtypeStruct((length // line, wide - first * tile), BF16)
    return pl.pallas_call(
        functools.partial(out_kernel, channels // LANES, line, first),
        out_shape=(part, part) + (block,) * line,
        in_specs=[pl.BlockSpec(memory_space=pltpu.SMEM)] + [vmem] * 8 + [pl.BlockSpec(memory_space=pl.ANY)],
        out_specs=(vmem,) * (2 + line),
        scratch_shapes=[
            pltpu.VMEM((length * SUB, LANES), F32),
            pltpu.VMEM((NSTATE * length, LANES), F32),
            pltpu.VMEM((length, channels), BF16),
            pltpu.VMEM((length, channels), BF16),
            pltpu.VMEM((wide // tile, channels, tile), BF16),
            pltpu.SemaphoreType.DMA((wide // tile,)),
        ],
        compiler_params=pltpu.CompilerParams(vmem_limit_bytes=48 * MIB),
        cost_estimate=cost(
            2 * length * channels * wide, 2 * channels * wide + 8 * MIB, NSTATE * length * channels
        ),
        name="readout_project",
    )(at, y, total, enter, bc, neg, x, z, skip, w)


class Fetch:
    def __init__(self, source, cols, target, sems, first):
        rows = target.shape[0] // 2
        self.copies = [
            pltpu.make_async_copy(
                source.at[pl.ds(h * rows, rows), cols],
                target.at[pl.ds(h * rows, rows), :],
                sems.at[first + h],
            )
            for h in range(2)
        ]

    def start(self):
        for copy in self.copies:
            copy.start()

    def wait(self):
        for copy in self.copies:
            copy.wait()


def gate_up_kernel(count, first, *refs):
    pieces, (gate_hbm, up_hbm, out_ref, rows_ref, gate_ref, up_ref, sems) = refs[:count], refs[count:]
    copies, at = [], 0
    for k, piece in enumerate(pieces):
        rows = pl.ds(at, piece.shape[0])
        copies.append(pltpu.make_async_copy(piece, rows_ref.at[rows, :], sems.at[k]))
        at += piece.shape[0]
    steps, tile = gate_ref.shape[0], gate_ref.shape[2]

    def fetch(j, k):
        cols = pl.ds(pl.multiple_of(first + j * tile, tile), tile)
        source, target = ((gate_hbm, gate_ref), (up_hbm, up_ref))[k]
        return Fetch(source, cols, target.at[j], sems, count + 4 * j + 2 * k)

    for copy in copies:
        copy.start()
    for j in range(steps):
        fetch(j, 0).start()
        fetch(j, 1).start()
    for copy in copies:
        copy.wait()

    def step(j, carry):
        fetch(j, 0).wait()
        fetch(j, 1).wait()
        gate = jnp.dot(rows_ref[...], gate_ref[j], preferred_element_type=F32)
        up = jnp.dot(rows_ref[...], up_ref[j], preferred_element_type=F32)
        cols = pl.ds(pl.multiple_of(j * tile, tile), tile)
        out_ref[:, cols] = (gate / (1.0 + jnp.exp(-gate)) * up).astype(BF16)
        return carry

    lax.fori_loop(0, steps, step, 0)


def gate_up(pieces, w_gate, w_up, first, width):
    depth = w_gate.shape[0]
    rows = sum(p.shape[0] for p in pieces)
    tile = min(256, width)
    steps = width // tile
    anywhere = pl.BlockSpec(memory_space=pl.ANY)
    return pl.pallas_call(
        functools.partial(gate_up_kernel, len(pieces), first),
        out_shape=jax.ShapeDtypeStruct((rows, width), BF16),
        in_specs=[anywhere] * (len(pieces) + 2),
        out_specs=pl.BlockSpec(memory_space=pltpu.VMEM),
        scratch_shapes=[
            pltpu.VMEM((rows, depth), BF16),
            pltpu.VMEM((steps, depth, tile), BF16),
            pltpu.VMEM((steps, depth, tile), BF16),
            pltpu.SemaphoreType.DMA((len(pieces) + 4 * steps,)),
        ],
        compiler_params=pltpu.CompilerParams(vmem_limit_bytes=49 * MIB),
        cost_estimate=cost(4 * rows * depth * width, 4 * depth * width + 2 * rows * depth),
        name="gate_up",
    )(*pieces, w_gate, w_up)


def finish_kernel(count, first, *refs):
    pieces, (have_ref, gate_hbm, up_hbm, down_hbm) = refs[:count], refs[count : count + 4]
    hidden_ref, outs = refs[count + 4], refs[count + 5 : -5]
    rows_ref, gate_ref, up_ref, down_ref, sems = refs[-5:]
    done = have_ref.shape[1]
    steps, tile = gate_ref.shape[0], gate_ref.shape[2]
    last_steps, last_tile = down_ref.shape[0], down_ref.shape[2]

    def fetch(j, k):
        cols = pl.ds(pl.multiple_of(done + j * tile, tile), tile)
        source, target = ((gate_hbm, gate_ref), (up_hbm, up_ref))[k]
        return Fetch(source, cols, target.at[j], sems, count + 4 * j + 2 * k)

    def last_fetch(j):
        cols = pl.ds(pl.multiple_of(first + j * last_tile, last_tile), last_tile)
        return Fetch(down_hbm, cols, down_ref.at[j], sems, count + 4 * steps + 2 * j)

    copies, at = [], 0
    for k, piece in enumerate(pieces):
        rows = pl.ds(at, piece.shape[0])
        copies.append(pltpu.make_async_copy(piece, rows_ref.at[rows, :], sems.at[k]))
        at += piece.shape[0]
    for copy in copies:
        copy.start()
    for j in range(steps):
        fetch(j, 0).start()
        fetch(j, 1).start()
    for j in range(last_steps):
        last_fetch(j).start()
    hidden_ref[:, pl.ds(0, done)] = have_ref[...]
    for copy in copies:
        copy.wait()

    def step(j, carry):
        fetch(j, 0).wait()
        fetch(j, 1).wait()
        gate = jnp.dot(rows_ref[...], gate_ref[j], preferred_element_type=F32)
        up = jnp.dot(rows_ref[...], up_ref[j], preferred_element_type=F32)
        cols = pl.ds(pl.multiple_of(done + j * tile, tile), tile)
        hidden_ref[:, cols] = (gate / (1.0 + jnp.exp(-gate)) * up).astype(BF16)
        return carry

    def last_step(j, carry):
        last_fetch(j).wait()
        out = jnp.dot(hidden_ref[...], down_ref[j], preferred_element_type=F32).astype(BF16)
        cols = pl.ds(pl.multiple_of(j * last_tile, last_tile), last_tile)
        start = 0
        for ref in outs:
            ref[:, cols] = out[start : start + ref.shape[0]]
            start += ref.shape[0]
        return carry

    lax.fori_loop(0, steps, step, 0)
    lax.fori_loop(0, last_steps, last_step, 0)


def finish(pieces, have, sizes, w_gate, w_up, w_down, first, width):
    depth, hidden = w_gate.shape
    rows, done = have.shape
    tile, last_tile = min(256, hidden - done), min(512, width)
    steps, last_steps = (hidden - done) // tile, width // last_tile
    vmem, anywhere = pl.BlockSpec(memory_space=pltpu.VMEM), pl.BlockSpec(memory_space=pl.ANY)
    shapes = [(rows, hidden)] + [(n, width) for n in sizes]
    hidden_out, *outs = pl.pallas_call(
        functools.partial(finish_kernel, len(pieces), first),
        out_shape=tuple(jax.ShapeDtypeStruct(shape, BF16) for shape in shapes),
        in_specs=[anywhere] * len(pieces) + [vmem] + [anywhere] * 3,
        out_specs=(vmem,) * len(shapes),
        scratch_shapes=[
            pltpu.VMEM((rows, depth), BF16),
            pltpu.VMEM((steps, depth, tile), BF16),
            pltpu.VMEM((steps, depth, tile), BF16),
            pltpu.VMEM((last_steps, hidden, last_tile), BF16),
            pltpu.SemaphoreType.DMA((len(pieces) + 4 * steps + 2 * last_steps,)),
        ],
        compiler_params=pltpu.CompilerParams(vmem_limit_bytes=49 * MIB),
        cost_estimate=cost(
            4 * rows * depth * (hidden - done) + 2 * rows * hidden * width,
            4 * depth * (hidden - done) + 2 * hidden * width + 2 * rows * (depth + width),
        ),
        name="gate_up_down",
    )(*pieces, have, w_gate, w_up, w_down)
    return hidden_out, outs


def down_kernel(count, first, *refs):
    pieces, w_hbm, outs = refs[:count], refs[count], refs[count + 1 : -3]
    rows_ref, w_ref, sems = refs[-3:]
    tiles, _, tile = w_ref.shape

    def fetch(j):
        source = pl.ds(pl.multiple_of(first + j * tile, tile), tile)
        return Fetch(w_hbm, source, w_ref.at[j], sems, 2 * j)

    for j in range(tiles):
        fetch(j).start()
    at = 0
    for piece in pieces:
        rows_ref[:, pl.ds(at, piece.shape[1])] = piece[...]
        at += piece.shape[1]

    def step(j, carry):
        fetch(j).wait()
        out = jnp.dot(rows_ref[...], w_ref[j], preferred_element_type=F32).astype(BF16)
        cols = pl.ds(pl.multiple_of(j * tile, tile), tile)
        start = 0
        for ref in outs:
            ref[:, cols] = out[start : start + ref.shape[0]]
            start += ref.shape[0]
        return carry

    lax.fori_loop(0, tiles, step, 0)


def down(pieces, sizes, w_down, first, width):
    hidden, rows = w_down.shape[0], pieces[0].shape[0]
    tile = min(512, width)
    vmem = pl.BlockSpec(memory_space=pltpu.VMEM)
    return pl.pallas_call(
        functools.partial(down_kernel, len(pieces), first),
        out_shape=tuple(jax.ShapeDtypeStruct((n, width), BF16) for n in sizes),
        in_specs=[vmem] * len(pieces) + [pl.BlockSpec(memory_space=pl.ANY)],
        out_specs=(vmem,) * len(sizes),
        scratch_shapes=[
            pltpu.VMEM((rows, hidden), BF16),
            pltpu.VMEM((width // tile, hidden, tile), BF16),
            pltpu.SemaphoreType.DMA((2 * (width // tile),)),
        ],
        compiler_params=pltpu.CompilerParams(vmem_limit_bytes=49 * MIB),
        cost_estimate=cost(2 * rows * hidden * width, 2 * hidden * width + 2 * rows * (hidden + width)),
        name="down",
    )(*pieces, w_down)


def add_up(*parts):
    return sum(p.astype(F32) for p in parts)


def along_line(block, distance):
    size = lax.axis_size("expert")
    return lax.ppermute(block, "expert", [(e, (e + 2 * distance) % size) for e in range(size)])


def cross(block, turn):
    owners, dps = lax.axis_size("expert"), lax.axis_size("dp")
    route = []
    for e in range(owners):
        for core in range(2):
            for d in range(dps):
                to = (e ^ 1, core, d) if core == turn else (e, core, d ^ 1)
                route.append(((e * 2 + core) * dps + d, (to[0] * 2 + core) * dps + to[2]))
    return lax.ppermute(block, ("expert", "context", "dp"), route)


def after(blocks, *others):
    return lax.optimization_barrier((blocks, others))[0]


def send_rows(packed, line, way=1):
    size = packed.shape[0] // line
    parts = [packed[size * s : size * (s + 1)] for s in range(line)]
    return [parts[0]] + [along_line(parts[s], way * s) for s in range(1, line)]


def plain_experts(packed, line, w_gate, w_up, w_down):
    own = jnp.concatenate(send_rows(packed, line), axis=0)
    rows = jnp.concatenate([own, swap_pair(own)], axis=0)
    rows = lax.all_gather(rows, ("context", "dp"), axis=0, tiled=True)
    hidden = gate_up([rows], w_gate, w_up, 0, w_gate.shape[1])
    out = down([hidden], (rows.shape[0],), w_down, 0, w_down.shape[1])[0]
    mine = lax.psum_scatter(out, ("context", "dp"), scatter_dimension=0, tiled=True)
    count = own.shape[0]
    result = add_up(mine[:count], swap_pair(mine[count:])).astype(BF16)
    return jnp.concatenate(send_rows(result, line, -1), axis=0)


def square_experts(early, late, line, w_gate, w_up, w_down):
    width = w_down.shape[1]
    half = width // 2
    hidden = w_down.shape[0]
    most = hidden // 2

    def pieces(two, four):
        return [two, four, shift(two, "context", 1), shift(four, "context", 1)]

    def part(terms, start, stop):
        return add_up(*[t[start:stop] for t in terms]).astype(BF16)

    def home_first(outs, *others):
        terms = [after(outs[0], *others), shift(outs[1], "context", 1)]
        rows = outs[0].shape[0]
        return terms, part(terms, rows // 2, rows)

    def home_second(terms, far):
        terms = terms + [far]
        rows = far.shape[0]
        return terms, part(terms, rows // 2, rows)

    def home_third(terms, far):
        return part(terms + [far], 0, far.shape[0])

    early_came = send_rows(early, line)
    early_own = jnp.concatenate(early_came, axis=0)
    late_came = send_rows(after(late, early_own), line)
    early_near = cross(early_own, 0)
    early_two = jnp.concatenate([early_own, early_near], axis=0)
    early_four = cross(early_two, 1)
    late_came[0] = after(late_came[0], early_near)
    late_own = jnp.concatenate(late_came, axis=0)
    late_near = cross(late_own, 0)
    sizes = (4 * early_own.shape[0],) * 2
    early_rows = after(pieces(early_two, early_four), late_own)
    early_first = gate_up(early_rows, w_gate, w_up, 0, most)

    late_two = jnp.concatenate([after(late_own, early_first), late_near], axis=0)
    late_four = cross(late_two, 1)
    early_rows = after(early_rows, late_two)
    early_out = finish(early_rows, early_first, sizes, w_gate, w_up, w_down, 0, width)[1]
    late_four = after(late_four, early_out)
    early_kept, early_go = home_first(early_out, late_four)
    early_far = cross(early_go, 1)
    sizes = (4 * late_own.shape[0],) * 2
    late_rows = after(pieces(late_two, late_four), early_go)
    late_hidden = gate_up(late_rows, w_gate, w_up, 0, hidden)
    early_kept, early_go = home_second(after(early_kept, late_hidden), early_far)
    early_far = cross(early_go, 0)
    late_hidden = after(late_hidden, early_go)
    out_left = down([late_hidden], sizes, w_down, 0, half)
    early_result = home_third(after(early_kept, out_left[0]), early_far)
    left = home_first(after(out_left, early_result))
    left_far = cross(left[1], 1)
    out_right = down([after(late_hidden, left[1])], sizes, w_down, half, half)
    left = home_second(after(left[0], out_right), left_far)
    left_far = cross(left[1], 0)
    right = home_first(after(out_right, left[1]))
    right_far = cross(right[1], 1)
    left_result = home_third(after(left[0], right[1]), left_far)
    right = home_second(after(right[0], left_result), right_far)
    right_far = cross(right[1], 0)
    few, many = early_result.shape[0] // line, left_result.shape[0] // line
    packed = []
    for s in range(line):
        mine = early_result[few * s : few * (s + 1)]
        packed += [mine[:, :half], mine[:, half:], left_result[many * s : many * (s + 1)]]
    left_came = send_rows(jnp.concatenate(packed, axis=0), line, -1)
    right_result = home_third(right[0], right_far)
    right_came = send_rows(right_result, line, -1)
    left_came = after(left_came, right_result)
    left_rows = [c[:few] for c in left_came] + [c[2 * few :] for c in left_came]
    right_rows = [c[few : 2 * few] for c in left_came] + right_came
    return [jnp.concatenate(rows, axis=0) for rows in (left_rows, right_rows)]


def on_device(
    residual,
    x_raw,
    z_gate,
    conv_w,
    conv_b,
    xproj_w,
    dtproj_w,
    dt_bias,
    a_rate,
    skip_gain,
    out_w,
    norm_gain,
    route_ids,
    route_w,
    w_gate,
    w_up,
    w_down,
):
    owners, contexts, dps = (lax.axis_size(a) for a in ("expert", "context", "dp"))
    me = lax.axis_index("expert")
    place, half = me // 2, me % 2
    line = owners // 2
    length, channels = x_raw.shape[2:]
    width = residual.shape[3]
    row_count = residual.shape[2]

    values = x_raw[0, 0]
    prior_rim = from_behind(values[length - (CONV - 1) :], "context", 1)
    padded = jnp.concatenate([prior_rim, values], axis=0).astype(F32)
    conv_sum = conv_b[None, :] + sum(
        (
            conv_w[lag_index][None, :] * padded[lag_index : lag_index + length]
            for lag_index in range(CONV)
        )
    )
    mixed_in = jax.nn.silu(conv_sum).astype(BF16)
    projected = jnp.dot(mixed_in, xproj_w, preferred_element_type=F32).astype(BF16)
    ids, weights = after((route_ids[0, 0], route_w[0, 0]), projected)
    shares = projected.reshape(line, length // line, -1)

    def share_of(s):
        return lax.dynamic_index_in_dim(shares, (place + s) % line, 0, keepdims=False)

    share = add_up(share_of(0), *[along_line(share_of(s), s) for s in range(1, line)]).astype(BF16)
    share = add_up(share, swap_pair(share)).astype(BF16)
    pieces = [share] + [along_line(share, s) for s in range(1, line)]

    where = jnp.stack([place, half]).astype(jnp.int32)
    y, total, end, bc, neg = run_scan(
        where, pieces, dtproj_w, dt_bias[None, :], a_rate, mixed_in
    )
    enter = from_behind(end, "context", 1)
    for step in range(contexts - 2):
        decay = jnp.exp(total[-SUB:][None] * neg.reshape(end.shape))
        enter = from_behind(end + decay * enter, "context", 1)
    kept, sent, *blocks = run_out(
        where, line, y, total, enter, bc, neg, mixed_in, z_gate[0, 0], skip_gain[None, :], out_w
    )
    got = swap_pair(sent)
    over_z = add_up(blocks[0], *[along_line(blocks[s], s) for s in range(1, line)])
    both = add_up(kept, got).astype(BF16).reshape(line, row_count, -1)
    other = swap_pair(over_z[row_count:].astype(BF16))
    sums = [
        add_up(both[0], *[along_line(both[s], s) for s in range(1, line)]),
        add_up(over_z[:row_count], other),
    ]
    mixer_out = jnp.concatenate(sums, axis=1)

    stream_f = (residual[0, 0].astype(F32) + mixer_out).astype(BF16).astype(F32)
    normed = (
        stream_f
        * lax.rsqrt(jnp.mean(stream_f * stream_f, axis=1, keepdims=True) + 1e-05)
        * norm_gain[None, :]
    ).astype(BF16)
    capacity = min(row_count, 8 * ((3 * row_count * TOP + 16 * line - 1) // (16 * line)))
    cuts = (0, 8, capacity) if contexts == 2 and dps == 2 and capacity > 8 else (0, capacity)
    named = jnp.any(ids[:, :, None] == jnp.arange(line, dtype=jnp.int32), axis=1)
    rank = jnp.cumsum(named.astype(jnp.int32), axis=0) - 1
    chosen = ids[:, :, None] == jnp.arange(line, dtype=jnp.int32)
    rank_of = jnp.sum(jnp.where(chosen, rank[:, None, :], 0), axis=2)
    away = (ids - place + line) % line
    placing, weighting, packed = [], [], []
    for low, high in zip(cuts[:-1], cuts[1:]):
        inside = (rank_of >= low) & (rank_of < high)
        slot_of = jnp.where(inside, away * (high - low) + rank_of - low, -1)
        hits = slot_of[:, :, None] == jnp.arange(line * (high - low), dtype=jnp.int32)
        placing = jnp.any(hits, axis=1).astype(BF16)
        weighting.append(jnp.sum(jnp.where(hits, weights[:, :, None], 0.0), axis=1))
        rows = lax.dot_general(
            placing, normed, (((0,), (0,)), ((), ())), preferred_element_type=F32
        )
        packed.append(rows.astype(BF16))
    if len(packed) == 2:
        back = square_experts(*packed, line, w_gate[0], w_up[0], w_down[0])
    else:
        back = [plain_experts(packed[0], line, w_gate[0], w_up[0], w_down[0])]
    weighting = jnp.concatenate(weighting, axis=1)
    expert_sum = jnp.concatenate(
        [
            jnp.dot(
                weighting,
                rows.astype(F32),
                precision=lax.Precision.HIGHEST,
                preferred_element_type=F32,
            )
            for rows in back
        ],
        axis=1,
    )
    mixed = (stream_f + expert_sum).astype(BF16)
    return mixed.reshape(1, 1, row_count, width)


def solution(mesh):
    placed = (
        P("dp", "context", "expert", None),
        P("dp", "context", None, "expert"),
        P("dp", "context", None, "expert"),
        P(None, "expert"),
        P("expert"),
        P("expert", None),
        P(None, "expert"),
        P("expert"),
        P(None, "expert"),
        P("expert"),
        P("expert", None),
        P(),
        P("dp", "context", "expert", None),
        P("dp", "context", "expert", None),
        P("expert", None, ("context", "dp")),
        P("expert", None, ("context", "dp")),
        P("expert", ("context", "dp"), None),
    )
    return jax.shard_map(
        on_device,
        mesh=mesh,
        in_specs=placed,
        out_specs=P("dp", "context", "expert", None),
        check_vma=False,
    )
```
